32 devices in a mesh: dp: 4 (over y, x), seq: 8 (over z, core).
Axes of the slice: x: 2, y: 2, z: 4, core: 2. Of those that a mesh axis runs over, the one named last changes fastest.
Arguments:
- inputs: bfloat16 [32, 512, 512], P('dp', 'seq'), may hold values from -6 to 6
- cotangent: bfloat16 [32, 512, 512], P('dp', 'seq'), may hold values from -6 to 6
- item_lengths: int32 [32, 2], P('dp'), may hold values from 64 to 250, as said below
- attn_gain: bfloat16 [2, 512], replicated, may hold values from 0.099609375 to 1.8984375
- attn_bias: bfloat16 [2, 512], replicated, may hold values from -1.5 to 1.5
- query_weight: bfloat16 [2, 512, 512], replicated, may hold values from -0.25 to 0.25
- key_weight: bfloat16 [2, 512, 512], replicated, may hold values from -0.25 to 0.25
- value_weight: bfloat16 [2, 512, 512], replicated, may hold values from -0.25 to 0.25
- output_weight: bfloat16 [2, 512, 512], replicated, may hold values from -1 to 1
- ffn_gain: bfloat16 [2, 512], replicated, may hold values from 0.099609375 to 1.8984375
- ffn_bias: bfloat16 [2, 512], replicated, may hold values from -1.5 to 1.5
- up_weight: bfloat16 [2, 512, 2048], replicated, may hold values from -0.25 to 0.25
- up_bias: bfloat16 [2, 2048], replicated, may hold values from -1.5 to 1.5
- down_weight: bfloat16 [2, 2048, 512], replicated, may hold values from -0.25 to 0.25
- down_bias: bfloat16 [2, 512], replicated, may hold values from -1.5 to 1.5
Outputs:
- output: bfloat16 [32, 512, 512], P('dp', 'seq')
- input_grad: bfloat16 [32, 512, 512], P('dp', 'seq')
- dattn_gain: float32 [2, 512], P(None, 'seq')
- dattn_bias: float32 [2, 512], P(None, 'seq')
- dquery_weight: float32 [2, 512, 512], P(None, 'seq')
- dkey_weight: float32 [2, 512, 512], P(None, 'seq')
- dvalue_weight: float32 [2, 512, 512], P(None, 'seq')
- doutput_weight: float32 [2, 512, 512], P(None, 'seq')
- dffn_gain: float32 [2, 512], P(None, 'seq')
- dffn_bias: float32 [2, 512], P(None, 'seq')
- dup_weight: float32 [2, 512, 2048], P(None, 'seq')
- dup_bias: float32 [2, 2048], P(None, 'seq')
- ddown_weight: float32 [2, 2048, 512], P(None, 'seq')
- ddown_bias: float32 [2, 512], P(None, 'seq')
The draws below stay inside these ranges and needn't reach their ends.
Inputs may be any that keep to these rules, and one draw needn't show every extreme that they name: `item_lengths`: every entry is 64, 128 or 250, and every row holds at least one of the first and one of the last.
All inputs are finite; a program needn't handle non-finite values.
Results may differ from the reference program's by a relative error of at most 0.02.
Values may be sent and summed in bfloat16 or wider, within the bound.
No kernel may reach another device: no remote copies, remote signals or barrier semaphores. Data moves between devices by JAX's collectives and lax.ppermute only.
A program may use at most 192 MiB of HBM per device.

```python
import jax
import jax.numpy as jnp
from jax import lax

D = 512
H = 8
HD = 64
FF = 2048
LAYERS = 2
SLOTS = 256
ROWS_ALL = 32
ROW_LEN = 512
ITEMS_ROW = 2


def draw_item_lengths(key, part):
    key = jax.random.fold_in(key, 7)
    pick_key, spot_key = jax.random.split(key)
    choose = jax.random.randint(pick_key, (ROWS_ALL, ITEMS_ROW), 0, 3)
    length_table = jnp.where(choose == 0, SLOTS // 4, jnp.where(choose == 1, SLOTS // 2, SLOTS - 6))
    long_spot = jax.random.randint(spot_key, (ROWS_ALL, 1), 0, ITEMS_ROW)
    column = lax.iota(jnp.int32, ITEMS_ROW)[None, :]
    length_table = jnp.where(column == long_spot, SLOTS - 6, length_table)
    length_table = jnp.where(column == (long_spot + 1) % ITEMS_ROW, SLOTS // 4, length_table)
    return length_table.astype(jnp.int32)


def shard_levels(key, extent, cuts, least, high):
    loudness, own = 1.0, jax.random.fold_in(key, 6)
    for axis_at, parts in cuts:
        steps = jnp.exp(jax.random.uniform(jax.random.fold_in(own, axis_at), (parts,), jnp.float32, least / len(cuts), high / len(cuts)))
        loudness = loudness * jnp.repeat(steps, extent[axis_at] // parts).reshape([-1 if axis == axis_at else 1 for axis in range(len(extent))])
    return loudness


def normal_values(own_key, dims, scale, most, cuts=(), kind=jnp.bfloat16):
    gain = shard_levels(own_key, dims, cuts, -0.22, 0.18) if cuts else 1.0
    values = jax.random.normal(own_key, dims, jnp.float32) * scale * gain
    return jnp.minimum(jnp.maximum(values, -most), most).astype(kind)


def setup_inputs(seed: int = 0) -> dict:
    streams_of = jax.random.split(jax.random.key(seed), 16)
    return {
        "inputs": normal_values(streams_of[0], (ROWS_ALL, ROW_LEN, D), 1.0, 6.0, ((0, 4), (1, 8))),
        "cotangent": normal_values(streams_of[1], (ROWS_ALL, ROW_LEN, D), 1.0, 6.0, ((0, 4), (1, 8))),
        "item_lengths": draw_item_lengths(jax.random.fold_in(streams_of[15], 71), 0),
        "attn_gain": jnp.clip(1.0 + 0.18 * jax.random.normal(streams_of[3], (LAYERS, D), jnp.float32), 0.099609375, 1.8984375).astype(jnp.bfloat16),
        "attn_bias": normal_values(streams_of[4], (LAYERS, D), 0.3, 1.5),
        "query_weight": normal_values(streams_of[5], (LAYERS, D, D), D ** -0.5, 0.25),
        "key_weight": normal_values(streams_of[6], (LAYERS, D, D), D ** -0.5, 0.25),
        "value_weight": normal_values(streams_of[7], (LAYERS, D, D), D ** -0.5, 0.25),
        "output_weight": normal_values(streams_of[8], (LAYERS, D, D), (D // 16) ** -0.5, 1.0),
        "ffn_gain": jnp.clip(1.0 + 0.18 * jax.random.normal(streams_of[9], (LAYERS, D), jnp.float32), 0.099609375, 1.8984375).astype(jnp.bfloat16),
        "ffn_bias": normal_values(streams_of[10], (LAYERS, D), 0.3, 1.5),
        "up_weight": normal_values(streams_of[11], (LAYERS, D, FF), D ** -0.5, 0.25),
        "up_bias": normal_values(streams_of[12], (LAYERS, FF), 0.3, 1.5),
        "down_weight": normal_values(streams_of[13], (LAYERS, FF, D), (FF // 4) ** -0.5, 0.25),
        "down_bias": normal_values(streams_of[14], (LAYERS, D), 0.3, 1.5),
    }


EPS = 1e-05
NEG = -1000000000.0
HIGH = lax.Precision.HIGHEST

@jax.custom_vjp
def low(v):
    return lax.optimization_barrier(v.astype(jnp.bfloat16)).astype(jnp.float32)

@jax.custom_vjp
def low_back(v):
    return v

def low_keep(v):
    return (low(v), None)

def low_pass(kept, grad):
    return (grad,)

def back_keep(v):
    return (v, None)

def back_low(kept, grad):
    return (low(grad),)
low.defvjp(low_keep, low_pass)
low_back.defvjp(back_keep, back_low)

def layer_norm(values, gain_term, bias_term):
    row_mean = lax.optimization_barrier(jnp.mean(values, axis=-1, keepdims=True))
    centered = values - row_mean
    variance = lax.optimization_barrier(jnp.mean(centered * centered, axis=-1, keepdims=True))
    return centered * lax.rsqrt(variance + EPS) * gain_term + bias_term

def matmul(left, right):
    return jnp.dot(left, right, precision=HIGH, preferred_element_type=jnp.float32)

def attend(query_rows, key_rows, value_rows, valid_row):
    item_count = query_rows.shape[0] // SLOTS
    item_shape = (item_count, SLOTS, H, HD)
    scores = jnp.einsum('ishd,ithd->ihst', query_rows.reshape(item_shape), key_rows.reshape(item_shape), precision=HIGH) * HD ** (-0.5)
    scores = low_back(jnp.where(valid_row.reshape(item_count, 1, 1, SLOTS), scores, NEG))
    row_max = lax.optimization_barrier(jnp.max(scores, axis=-1, keepdims=True))
    exp_scores = jnp.exp(scores - row_max)
    probs_low = low(exp_scores / lax.optimization_barrier(jnp.sum(exp_scores, axis=-1, keepdims=True)))
    attn_out = jnp.einsum('ihst,ithd->ishd', probs_low, value_rows.reshape(item_shape), precision=HIGH)
    return attn_out.reshape(query_rows.shape[0], H * HD)

def row_forward(row_input, valid_row, weights):
    attn_gain, attn_bias, query_weight, key_weight, value_weight, output_weight, ffn_gain, ffn_bias, up_weight, up_bias, down_weight, down_bias = weights
    hidden = row_input
    for layer_index in range(LAYERS):
        normed = low(layer_norm(hidden, attn_gain[layer_index], attn_bias[layer_index]))
        query_rows = low(low_back(matmul(normed, query_weight[layer_index])))
        key_rows = low(low_back(matmul(normed, key_weight[layer_index])))
        value_rows = low(low_back(matmul(normed, value_weight[layer_index])))
        mixed_rows = low(low_back(attend(query_rows, key_rows, value_rows, valid_row)))
        hidden = hidden + low_back(matmul(mixed_rows, output_weight[layer_index]))
        normed_ffn = low(layer_norm(hidden, ffn_gain[layer_index], ffn_bias[layer_index]))
        pre_act = low_back(matmul(normed_ffn, up_weight[layer_index]) + up_bias[layer_index])
        active = low(jax.nn.gelu(pre_act))
        hidden = hidden + low_back(matmul(active, down_weight[layer_index]) + down_bias[layer_index])
    return hidden

def reference(inputs, cotangent, item_lengths, attn_gain, attn_bias, query_weight, key_weight, value_weight, output_weight, ffn_gain, ffn_bias, up_weight, up_bias, down_weight, down_bias):
    slot_index = lax.iota(jnp.int32, SLOTS)
    valid_mask = (slot_index[None, None, :] < item_lengths[:, :, None]).reshape(item_lengths.shape[0], -1)
    weights = tuple((array.astype(jnp.float32) for array in (attn_gain, attn_bias, query_weight, key_weight, value_weight, output_weight, ffn_gain, ffn_bias, up_weight, up_bias, down_weight, down_bias)))

    def forward(start_rows, params):

        def single_row(row_pair):
            return row_forward(row_pair[0], row_pair[1], params)
        return lax.map(jax.checkpoint(single_row), (start_rows, valid_mask))
    result, pullback = jax.vjp(forward, inputs.astype(jnp.float32), weights)
    seed_grad = cotangent.astype(jnp.float32) * valid_mask[:, :, None].astype(jnp.float32)
    input_grad, grad_list = pullback(seed_grad)
    return (result.astype(jnp.bfloat16), input_grad.astype(jnp.bfloat16), grad_list[0], grad_list[1], grad_list[2], grad_list[3], grad_list[4], grad_list[5], grad_list[6], grad_list[7], grad_list[8], grad_list[9], grad_list[10], grad_list[11])
```

```python
import functools
import jax
import jax.numpy as jnp
from jax import lax
from jax.experimental import pallas as pl
from jax.experimental.pallas import tpu as pltpu

H = 8
SLOTS = 256
EPS = 1e-05
NEG = -1000000000.0
BF = jnp.bfloat16
F32 = jnp.float32
GELU_C = 0.7978845608028654
GELU_A = 0.044715

NN = (((1,), (0,)), ((), ()))
NT = (((1,), (1,)), ((), ()))
TN = (((0,), (0,)), ((), ()))


def dot(left, right, form=NN):
    return lax.dot_general(left, right, form, preferred_element_type=F32)


def normalize(values):
    centered = values - jnp.mean(values, axis=-1, keepdims=True)
    inv = lax.rsqrt(jnp.mean(centered * centered, axis=-1, keepdims=True) + EPS)
    return centered * inv, inv


def head_masks(width):
    lane = lax.broadcasted_iota(jnp.int32, (1, 2 * width), 1)
    low = (lane < width).astype(F32).astype(BF)
    return low, (1.0 - low.astype(F32)).astype(BF)


def attn_fwd_body(lens, h_ref, gain, bias, wq, wk, wv, a_ref, q_ref, k_ref, v_ref, o_ref, lse_ref):
    head = 64
    masks = head_masks(head)
    units = h_ref.shape[0] // SLOTS
    for i in range(units):
        rows = slice(SLOTS * i, SLOTS * (i + 1))
        xhat, _ = normalize(h_ref[rows, :].astype(F32))
        a = (xhat * gain[...] + bias[...]).astype(BF)
        a_ref[rows, :] = a
        q_ref[rows, :] = (dot(a, wq[...]).astype(BF).astype(F32) * 0.125).astype(BF)
        k_ref[rows, :] = dot(a, wk[...]).astype(BF)
        v_ref[rows, :] = dot(a, wv[...]).astype(BF)
    key = lax.broadcasted_iota(jnp.int32, (SLOTS, 1), 0)
    for i in range(units):
        rows = slice(SLOTS * i, SLOTS * (i + 1))
        valid = key < lens[0, i]
        for pair in range(H // 2):
            cols = slice(128 * pair, 128 * pair + 128)
            qp, kp, vp = q_ref[rows, cols], k_ref[rows, cols], v_ref[rows, cols]
            acc = None
            for hh in range(2):
                st = dot(kp * masks[hh], qp, NT)
                st = jnp.where(valid, st, NEG)
                top = jnp.max(st, axis=0, keepdims=True)
                e = jnp.exp(st - top)
                tot = jnp.sum(e, axis=0, keepdims=True)
                pt = (e * (1.0 / tot)).astype(BF)
                part = dot(pt, vp * masks[hh], TN)
                acc = part if acc is None else acc + part
                lse_ref[i * H + 2 * pair + hh, :] = (top + jnp.log(tot))[0]
            o_ref[rows, cols] = acc.astype(BF)


def attn_fwd(lens, h, gain, bias, wq, wk, wv):
    m, d = h.shape
    sd = jax.ShapeDtypeStruct
    vm = pl.BlockSpec(memory_space=pltpu.VMEM)
    return pl.pallas_call(
        attn_fwd_body,
        in_specs=[pl.BlockSpec(memory_space=pltpu.SMEM)] + [vm] * 6,
        out_specs=[vm] * 6,
        out_shape=[sd((m, d), BF)] * 5 + [sd((m // SLOTS * H, SLOTS), F32)],
        compiler_params=pltpu.CompilerParams(vmem_limit_bytes=56 << 20),
    )(lens, h, gain, bias, wq, wk, wv)


def ffn_fwd_body(h_ref, o_ref, wo, gain, bias, wup, bup, wdown, bdown, g_ref, c_ref, u_ref, gp_ref, n_ref):
    m = h_ref.shape[0]
    ff = wup.shape[1]
    step = 512
    for i in range(m // SLOTS):
        rows = slice(SLOTS * i, SLOTS * (i + 1))
        g = h_ref[rows, :].astype(F32) + dot(o_ref[rows, :], wo[...])
        g_ref[rows, :] = g
        xhat, _ = normalize(g)
        c_ref[rows, :] = (xhat * gain[...] + bias[...]).astype(BF)
    for f in range(ff // step):
        fs = slice(step * f, step * f + step)
        for i in range(m // SLOTS):
            rows = slice(SLOTS * i, SLOTS * (i + 1))
            z = dot(c_ref[rows, :], wup[:, fs]) + bup[:, fs]
            z2 = z * z
            t = jnp.tanh(GELU_C * (z * (1.0 + GELU_A * z2)))
            half = 0.5 + 0.5 * t
            u = z * half
            gp = half + (0.5 * z) * (1.0 - t * t) * (GELU_C * (1.0 + 3.0 * GELU_A * z2))
            u_ref[rows, fs] = u.astype(BF)
            gp_ref[rows, fs] = gp.astype(BF)
    for i in range(m // SLOTS):
        rows = slice(SLOTS * i, SLOTS * (i + 1))
        n_ref[rows, :] = g_ref[rows, :] + (dot(u_ref[rows, :], wdown[...]) + bdown[...])


def ffn_fwd(h, o, wo, gain, bias, wup, bup, wdown, bdown):
    m, d = h.shape
    ff = wup.shape[1]
    sd = jax.ShapeDtypeStruct
    vm = pl.BlockSpec(memory_space=pltpu.VMEM)
    return pl.pallas_call(
        ffn_fwd_body,
        in_specs=[vm] * 9,
        out_specs=[vm] * 5,
        out_shape=[sd((m, d), F32), sd((m, d), BF), sd((m, ff), BF), sd((m, ff), BF), sd((m, d), F32)],
        compiler_params=pltpu.CompilerParams(vmem_limit_bytes=56 << 20),
    )(h, o, wo, gain, bias, wup, bup, wdown, bdown)


def norm_back(dy, values, gain):
    xhat, inv = normalize(values)
    dgain = jnp.sum(dy * xhat, axis=0, keepdims=True)
    dbias = jnp.sum(dy, axis=0, keepdims=True)
    dx = dy * gain
    dx = inv * (dx - jnp.mean(dx, axis=-1, keepdims=True) - xhat * jnp.mean(dx * xhat, axis=-1, keepdims=True))
    return dx, dgain, dbias


def ffn_bwd_body(dh_ref, u_ref, gp_ref, c_ref, g_ref, gain, wup, wdown, buf_ref, dg_ref, dn_ref, dbu_ref, dz_ref):
    m, d = dh_ref.shape
    ff = wup.shape[1]
    step = 512
    dm = dh_ref[...].astype(BF)
    for f in range(ff // step):
        fs = slice(step * f, step * f + step)
        res = dot(dm, u_ref[:, fs], TN)
        for t in range(2):
            buf_ref[2 * f + t, :, 0:256] = res[:, 256 * t : 256 * t + 256].astype(BF)
        dz = (dot(dm, wdown[fs, :], NT) * gp_ref[:, fs].astype(F32)).astype(BF)
        dz_ref[:, fs] = dz
        dbu_ref[:, fs] = jnp.sum(dz.astype(F32), axis=0, keepdims=True)
        res = dot(c_ref[...], dz, TN)
        for t in range(2):
            at = (2 * f + t) * 64
            buf_ref[:, at : at + 64, 256:512] = res[:, 256 * t : 256 * t + 256].astype(BF).reshape(8, 64, 256)
    dgain = dbias = dbd = None
    for i in range(m // SLOTS):
        rows = slice(SLOTS * i, SLOTS * (i + 1))
        dc = dot(dz_ref[rows, :], wup[...], NT)
        dx, dg1, db1 = norm_back(dc, g_ref[rows, :], gain[...])
        dg_ref[rows, :] = dh_ref[rows, :] + dx
        s1 = jnp.sum(dh_ref[rows, :].astype(BF).astype(F32), axis=0, keepdims=True)
        dgain, dbias, dbd = (dg1, db1, s1) if i == 0 else (dgain + dg1, dbias + db1, dbd + s1)
    dn_ref[0:1, :] = dgain
    dn_ref[1:2, :] = dbias
    dn_ref[2:3, :] = dbd


def ffn_bwd(dh, u, gp, c, g, gain, wup, wdown):
    m, d = dh.shape
    ff = wup.shape[1]
    sd = jax.ShapeDtypeStruct
    vm = pl.BlockSpec(memory_space=pltpu.VMEM)
    return pl.pallas_call(
        ffn_bwd_body,
        in_specs=[vm] * 8,
        out_specs=[vm] * 4,
        out_shape=[sd((8, 512, 512), BF), sd((m, d), F32), sd((8, d), F32), sd((1, ff), F32)],
        scratch_shapes=[pltpu.VMEM((m, ff), BF)],
        compiler_params=pltpu.CompilerParams(vmem_limit_bytes=56 << 20),
    )(dh, u, gp, c, g, gain, wup, wdown)


def attn_bwd_body(lens, dg_ref, o_ref, q_ref, k_ref, v_ref, lse_ref, a_ref, h_ref, gain, wq, wk, wv, wo,
                  buf_ref, dh_ref, dn_ref, do_ref, dq_ref, dk_ref, dv_ref):
    m, d = dg_ref.shape
    head = 64
    masks = head_masks(head)
    units = m // SLOTS
    dr = dg_ref[...].astype(BF)
    do_ref[...] = dot(dr, wo[...], NT).astype(BF)
    buf_ref[:, 0:64, :] = dot(o_ref[...], dr, TN).astype(BF).reshape(8, 64, d)
    key = lax.broadcasted_iota(jnp.int32, (SLOTS, 1), 0)
    for i in range(units):
        rows = slice(SLOTS * i, SLOTS * (i + 1))
        valid = key < lens[0, i]
        for pair in range(H // 2):
            cols = slice(128 * pair, 128 * pair + 128)
            qp, kp, vp, dop = q_ref[rows, cols], k_ref[rows, cols], v_ref[rows, cols], do_ref[rows, cols]
            dq = dk = dv = None
            for hh in range(2):
                mk = masks[hh]
                km = kp * mk
                st = jnp.where(valid, dot(km, qp, NT), NEG)
                pt = jnp.exp(st - lse_ref[i * H + 2 * pair + hh, :][None, :])
                dpt = dot(vp * mk, dop, NT)
                delta = jnp.sum(pt * dpt, axis=0, keepdims=True)
                dst = (pt * (dpt - delta)).astype(BF)
                p1 = dot(dst, km, TN)
                p2 = dot(dst, qp * mk)
                p3 = dot(pt.astype(BF), dop * mk)
                dq, dk, dv = (p1, p2, p3) if dq is None else (dq + p1, dk + p2, dv + p3)
            dq_ref[rows, cols] = (dq * 0.125).astype(BF)
            dk_ref[rows, cols] = dk.astype(BF)
            dv_ref[rows, cols] = dv.astype(BF)
    a = a_ref[...]
    for n, ref in enumerate((dq_ref, dk_ref, dv_ref)):
        buf_ref[:, 64 * n + 64 : 64 * n + 128, :] = dot(a, ref[...], TN).astype(BF).reshape(8, 64, d)
    dgain = dbias = None
    for i in range(units):
        rows = slice(SLOTS * i, SLOTS * (i + 1))
        da = dot(dq_ref[rows, :], wq[...], NT) + dot(dk_ref[rows, :], wk[...], NT) + dot(dv_ref[rows, :], wv[...], NT)
        dx, dg1, db1 = norm_back(da, h_ref[rows, :].astype(F32), gain[...])
        dh_ref[rows, :] = dg_ref[rows, :] + dx
        dgain, dbias = (dg1, db1) if i == 0 else (dgain + dg1, dbias + db1)
    dn_ref[0:1, :] = dgain
    dn_ref[1:2, :] = dbias


def attn_bwd(lens, dg, o, q, k, v, lse, a, h, gain, wq, wk, wv, wo):
    m, d = dg.shape
    sd = jax.ShapeDtypeStruct
    vm = pl.BlockSpec(memory_space=pltpu.VMEM)
    return pl.pallas_call(
        attn_bwd_body,
        in_specs=[pl.BlockSpec(memory_space=pltpu.SMEM)] + [vm] * 13,
        out_specs=[vm] * 3,
        out_shape=[sd((8, 256, 512), BF), sd((m, d), F32), sd((8, d), F32)],
        scratch_shapes=[pltpu.VMEM((m, d), BF)] * 4,
        compiler_params=pltpu.CompilerParams(vmem_limit_bytes=56 << 20),
    )(lens, dg, o, q, k, v, lse, a, h, gain, wq, wk, wv, wo)


def take(array, index, axis=0):
    return lax.dynamic_index_in_dim(array, index, axis, keepdims=False)


def add(left, right):
    return (left.astype(F32) + right.astype(F32)).astype(BF)


def gather_units(local, group, member):
    rows, width, depth = local.shape
    parts = local.reshape(group, rows // group, width, depth)
    size = lax.axis_size("seq")
    pieces = [take(parts, member)]
    for d in range(1, group):
        pairs = [(s, s ^ d) for s in range(size)]
        pieces.append(lax.ppermute(take(parts, member ^ d), "seq", pairs))
    stacked = jnp.stack(pieces)
    blocks = [take(stacked, member ^ b) for b in range(group)]
    return jnp.stack(blocks, axis=1).reshape(rows // group * group * width, depth)


def return_units(units, rows, group, member):
    depth = units.shape[-1]
    width = units.shape[0] // rows
    blocks = units.reshape(rows // group, group, width, depth)
    size = lax.axis_size("seq")
    pieces = [take(blocks, member, 1)]
    for d in range(1, group):
        pairs = [(s, s ^ d) for s in range(size)]
        pieces.append(lax.ppermute(take(blocks, member ^ d, 1), "seq", pairs))
    stacked = jnp.stack(pieces)
    parts = [take(stacked, member ^ b) for b in range(group)]
    return jnp.concatenate(parts, axis=0)


BOTH = ("dp", "seq")


def pairs_of(flip):
    out = []
    for y in range(2):
        for x in range(2):
            for z in range(4):
                for c in range(2):
                    y2, x2, z2, c2 = flip(y, x, z, c)
                    out.append((y * 16 + x * 8 + z * 2 + c, y2 * 16 + x2 * 8 + z2 * 2 + c2))
    return out


CORE = pairs_of(lambda y, x, z, c: (y, x, z, 1 - c))
PLANE_1 = pairs_of(lambda y, x, z, c: (y, 1 - x, z, c) if c == 0 else (1 - y, x, z, c))
PLANE_2 = pairs_of(lambda y, x, z, c: (y, 1 - x, z, c) if c == 1 else (1 - y, x, z, c))
LINE_1 = pairs_of(lambda y, x, z, c: (y, x, z ^ 1, c))
LINE_2 = pairs_of(lambda y, x, z, c: (y, x, z ^ 2, c))


def halve(parts, bit, axis, pairs):
    received = lax.ppermute(take(parts, 1 - bit, axis), BOTH, pairs)
    return add(take(parts, bit, axis), received)


def doubled(piece, bit, pairs):
    other = lax.ppermute(piece, BOTH, pairs)
    low = jnp.where(bit == 0, piece, other)
    high = jnp.where(bit == 0, other, piece)
    return jnp.concatenate([low, high], axis=0)


def reduce_buffer(buf):
    rows, width = buf.shape[1:]
    dp, seq = lax.axis_index("dp"), lax.axis_index("seq")
    core, z = seq % 2, seq // 2
    y, x = dp // 2, dp % 2
    first = jnp.where(core == 0, x, y)
    second = jnp.where(core == 0, y, x)
    part = halve(buf.reshape(4, 2, rows, width), core, 1, CORE)
    part = halve(part.reshape(4, 2, rows // 2, width), first, 1, PLANE_1)
    part = halve(part.reshape(4, 2, rows // 4, width), second, 1, PLANE_2)
    part = halve(part.reshape(2, 2, rows // 4, width), z % 2, 1, LINE_1)
    part = halve(part, z // 2, 0, LINE_2)
    part = doubled(part, second, PLANE_2)
    return doubled(part, first, PLANE_1)


def on_device(
    inputs, cotangent, item_lengths, attn_gain, attn_bias, query_weight, key_weight, value_weight, output_weight,
    ffn_gain, ffn_bias, up_weight, up_bias, down_weight, down_bias,
):
    rows, width, depth = inputs.shape
    layers, _, ff = up_weight.shape
    group = SLOTS // width
    seq = lax.axis_index("seq")
    member, item = seq % group, seq // group
    mine = take(item_lengths.reshape(group, rows // group, -1), member)
    lens = take(mine, item, 1).reshape(1, -1)
    units = rows // group

    hidden = gather_units(inputs, group, member)
    cot = gather_units(cotangent, group, member)
    valid = lax.iota(jnp.int32, SLOTS)[None, :] < lens[0][:, None]

    def row(array, layer):
        return array[layer].astype(F32).reshape(1, -1)

    kept = []
    for l in range(layers):
        a, q, k, v, o, lse = attn_fwd(
            lens, hidden, row(attn_gain, l), row(attn_bias, l), query_weight[l], key_weight[l], value_weight[l])
        g, c, u, gp, following = ffn_fwd(
            hidden, o, output_weight[l], row(ffn_gain, l), row(ffn_bias, l), up_weight[l], row(up_bias, l),
            down_weight[l], row(down_bias, l))
        kept.append((hidden, a, q, k, v, o, lse, g, c, u, gp))
        hidden = following
    output = return_units(hidden.astype(BF), rows, group, member)
    dh = jnp.where(valid[:, :, None], cot.reshape(units, SLOTS, depth).astype(F32), 0.0).reshape(-1, depth)

    bufs, smalls = [None] * layers, [None] * layers
    for l in reversed(range(layers)):
        hidden, a, q, k, v, o, lse, g, c, u, gp = kept[l]
        wide, dg, dn_ffn, dbu = ffn_bwd(dh, u, gp, c, g, row(ffn_gain, l), up_weight[l], down_weight[l])
        narrow, dh, dn_attn = attn_bwd(
            lens, dg, o, q, k, v, lse, a, hidden, row(attn_gain, l), query_weight[l], key_weight[l], value_weight[l],
            output_weight[l])
        bufs[l] = (wide, narrow)
        smalls[l] = (dn_attn[0], dn_attn[1], dn_ffn[0], dn_ffn[1], dn_ffn[2], dbu[0])
    input_grad = return_units(dh.astype(BF), rows, group, member)

    if lax.axis_size("dp") == 4 and lax.axis_size("seq") == 8:
        shards = 8
        small = jnp.stack([jnp.concatenate([v.reshape(shards, -1) for v in s], axis=1) for s in smalls], axis=1)
        count = small.shape[1] * small.shape[2]
        small = small.reshape(shards, count)
        small = jnp.pad(small, ((0, 0), (0, 64 * depth - count))).reshape(shards, 64, depth).astype(BF)
        sums = [None] * layers
        for l in reversed(range(layers)):
            wide, narrow = bufs[l]
            if l == 0:
                narrow = jnp.concatenate([narrow, small], axis=1)
            sums[l] = (reduce_buffer(wide), reduce_buffer(narrow))
        small = sums[0][1][256:].reshape(-1)[:count].reshape(layers, -1).astype(F32)
        cuts = [depth // shards] * 5 + [ff // shards]
        ends = [sum(cuts[: n + 1]) for n in range(6)]
        pieces = [small[:, e - n : e] for e, n in zip(ends, cuts)]
        up, down, square = [], [], []
        for l in range(layers):
            wide, narrow = (v.astype(F32) for v in sums[l])
            down.append(wide[:, :256].T)
            up.append(wide[:, 256:].reshape(8, 64, 256).transpose(1, 0, 2).reshape(64, ff))
            square.append(narrow[:256].reshape(4, 64, depth))
        up, down = jnp.stack(up), jnp.stack(down)
        square = jnp.stack(square, axis=1)
        grads = (pieces[0], pieces[1], square[1], square[2], square[3], square[0], pieces[2], pieces[3], up, pieces[5],
                 down, pieces[4])
        return (output, input_grad) + grads

    full = []
    for l in range(layers):
        wide, narrow = bufs[l]
        down = wide[:, :, :256].transpose(0, 2, 1).reshape(ff, depth)
        up = wide[:, :, 256:].reshape(8, 8, 64, 256).transpose(0, 2, 1, 3).reshape(depth, ff)
        square = narrow.reshape(8, 4, 64, depth).transpose(1, 0, 2, 3).reshape(4, depth, depth)
        s = smalls[l]
        full.append((s[0], s[1], square[1], square[2], square[3], square[0], s[2], s[3], up, s[5], down, s[4]))
    grads = []
    for n in range(12):
        term = jnp.stack([full[l][n] for l in range(layers)]).astype(F32)
        share = lax.psum_scatter(term, "seq", scatter_dimension=1, tiled=True)
        grads.append(lax.psum(share.astype(BF), "dp").astype(F32))
    return (output, input_grad) + tuple(grads)


def solution(mesh):
    whole, split = jax.sharding.PartitionSpec(), jax.sharding.PartitionSpec("dp", "seq", None)
    spec = jax.sharding.PartitionSpec
    vec, mat = spec(None, "seq"), spec(None, "seq", None)
    return jax.shard_map(
        on_device,
        mesh=mesh,
        in_specs=(split, split, spec("dp", None)) + (whole,) * 12,
        out_specs=(split, split, vec, vec, mat, mat, mat, mat, vec, vec, mat, vec, mat, vec),
        check_vma=False,
    )
```

```python
import jax
import jax.numpy as jnp
from jax import lax
from jax.experimental import pallas as pl
from jax.experimental.pallas import tpu as pltpu

H = 8
SLOTS = 256
EPS = 1e-05
NEG = -1000000000.0
BF = jnp.bfloat16
F32 = jnp.float32
GELU_C = 0.7978845608028654
GELU_A = 0.044715
LIMIT = 60 << 20
STEP = 512
SHARDS = 8
FIRST = slice(0, 128)
SECOND = slice(128, 192)

NN = (((1,), (0,)), ((), ()))
NT = (((1,), (1,)), ((), ()))
TN = (((0,), (0,)), ((), ()))

SDS = jax.ShapeDtypeStruct
IN_VMEM = pl.BlockSpec(memory_space=pltpu.VMEM)
IN_SMEM = pl.BlockSpec(memory_space=pltpu.SMEM)
ANYWHERE = pl.BlockSpec(memory_space=pl.ANY)


def dot(left, right, form=NN):
    return lax.dot_general(left, right, form, preferred_element_type=F32)


def normalize(values):
    centered = values - jnp.mean(values, axis=-1, keepdims=True)
    inv = lax.rsqrt(jnp.mean(centered * centered, axis=-1, keepdims=True) + EPS)
    return centered * inv, inv


def norm_back(dy, values, gain):
    xhat, inv = normalize(values)
    dgain = jnp.sum(dy * xhat, axis=0, keepdims=True)
    dbias = jnp.sum(dy, axis=0, keepdims=True)
    dx = dy * gain
    dx = inv * (dx - jnp.mean(dx, axis=-1, keepdims=True) - xhat * jnp.mean(dx * xhat, axis=-1, keepdims=True))
    return dx, dgain, dbias


def head_masks(width):
    lane = lax.broadcasted_iota(jnp.int32, (1, 2 * width), 1)
    low = (lane < width).astype(F32).astype(BF)
    return low, (1.0 - low.astype(F32)).astype(BF)


def tiles(m):
    return [slice(SLOTS * i, SLOTS * (i + 1)) for i in range(m // SLOTS)]


def wait_all(copies):
    for copy in copies:
        copy.wait()


class Copies:
    def __init__(self, sems):
        self.sems, self.used, self.open = sems, 0, []

    def start(self, source, target):
        copy = pltpu.make_async_copy(source, target, self.sems.at[self.used])
        self.used += 1
        copy.start()
        return copy

    def load(self, *pairs):
        return [self.start(source, target) for source, target in pairs]

    def save(self, source, target):
        self.open.append(self.start(source, target))

    def finish(self):
        wait_all(self.open)


def call(body, name, operands, outs, scratch, sems, flops, moved, after=(), aliases=None):
    count, skip = len(operands), len(after)

    def run(*refs):
        refs = list(refs)
        body(*refs[:count], *refs[count + skip :])

    return pl.pallas_call(
        run,
        in_specs=[spec for _, spec in operands] + [ANYWHERE] * skip,
        out_specs=[spec for _, spec in outs],
        out_shape=[shape for shape, _ in outs],
        scratch_shapes=list(scratch) + ([pltpu.SemaphoreType.DMA((sems,))] if sems else []),
        compiler_params=pltpu.CompilerParams(vmem_limit_bytes=LIMIT),
        cost_estimate=pl.CostEstimate(flops=flops, bytes_accessed=moved, transcendentals=0),
        input_output_aliases=aliases or {},
        name=name,
    )(*[array for array, _ in operands], *after)


def pack_body(member, x_ref, *outs):
    for d, out in enumerate(outs):
        n = out.shape[0]
        out[...] = x_ref[pl.ds((member[0, 0] ^ (d + 1)) * n, n)]


def pack(member, local, group):
    rows, width, depth = local.shape
    shape = SDS((rows // group, width, depth), local.dtype)
    return call(pack_body, "pack", [(member, IN_SMEM), (local, IN_VMEM)], [(shape, IN_VMEM)] * (group - 1), [], 0, 0, 1 << 20)


def unpack_body(member, *refs):
    out = refs[-1]
    for d, ref in enumerate(refs[:-1]):
        n = ref.shape[0]
        out[pl.ds((member[0, 0] ^ d) * n, n)] = ref[...]


def unpack(member, pieces):
    n, width, depth = pieces[0].shape
    shape = SDS((n * len(pieces), width, depth), pieces[0].dtype)
    return call(unpack_body, "unpack", [(member, IN_SMEM)] + [(p, IN_VMEM) for p in pieces], [(shape, IN_VMEM)], [], 0, 0, 1 << 20)[0]


def regroup(member, lens, local, others, put):
    n, width, _ = others[0].shape
    j = member[0, 0]
    for d in range(len(others) + 1):
        for u in range(n):
            start = (j ^ d) * width
            at = pl.ds(pl.multiple_of(u * SLOTS + start, width), width)
            block = local[j * n + u] if d == 0 else others[d - 1][u]
            if lens is not None:
                slot = lax.broadcasted_iota(jnp.int32, (width, 1), 0) + start
                block = jnp.where(slot < lens[0, u], block.astype(F32), 0.0)
            put(at, block)


def deal(member, values, pieces):
    for d, piece in enumerate(pieces):
        n, width, _ = piece.shape
        for u in range(n):
            at = pl.ds(pl.multiple_of(u * SLOTS + (member[0, 0] ^ d) * width, width), width)
            piece[u] = values[at, :].astype(BF)


def forward_attention(lens, h, gain, bias, wq, wk, wv, a_ref, q_ref, k_ref, v_ref, o_ref, lse_ref, event):
    masks = head_masks(64)
    for i, rows in enumerate(tiles(h.shape[0])):
        xhat, _ = normalize(h[rows, :].astype(F32))
        a = (xhat * gain + bias).astype(BF)
        a_ref[rows, :] = a
        if i == 0:
            event("project")
        q_ref[rows, :] = (dot(a, wq[...]).astype(BF).astype(F32) * 0.125).astype(BF)
        k_ref[rows, :] = dot(a, wk[...]).astype(BF)
        v_ref[rows, :] = dot(a, wv[...]).astype(BF)
    event("attend")
    key = lax.broadcasted_iota(jnp.int32, (SLOTS, 1), 0)
    for i, rows in enumerate(tiles(h.shape[0])):
        valid = key < lens[0, i]
        for pair in range(H // 2):
            cols = slice(128 * pair, 128 * pair + 128)
            qp, kp, vp = q_ref[rows, cols], k_ref[rows, cols], v_ref[rows, cols]
            acc = None
            for hh in range(2):
                st = jnp.where(valid, dot(kp * masks[hh], qp, NT), NEG)
                top = jnp.max(st, axis=0, keepdims=True)
                e = jnp.exp(st - top)
                tot = jnp.sum(e, axis=0, keepdims=True)
                pt = (e * (1.0 / tot)).astype(BF)
                part = dot(pt, vp * masks[hh], TN)
                acc = part if acc is None else acc + part
                lse_ref[i * H + 2 * pair + hh, :] = (top + jnp.log(tot))[0]
            o_ref[rows, cols] = acc.astype(BF)


def forward_ffn(h, o, wo, gain, bias, wup, bup, wdown, bdown, g_ref, c_ref, u_ref, gp_ref, n_ref, event):
    m, ff = h.shape[0], wup.shape[1]
    event("mix")
    for rows in tiles(m):
        g = h[rows, :].astype(F32) + dot(o[rows, :], wo[...])
        g_ref[rows, :] = g
        xhat, _ = normalize(g)
        c_ref[rows, :] = (xhat * gain + bias).astype(BF)
    for f in range(ff // STEP):
        fs = slice(STEP * f, STEP * f + STEP)
        for rows in tiles(m):
            z = dot(c_ref[rows, :], wup[:, fs]) + bup[:, fs]
            z2 = z * z
            t = jnp.tanh(GELU_C * (z * (1.0 + GELU_A * z2)))
            half = 0.5 + 0.5 * t
            gp = half + (0.5 * z) * (1.0 - t * t) * (GELU_C * (1.0 + 3.0 * GELU_A * z2))
            u_ref[rows, fs] = (z * half).astype(BF)
            gp_ref[rows, fs] = gp.astype(BF)
        event(f)
    for rows in tiles(m):
        n_ref[rows, :] = g_ref[rows, :] + (dot(u_ref[rows, :], wdown[...]) + bdown)


def ffn_terms(dm_ref, u_ref, gp_ref, c_ref, wdown, buf, dz_ref, sm_ref, event):
    ff = u_ref.shape[1]
    event("down")
    dm = dm_ref[...]
    for f in range(ff // STEP):
        res = dot(dm, u_ref[:, STEP * f : STEP * f + STEP], TN)
        for t in range(2):
            buf[2 * f + t, :, :, 0:256] = res[:, 256 * t : 256 * t + 256].astype(BF).reshape(4, 128, 256)
    event("up")
    sm_ref[...] = jnp.zeros_like(sm_ref)
    sm_ref[0:1, :] = jnp.sum(dm.astype(F32), axis=0, keepdims=True)
    for f in range(ff // STEP):
        fs = slice(STEP * f, STEP * f + STEP)
        dz = (dot(dm, wdown[fs, :], NT) * gp_ref[:, fs].astype(F32)).astype(BF)
        dz_ref[:, fs] = dz
        sm_ref[1 + f : 2 + f, :] = jnp.sum(dz.astype(F32), axis=0, keepdims=True)
        res = dot(c_ref[...], dz, TN)
        for t in range(2):
            buf[:, f, 64 * t : 64 * t + 64, 256:512] = res[:, 256 * t : 256 * t + 256].astype(BF).reshape(SHARDS, 64, 256)


def save_terms(go, core, buf, keep, send, rows):
    for z in range(SHARDS // 2):
        at = 2 * (z % 2) + z // 2
        go.save(buf.at[2 * z + core[0, 0]], keep.at[:, at, rows])
        go.save(buf.at[2 * z + 1 - core[0, 0]], send.at[:, at, rows])


KEPT = ("a", "q", "k", "v", "o", "lse", "g", "c", "u", "gp")


def kept_shapes(m, d, ff):
    wide, narrow = (m, ff), (m, d)
    return [(narrow, BF)] * 5 + [((m // SLOTS * H, SLOTS), F32), (narrow, F32), (narrow, BF), (wide, BF), (wide, BF)]


def layer_weights(weights):
    return [(w, IN_VMEM if w.ndim == 2 else ANYWHERE) for w in weights]


def forward_body(l, go, lens, h, params, wts, held, saved, last, fetch_more):
    ag, ab, wq, wk, wv, wo, fg, fb, wup, bup, wdown, bdown = params
    vq, vk, vv, vo, vup, vdown = wts
    early = go.load((wq.at[l], vq), (wk.at[l], vk), (wv.at[l], vv))
    late = []
    fetch_more("start")

    def keep(*members):
        for s in members:
            if s in saved:
                go.save(held[s], saved[s])

    def event(name):
        if name == "project":
            wait_all(early)
            late.extend(go.load((wo.at[l], vo), (wup.at[l], vup), (wdown.at[l], vdown)))
        elif name == "attend":
            keep(0, 1, 2, 3)
        elif name == "mix":
            wait_all(late)
            keep(4, 5)
        elif name == 0:
            keep(6, 7)
        if name in (1, 3):
            fs = slice(1024 * (name // 2), 1024 * (name // 2) + 1024)
            for s in (8, 9):
                if s in saved:
                    go.save(held[s].at[:, fs], saved[s].at[:, fs])

    def row(ref):
        return ref[l : l + 1, :].astype(F32)

    a, q, k, v, o, lse, g, c, u, gp = held
    forward_attention(lens, h, row(ag), row(ab), vq, vk, vv, a, q, k, v, o, lse, event)
    forward_ffn(h, o, vo, row(fg), row(fb), vup, row(bup), vdown, row(bdown), g, c, u, gp, last, event)


def weight_scratch(d, ff):
    return [pltpu.VMEM((d, d), BF)] * 4 + [pltpu.VMEM((d, ff), BF), pltpu.VMEM((ff, d), BF)]


def forward_first(member, lens, local, others, weights):
    _, d, ff = weights[8].shape
    n, width, _ = others[0].shape
    count = len(others)
    m = n * (count + 1) * width
    per = kept_shapes(m, d, ff)

    def body(*refs):
        member, lens, local = refs[:3]
        others = refs[3 : 3 + count]
        params = refs[3 + count : 15 + count]
        saved = refs[15 + count : 27 + count]
        held = refs[27 + count : 37 + count]
        x_ref, last, *wts, sems = refs[37 + count :]
        go = Copies(sems)

        def place(name):
            def put(at, block):
                x_ref[at, :] = block

            regroup(member, None, local, others, put)
            go.save(x_ref, saved[10])

        forward_body(0, go, lens, x_ref, params, wts, held, dict(enumerate(saved[:10])), last, place)
        go.save(last, saved[11])
        go.finish()

    shapes = [SDS(s, t) for s, t in per] + [SDS((m, d), BF), SDS((m, d), F32)]
    res = call(
        body, "forward_first",
        [(member, IN_SMEM), (lens, IN_SMEM), (local, IN_VMEM)] + [(x, IN_VMEM) for x in others] + layer_weights(weights),
        [(s, ANYWHERE) for s in shapes],
        [pltpu.VMEM(s, t) for s, t in per] + [pltpu.VMEM((m, d), BF), pltpu.VMEM((m, d), F32)] + weight_scratch(d, ff),
        22, 2 * m * (4 * d * d + 2 * d * ff), 24 << 20)
    return res[:11], res[11]


def chunk_shape(rows):
    return SDS((4, SHARDS // 2, rows, 512), BF)


def forward_last(l, member, core, lens, h, local, others, weights):
    _, d, ff = weights[8].shape
    n, width, _ = others[0].shape
    count = len(others)
    m = n * (count + 1) * width
    per = kept_shapes(m, d, ff)

    def body(*refs):
        member, core, lens, h, local = refs[:5]
        others = refs[5 : 5 + count]
        params = refs[5 + count : 17 + count]
        refs = refs[17 + count :]
        saved, pieces = refs[:7], refs[7 : 8 + count]
        keep, send, dz_out, sm_ref = refs[8 + count : 12 + count]
        held = refs[12 + count : 22 + count]
        h_ref, last, dm_ref, dz_ref, buf, *wts, sems = refs[22 + count :]
        go = Copies(sems)
        first = go.load((h, h_ref))

        def place(name):
            def put(at, block):
                dm_ref[at, :] = block.astype(BF)

            regroup(member, lens, local, others, put)
            wait_all(first)

        forward_body(l, go, lens, h_ref, params, wts, held, dict(enumerate(saved)), last, place)
        deal(member, last, pieces)
        ffn_terms(dm_ref, held[8], held[9], held[7], wts[5], buf, dz_ref, sm_ref, lambda name: None)
        save_terms(go, core, buf, keep, send, slice(0, 128))
        go.save(dz_ref, dz_out)
        go.finish()

    outs = [(SDS(s, t), ANYWHERE) for s, t in per[:7]] + [(SDS((n, width, d), BF), IN_VMEM)] * (count + 1)
    outs += [(chunk_shape(128), ANYWHERE)] * 2 + [(SDS((m, ff), BF), ANYWHERE), (SDS((8, d), F32), IN_VMEM)]
    res = call(
        body, "forward_last",
        [(member, IN_SMEM), (core, IN_SMEM), (lens, IN_SMEM), (h, ANYWHERE), (local, IN_VMEM)] + [(x, IN_VMEM) for x in others]
        + layer_weights(weights),
        outs,
        [pltpu.VMEM(s, t) for s, t in per] + [pltpu.VMEM((m, d), F32)] * 2
        + [pltpu.VMEM((m, d), BF), pltpu.VMEM((m, ff), BF), pltpu.VMEM((SHARDS, 4, 128, 512), BF)] + weight_scratch(d, ff),
        28, 2 * m * (4 * d * d + 5 * d * ff), 24 << 20)
    return list(res[:7]) + [None, None, None, h], res[7 : 8 + count], res[8 + count : 10 + count], res[10 + count], res[11 + count]


def ffn_back(l, core, dm, kept, chunk, weights, after):
    c, u, gp = kept[7:10]
    m, ff = u.shape
    d = c.shape[1]
    wdown = weights[10]

    def body(core, dm, u, gp, c, wdown, k0, s0, keep, send, dz_out, sm_ref, vdm, vu, vgp, vc, vdown, buf, dz_ref, sems):
        go = Copies(sems)
        first = go.load((dm, vdm), (u, vu))
        later = []

        def event(name):
            if name == "down":
                wait_all(first)
                later.extend(go.load((wdown.at[l], vdown), (gp, vgp), (c, vc)))
            else:
                wait_all(later)

        ffn_terms(vdm, vu, vgp, vc, vdown, buf, dz_ref, sm_ref, event)
        save_terms(go, core, buf, keep, send, FIRST)
        go.save(dz_ref, dz_out)
        go.finish()

    v = pltpu.VMEM
    return call(
        body, "ffn_back",
        [(core, IN_SMEM)] + [(x, ANYWHERE) for x in (dm, u, gp, c, wdown, *chunk)],
        [(chunk_shape(192), ANYWHERE)] * 2 + [(SDS((m, ff), BF), ANYWHERE), (SDS((8, d), F32), IN_VMEM)],
        [v((m, d), BF), v((m, ff), BF), v((m, ff), BF), v((m, d), BF), v((ff, d), BF), v((SHARDS, 4, 128, 512), BF), v((m, ff), BF)],
        16, 2 * m * 3 * d * ff, 14 << 20, after, {6: 0, 7: 1})


def mid_back(l, flow, kept, dz, weights, after):
    g, o = kept[6], kept[4]
    m, ff = dz.shape
    d = g.shape[1]
    top = isinstance(flow, tuple)
    if top:
        member, lens, local, others = flow
        ops = [(member, IN_SMEM), (lens, IN_SMEM), (local, IN_VMEM)] + [(x, IN_VMEM) for x in others]
    else:
        ops = [(flow, ANYWHERE)]
    lead = len(ops)

    def body(*refs):
        source = refs[:lead]
        g, o, dz, gain, wup, wo, dg_out, do_ref, dout_ref, sm_ref, vg, vo, vdz, vup, vwo, dh_ref, dg_ref, dr_ref, sems = refs[lead:]
        go = Copies(sems)
        first = go.load((wup.at[l], vup), (dz, vdz))
        if top:
            def put(at, block):
                dh_ref[at, :] = block

            regroup(source[0], source[1], source[2], source[3:], put)
        later = go.load((g, vg), (wo.at[l], vwo), (o, vo))
        if not top:
            later += go.load((source[0], dh_ref))
        wait_all(first + later)
        dgain = dbias = None
        for i, rows in enumerate(tiles(m)):
            dc = dot(vdz[rows, :], vup[...], NT)
            dx, dg1, db1 = norm_back(dc, vg[rows, :], gain[l : l + 1, :].astype(F32))
            dg = dh_ref[rows, :] + dx
            dg_ref[rows, :] = dg
            dr_ref[rows, :] = dg.astype(BF)
            dgain, dbias = (dg1, db1) if i == 0 else (dgain + dg1, dbias + db1)
        go.save(dg_ref, dg_out)
        sm_ref[...] = jnp.zeros_like(sm_ref)
        sm_ref[0:1, :] = dgain
        sm_ref[1:2, :] = dbias
        do_ref[...] = dot(dr_ref[...], vwo[...], NT).astype(BF)
        dout_ref[...] = dot(vo[...], dr_ref[...], TN).astype(BF).reshape(SHARDS, d // SHARDS, d)
        go.finish()

    v = pltpu.VMEM
    return call(
        body, "mid_back",
        ops + [(g, ANYWHERE), (o, ANYWHERE), (dz, ANYWHERE), (weights[6], IN_VMEM), (weights[8], ANYWHERE), (weights[5], ANYWHERE)],
        [(SDS((m, d), F32), ANYWHERE), (SDS((m, d), BF), IN_VMEM), (SDS((SHARDS, d // SHARDS, d), BF), IN_VMEM), (SDS((8, d), F32), IN_VMEM)],
        [v((m, d), F32), v((m, d), BF), v((m, ff), BF), v((d, ff), BF), v((d, d), BF), v((m, d), F32), v((m, d), F32), v((m, d), BF)],
        8, 2 * m * (d * ff + 2 * d * d), 9 << 20, after)


def attn_back(l, member, core, lens, dg, do, dout, smalls, kept, weights, piece, after):
    a, q, k, v, o, lse, g, c, u, gp, h = kept
    m, d = dg.shape
    bottom = l == 0
    rows_of = slice(0, 80) if bottom else SECOND
    width = 80 if bottom else 64
    count = len(smalls)

    def body(*refs):
        member, core, lens = refs[:3]
        dg, do, dout, lse, q, k, v, a, h, wq, wk, wv, gain = refs[3:16]
        smalls = refs[16 : 16 + count]
        refs = refs[16 + count :]
        keep, send, *outs = refs[: 6 if bottom else 5]
        vdg, vdo, vdout, vlse, vq, vk, vv, va, vh, vwq, vwk, vwv, buf, dh_ref, dm_ref, dq_ref, dk_ref, dv_ref, sems = refs[6 if bottom else 5 :]
        go = Copies(sems)
        first = go.load((do, vdo), (lse, vlse), (q, vq), (k, vk), (v, vv))
        wait_all(first)
        later = go.load((a, va), (h, vh), (wq.at[l], vwq), (wk.at[l], vwk), (wv.at[l], vwv), (dg, vdg), (dout, vdout))
        masks = head_masks(64)
        key = lax.broadcasted_iota(jnp.int32, (SLOTS, 1), 0)
        for i, rows in enumerate(tiles(m)):
            valid = key < lens[0, i]
            for pair in range(H // 2):
                cols = slice(128 * pair, 128 * pair + 128)
                qp, kp, vp, dop = vq[rows, cols], vk[rows, cols], vv[rows, cols], vdo[rows, cols]
                dq = dk = dv = None
                for hh in range(2):
                    mk = masks[hh]
                    km = kp * mk
                    st = jnp.where(valid, dot(km, qp, NT), NEG)
                    pt = jnp.exp(st - vlse[i * H + 2 * pair + hh, :][None, :])
                    dpt = dot(vp * mk, dop, NT)
                    delta = jnp.sum(pt * dpt, axis=0, keepdims=True)
                    dst = (pt * (dpt - delta)).astype(BF)
                    p1 = dot(dst, km, TN)
                    p2 = dot(dst, qp * mk)
                    p3 = dot(pt.astype(BF), dop * mk)
                    dq, dk, dv = (p1, p2, p3) if dq is None else (dq + p1, dk + p2, dv + p3)
                dq_ref[rows, cols] = (dq * 0.125).astype(BF)
                dk_ref[rows, cols] = dk.astype(BF)
                dv_ref[rows, cols] = dv.astype(BF)
        wait_all(later)
        at = va[...]
        buf[:, 0, 0:64, :] = vdout[...]
        for n, ref in enumerate((dq_ref, dk_ref, dv_ref)):
            buf[:, n + 1, 0:64, :] = dot(at, ref[...], TN).astype(BF).reshape(SHARDS, 64, d)
        if not bottom:
            save_terms(go, core, buf, keep, send, rows_of)
        dgain = dbias = None
        for i, rows in enumerate(tiles(m)):
            da = dot(dq_ref[rows, :], vwq[...], NT) + dot(dk_ref[rows, :], vwk[...], NT) + dot(dv_ref[rows, :], vwv[...], NT)
            dx, dg1, db1 = norm_back(da, vh[rows, :].astype(F32), gain[l : l + 1, :].astype(F32))
            dh = vdg[rows, :] + dx
            dh_ref[rows, :] = dh
            dm_ref[rows, :] = dh.astype(BF)
            dgain, dbias = (dg1, db1) if i == 0 else (dgain + dg1, dbias + db1)
        if bottom:
            attn1, mid0, mid1, ffn0, ffn1 = smalls
            rows = [dgain, attn1[0:1, :], dbias, attn1[1:2, :], mid0[0:1, :], mid1[0:1, :], mid0[1:2, :], mid1[1:2, :],
                    ffn0[0:1, :], ffn1[0:1, :]]
            zero = jnp.zeros((1, d), F32)
            block = jnp.concatenate(rows + [zero] * 6, axis=0).astype(BF)
            other = jnp.concatenate([ffn0[1:5, :], ffn1[1:5, :]] + [zero] * 8, axis=0).astype(BF)
            for s in range(SHARDS):
                buf[s, 0, 64:80, :] = block
                buf[s, 1, 64:80, :] = other
                for t in (2, 3):
                    buf[s, t, 64:80, :] = jnp.zeros((16, d), BF)
            save_terms(go, core, buf, keep, send, rows_of)
            deal(member, dh_ref, outs)
        else:
            go.save(dh_ref, outs[0])
            go.save(dm_ref, outs[1])
            outs[2][...] = jnp.zeros_like(outs[2])
            outs[2][0:1, :] = dgain
            outs[2][1:2, :] = dbias
        go.finish()

    vm = pltpu.VMEM
    narrow = vm((m, d), BF)
    outs = [(chunk_shape(80 if bottom else 192), ANYWHERE)] * 2
    if bottom:
        outs += [(SDS(piece, BF), IN_VMEM)] * 4
    else:
        outs += [(SDS((m, d), F32), ANYWHERE), (SDS((m, d), BF), ANYWHERE), (SDS((8, d), F32), IN_VMEM)]
    ins = [dg, do, dout, lse, q, k, v, a, h, weights[2], weights[3], weights[4]]
    return call(
        body, "attn_back",
        [(member, IN_SMEM), (core, IN_SMEM), (lens, IN_SMEM)] + [(x, ANYWHERE) for x in ins] + [(weights[0], IN_VMEM)]
        + [(x, IN_VMEM) for x in smalls],
        outs,
        [vm((m, d), F32), narrow, vm(dout.shape, BF), vm(lse.shape, F32)] + [narrow] * 4 + [vm((m, d), h.dtype)] + [vm((d, d), BF)] * 3
        + [vm((SHARDS, 4, width, d), BF), vm((m, d), F32)] + [narrow] * 4,
        22, 2 * m * 10 * d * d, 12 << 20, after)


def finish_wide(order, wide1, mixed, d, ff):
    def body(order, *refs):
        w, x = refs[:4], refs[4:8]
        down, up, *square = refs[8:14]
        vdown, vup, vsq, sems = refs[14:]
        go = Copies(sems)
        for n in range(4):
            at = order[0, n]
            for l, ref in ((1, w[n]), (0, x[n])):
                part = ref[0:128, :].astype(F32)
                vdown[l, :, pl.ds(pl.multiple_of(at * 128, 128), 128)] = part[:, 0:256].T
                for t in range(2):
                    vup[l, :, pl.ds(pl.multiple_of(at * 512 + 256 * t, 256), 256)] = part[64 * t : 64 * t + 64, 256:512]
            vsq[at] = x[n][128:192, :].astype(F32)
        go.save(vdown, down)
        go.save(vup, up)
        for n in range(4):
            go.save(vsq.at[n], square[n].at[1])
        go.finish()

    ops = [(order, IN_SMEM)] + [(x, IN_VMEM) for x in (*wide1, *mixed)]
    sq = (SDS((2, 64, d), F32), ANYWHERE)
    return call(body, "finish_wide", ops, [(SDS((2, 256, d), F32), ANYWHERE), (SDS((2, 64, ff), F32), ANYWHERE)] + [sq] * 4,
                [pltpu.VMEM((2, 256, d), F32), pltpu.VMEM((2, 64, ff), F32), pltpu.VMEM((4, 64, d), F32)], 6, 0, 6 << 20)


def finish_last(order, shard, narrow, square, d, ff):
    def body(order, shard, *refs):
        x = refs[:4]
        outs = refs[8:12]
        ag, ab, fg, fb, bd, bu = refs[12:18]
        vsq, vsm, sems = refs[18:]
        go = Copies(sems)
        for n in range(4):
            at = order[0, n]
            vsq[at] = x[n][0:64, :].astype(F32)
            vsm[at] = x[n][64:80, :].astype(F32)
        for n in range(4):
            go.save(vsq.at[n], outs[n].at[0])
        s = shard[0, 0]
        pair = vsm[0, :, pl.ds(pl.multiple_of((s // 2) * 128, 128), 128)]
        mine = jnp.where(s % 2 == 0, pair[:, 0:64], pair[:, 64:128])
        for n, ref in enumerate((ag, ab, fg, fb, bd)):
            ref[...] = mine[2 * n : 2 * n + 2, :]
        for l in range(2):
            bu[l : l + 1, :] = vsm[1, pl.ds(4 * l + s // 2, 1), pl.ds(pl.multiple_of((s % 2) * 256, 256), 256)]
        go.finish()

    ops = [(order, IN_SMEM), (shard, IN_SMEM)] + [(x, IN_VMEM) for x in narrow] + [(x, ANYWHERE) for x in square]
    sq = (SDS((2, 64, d), F32), ANYWHERE)
    return call(body, "finish_last", ops, [sq] * 4 + [(SDS((2, 64), F32), IN_VMEM)] * 5 + [(SDS((2, 256), F32), IN_VMEM)],
                [pltpu.VMEM((4, 64, d), F32), pltpu.VMEM((4, 16, d), F32)], 4, 0, 2 << 20, (), {6: 0, 7: 1, 8: 2, 9: 3})


def take(array, index, axis=0):
    return lax.dynamic_index_in_dim(array, index, axis, keepdims=False)


def add(left, right):
    return (left.astype(F32) + right.astype(F32)).astype(BF)


def swap(sends):
    size = lax.axis_size("seq")
    return [lax.ppermute(s, "seq", [(i, i ^ (d + 1)) for i in range(size)]) for d, s in enumerate(sends)]


BOTH = ("dp", "seq")


def pairs_of(flip):
    out = []
    for y in range(2):
        for x in range(2):
            for z in range(4):
                for c in range(2):
                    y2, x2, z2, c2 = flip(y, x, z, c)
                    out.append((y * 16 + x * 8 + z * 2 + c, y2 * 16 + x2 * 8 + z2 * 2 + c2))
    return out


CORE = pairs_of(lambda y, x, z, c: (y, x, z, 1 - c))
PLANE_1 = pairs_of(lambda y, x, z, c: (y, 1 - x, z, c) if c == 0 else (1 - y, x, z, c))
PLANE_2 = pairs_of(lambda y, x, z, c: (y, 1 - x, z, c) if c == 1 else (1 - y, x, z, c))
LINE_1 = pairs_of(lambda y, x, z, c: (y, x, z ^ 1, c))
LINE_2 = pairs_of(lambda y, x, z, c: (y, x, z ^ 2, c))


class Reduction:
    def __init__(self, halves):
        dp, seq = lax.axis_index("dp"), lax.axis_index("seq")
        core, z = seq % 2, seq // 2
        y, x = dp // 2, dp % 2
        first, second = jnp.where(core == 0, x, y), jnp.where(core == 0, y, x)
        self.steps = [(PLANE_1, first), (PLANE_2, second), (LINE_1, z % 2), (LINE_2, z // 2)]
        self.kept = halves[0].reshape((16,) + halves[0].shape[2:])
        self.moved = lax.ppermute(halves[1].reshape(self.kept.shape), BOTH, CORE)

    def step(self, *others):
        pairs, bit = self.steps.pop(0)
        half = self.kept.shape[0] // 2
        view = (2, half) + self.kept.shape[1:]
        kept, moved = self.kept.reshape(view), self.moved.reshape(view)
        sent = add(take(kept, 1 - bit), take(moved, 1 - bit))
        self.kept = add(take(kept, bit), take(moved, bit))
        sent, *others = lax.optimization_barrier((sent, *others))
        self.moved = lax.ppermute(sent, BOTH, pairs)
        return others

    def result(self):
        mine = add(self.kept, self.moved)[0]
        other = lax.ppermute(mine, BOTH, PLANE_2)
        far = lax.ppermute(jnp.concatenate([mine, other], axis=0), BOTH, PLANE_1)
        return [mine, other, far[: mine.shape[0]], far[mine.shape[0] :]]


def scattered(term):
    share = lax.psum_scatter(term.astype(F32), "seq", scatter_dimension=1, tiled=True)
    return lax.psum(share.astype(BF), "dp").astype(F32)


def joined(halves):
    quarters, _, rows, width = halves[0].shape
    shards = jnp.stack([half.reshape(quarters, 2, 2, rows, width) for half in halves])
    return shards.transpose(3, 2, 0, 1, 4, 5).reshape(SHARDS, quarters, rows, width)


def plain_sums(wide1, mixed, narrow, d, ff):
    wide1, mixed, narrow = joined(wide1), joined(mixed), joined(narrow)
    down, up, square = [], [], []
    for wide, part in ((mixed[:, :, :128], narrow[:, :, :64]), (wide1, mixed[:, :, 128:])):
        wide = wide.reshape(SHARDS, 512, 512)
        down.append(wide[:, :, :256].transpose(0, 2, 1).reshape(ff, d))
        up.append(wide[:, :, 256:].reshape(SHARDS, ff // 256, d // SHARDS, 256).transpose(0, 2, 1, 3).reshape(d, ff))
        square.append(part.transpose(1, 0, 2, 3).reshape(4, d, d))
    square = jnp.stack(square, axis=1)
    small = narrow[0, 0, 64:74].reshape(5, 2, d)
    bias = narrow[0, 1, 64:72].reshape(2, ff)
    terms = (small[0], small[1], square[1], square[2], square[3], square[0], small[2], small[3], jnp.stack(up), bias,
             jnp.stack(down), small[4])
    return tuple(scattered(term) for term in terms)


def on_device(
    inputs, cotangent, item_lengths, attn_gain, attn_bias, query_weight, key_weight, value_weight, output_weight,
    ffn_gain, ffn_bias, up_weight, up_bias, down_weight, down_bias,
):
    rows, width, depth = inputs.shape
    ff = up_weight.shape[2]
    group = SLOTS // width
    seq = lax.axis_index("seq")
    slot, item = seq % group, seq // group
    mine = take(item_lengths.reshape(group, rows // group, -1), slot)
    lens = take(mine, item, 1).reshape(1, -1)
    halving = lax.axis_size("dp") == 4 and lax.axis_size("seq") == 8
    member = slot.reshape(1, 1)
    core = (seq % 2 if halving else seq * 0).reshape(1, 1)
    weights = (
        attn_gain, attn_bias, query_weight, key_weight, value_weight, output_weight,
        ffn_gain, ffn_bias, up_weight, up_bias, down_weight, down_bias,
    )
    x_parts = swap(pack(member, inputs, group))
    cot_parts = swap(pack(member, cotangent, group))
    kept0, h1 = forward_first(member, lens, inputs, x_parts, weights)
    kept1, pieces, wide1, dz1, ffn1 = forward_last(1, member, core, lens, h1, cotangent, cot_parts, weights)
    output = unpack(member, [pieces[0]] + swap(pieces[1:]))

    if halving:
        sum1 = Reduction(wide1)
    dg, do, dout, mid1 = mid_back(1, (member, lens, cotangent, cot_parts), kept1, dz1, weights, ())
    if halving:
        dg, do = sum1.step(dg, do)
    *mixed, dh, dm, attn1 = attn_back(1, member, core, lens, dg, do, dout, (), kept1, weights, None, ())
    if halving:
        dm, = sum1.step(dm)
    *mixed, dz0, ffn0 = ffn_back(0, core, dm, kept0, mixed, weights, ())
    if halving:
        mixed[0], mixed[1], dz0 = sum1.step(mixed[0], mixed[1], dz0)
        sum2 = Reduction(mixed)
    dg, do, dout, mid0 = mid_back(0, dh, kept0, dz0, weights, ())
    if halving:
        dg, = sum2.step(dg)
        do, = sum1.step(do)
    *narrow, p0, p1, p2, p3 = attn_back(
        0, member, core, lens, dg, do, dout, (attn1, mid0, mid1, ffn0, ffn1), kept0, weights, pieces[0].shape, ())
    input_grad = unpack(member, [p0] + swap([p1, p2, p3]))
    if not halving:
        return (output, input_grad) + plain_sums(wide1, mixed, narrow, depth, ff)

    sum3 = Reduction(narrow)
    sum2.step()
    sum3.step()
    wide1 = sum1.result()
    sum2.step()
    sum3.step()
    sum2.step()
    sum3.step()
    mixed = sum2.result()
    sum3.step()
    narrow = sum3.result()
    dp = lax.axis_index("dp")
    y, x = dp // 2, dp % 2
    first, second = jnp.where(core[0, 0] == 0, x, y), jnp.where(core[0, 0] == 0, y, x)
    own = 2 * first + second
    order = jnp.stack([own, own ^ 1, own ^ 2, own ^ 3]).reshape(1, 4)
    down, up, *square = finish_wide(order, wide1, mixed, depth, ff)
    do, dq, dk, dv, ag, ab, fg, fb, bd, bu = finish_last(order, seq.reshape(1, 1), narrow, square, depth, ff)
    return output, input_grad, ag, ab, dq, dk, dv, do, fg, fb, up, bu, down, bd


def solution(mesh):
    spec = jax.sharding.PartitionSpec
    whole, split = spec(), spec("dp", "seq", None)
    vec, mat = spec(None, "seq"), spec(None, "seq", None)
    return jax.shard_map(
        on_device,
        mesh=mesh,
        in_specs=(split, split, spec("dp", None)) + (whole,) * 12,
        out_specs=(split, split, vec, vec, mat, mat, mat, mat, vec, vec, mat, vec, mat, vec),
        check_vma=False,
    )
```

```python
import jax
import jax.numpy as jnp
from jax import lax
from jax.experimental import pallas as pl
from jax.experimental.pallas import tpu as pltpu

H = 8
SLOTS = 256
EPS = 1e-05
NEG = -1000000000.0
BF = jnp.bfloat16
F32 = jnp.float32
GELU_C = 0.7978845608028654
GELU_A = 0.044715
STEP = 512
SHARDS = 8
LONG = 30_000_000_000
SECOND = slice(128, 192)

NN = (((1,), (0,)), ((), ()))
NT = (((1,), (1,)), ((), ()))
TN = (((0,), (0,)), ((), ()))

SDS = jax.ShapeDtypeStruct
IN_VMEM = pl.BlockSpec(memory_space=pltpu.VMEM)
IN_SMEM = pl.BlockSpec(memory_space=pltpu.SMEM)


def dot(left, right, form=NN):
    return lax.dot_general(left, right, form, preferred_element_type=F32)


def normalize(values):
    centered = values - jnp.mean(values, axis=-1, keepdims=True)
    inv = lax.rsqrt(jnp.mean(centered * centered, axis=-1, keepdims=True) + EPS)
    return centered * inv, inv


def norm_back(dy, values, gain):
    xhat, inv = normalize(values)
    dgain = jnp.sum(dy * xhat, axis=0, keepdims=True)
    dbias = jnp.sum(dy, axis=0, keepdims=True)
    dx = dy * gain
    dx = inv * (dx - jnp.mean(dx, axis=-1, keepdims=True) - xhat * jnp.mean(dx * xhat, axis=-1, keepdims=True))
    return dx, dgain, dbias


def head_masks(width):
    lane = lax.broadcasted_iota(jnp.int32, (1, 2 * width), 1)
    low = (lane < width).astype(F32).astype(BF)
    return low, (1.0 - low.astype(F32)).astype(BF)


def tiles(m):
    return [slice(SLOTS * i, SLOTS * (i + 1)) for i in range(m // SLOTS)]


def call(body, name, operands, outs, scratch, limit, flops, moved):
    return pl.pallas_call(
        body,
        in_specs=[IN_SMEM if x.dtype == jnp.int32 else IN_VMEM for x in operands],
        out_specs=[IN_VMEM] * len(outs),
        out_shape=[SDS(*out) for out in outs],
        scratch_shapes=[pltpu.VMEM(*x) for x in scratch],
        compiler_params=pltpu.CompilerParams(vmem_limit_bytes=limit << 20),
        cost_estimate=pl.CostEstimate(flops=flops, bytes_accessed=moved, transcendentals=0),
        name=name,
    )(*operands)


def member_of(group):
    return lax.axis_index("seq") % group


def lengths_of(lengths, units, group):
    seq = lax.axis_index("seq")
    return [lengths[seq // group, (seq % group) * units + u] for u in range(units)]


def pack(local, group):
    rows, width, depth = local.shape
    n = rows // group

    def body(x_ref, *outs):
        for d, out in enumerate(outs):
            out[...] = x_ref[pl.ds((member_of(group) ^ d) * n, n)]

    return call(body, "pack", [local], [((n, width, depth), local.dtype)] * group, [], 4, 20_000_000_000, 1 << 20)


def unpack(pieces):
    _, n, width, depth = pieces[0].shape

    def body(*refs):
        outs = refs[-2:]
        for d, ref in enumerate(refs[:-2]):
            for t in range(2):
                outs[t][pl.ds((member_of(len(pieces)) ^ d) * n, n)] = ref[t]

    return call(body, "unpack", pieces, [((n * len(pieces), width, depth), BF)] * 2, [], 4, 0, 1 << 20)


def regroup(lens, pieces, put):
    n, width, _ = pieces[0].shape
    j = member_of(len(pieces))
    for d, piece in enumerate(pieces):
        for u in range(n):
            start = (j ^ d) * width
            at = pl.ds(pl.multiple_of(u * SLOTS + start, width), width)
            block = piece[u]
            if lens is not None:
                slot = lax.broadcasted_iota(jnp.int32, (width, 1), 0) + start
                block = jnp.where(slot < lens[u], block.astype(F32), 0.0)
            put(at, block)


def deal(values, pieces):
    for d, piece in enumerate(pieces):
        n, width, _ = piece.shape
        for u in range(n):
            at = pl.ds(pl.multiple_of(u * SLOTS + (member_of(len(pieces)) ^ d) * width, width), width)
            piece[u] = values[at, :].astype(BF)


def forward_attention(lens, h, gain, bias, wq, wk, wv, a_ref, q_ref, k_ref, v_ref, o_ref, lse_ref):
    masks = head_masks(64)
    for i, rows in enumerate(tiles(h.shape[0])):
        xhat, _ = normalize(h[rows, :].astype(F32))
        a = (xhat * gain + bias).astype(BF)
        a_ref[rows, :] = a
        q_ref[rows, :] = (dot(a, wq[...]).astype(BF).astype(F32) * 0.125).astype(BF)
        k_ref[rows, :] = dot(a, wk[...]).astype(BF)
        v_ref[rows, :] = dot(a, wv[...]).astype(BF)
    key = lax.broadcasted_iota(jnp.int32, (SLOTS, 1), 0)
    for i, rows in enumerate(tiles(h.shape[0])):
        valid = key < lens[i]
        for pair in range(H // 2):
            cols = slice(128 * pair, 128 * pair + 128)
            qp, kp, vp = q_ref[rows, cols], k_ref[rows, cols], v_ref[rows, cols]
            acc = None
            for hh in range(2):
                st = jnp.where(valid, dot(kp * masks[hh], qp, NT), NEG)
                top = jnp.max(st, axis=0, keepdims=True)
                e = jnp.exp(st - top)
                tot = jnp.sum(e, axis=0, keepdims=True)
                pt = (e * (1.0 / tot)).astype(BF)
                part = dot(pt, vp * masks[hh], TN)
                acc = part if acc is None else acc + part
                lse_ref[i * H + 2 * pair + hh, :] = (top + jnp.log(tot))[0]
            o_ref[rows, cols] = acc.astype(BF)


def forward_ffn(h, o, wo, gain, bias, wup, bup, wdown, bdown, g_ref, c_ref, u_ref, gp_ref, n_ref):
    m, ff = h.shape[0], wup.shape[1]
    for rows in tiles(m):
        g = h[rows, :].astype(F32) + dot(o[rows, :], wo[...])
        g_ref[rows, :] = g
        xhat, _ = normalize(g)
        c_ref[rows, :] = (xhat * gain + bias).astype(BF)
    for f in range(ff // STEP):
        fs = slice(STEP * f, STEP * f + STEP)
        for rows in tiles(m):
            z = dot(c_ref[rows, :], wup[:, fs]) + bup[:, fs]
            z2 = z * z
            t = jnp.tanh(GELU_C * (z * (1.0 + GELU_A * z2)))
            half = 0.5 + 0.5 * t
            gp = half + (0.5 * z) * (1.0 - t * t) * (GELU_C * (1.0 + 3.0 * GELU_A * z2))
            u_ref[rows, fs] = (z * half).astype(BF)
            gp_ref[rows, fs] = gp.astype(BF)
    for rows in tiles(m):
        n_ref[rows, :] = g_ref[rows, :] + (dot(u_ref[rows, :], wdown[...]) + bdown)


def store(core, keep, send, quarter, z, rows, cols, even, odd):
    mine, other = jnp.where(core == 0, even, odd), jnp.where(core == 0, odd, even)
    at = 2 * (z % 2) + z // 2
    keep[quarter, at, rows, cols] = mine
    send[quarter, at, rows, cols] = other


def ffn_terms(core, dm_ref, u_ref, gp_ref, c_ref, wdown, keep, send, dz_ref, sm_ref):
    ff = u_ref.shape[1]
    dm = dm_ref[...]
    for f in range(ff // STEP):
        res = dot(dm, u_ref[:, STEP * f : STEP * f + STEP], TN).astype(BF).reshape(4, 128, STEP)
        store(core, keep, send, slice(None), f, slice(0, 128), slice(0, 256), res[:, :, 0:256], res[:, :, 256:512])
    sm_ref[...] = jnp.zeros_like(sm_ref)
    sm_ref[0:1, :] = jnp.sum(dm.astype(F32), axis=0, keepdims=True)
    for f in range(ff // STEP):
        fs = slice(STEP * f, STEP * f + STEP)
        dz = (dot(dm, wdown[fs, :], NT) * gp_ref[:, fs].astype(F32)).astype(BF)
        dz_ref[:, fs] = dz
        sm_ref[1 + f : 2 + f, :] = jnp.sum(dz.astype(F32), axis=0, keepdims=True)
        res = dot(c_ref[...], dz, TN).astype(BF).reshape(4, 128, STEP)
        for t in range(2):
            rows, part = slice(64 * t, 64 * t + 64), res[:, :, 256 * t : 256 * t + 256]
            for z in range(4):
                store(core, keep, send, f, z, rows, slice(256, 512), part[z, 0:64], part[z, 64:128])


KEPT = ("a", "q", "k", "v", "o", "lse", "g", "c", "u", "gp")


def kept_shapes(m, d, ff):
    wide, narrow = (m, ff), (m, d)
    return [(narrow, BF)] * 5 + [((m // SLOTS * H, SLOTS), F32), (narrow, F32), (narrow, BF), (wide, BF), (wide, BF)]


def row(ref, l):
    return ref[l : l + 1, :].astype(F32)


def forward_layer(l, lens, h, norms, wts, kept, last):
    ag, ab, fg, fb, bup, bdown = norms
    wq, wk, wv, wo, wup, wdown = [w.at[l] for w in wts]
    a, q, k, v, o, lse, g, c, u, gp = kept
    forward_attention(lens, h, row(ag, l), row(ab, l), wq, wk, wv, a, q, k, v, o, lse)
    forward_ffn(h, o, wo, row(fg, l), row(fb, l), wup, row(bup, l), wdown, row(bdown, l), g, c, u, gp, last)


def chunk_shape(rows):
    return ((4, SHARDS // 2, rows, 512), BF)


def parity(halving):
    return lax.axis_index("seq") % 2 if halving else 0


def forward_first(lengths, parts, norms, wts):
    _, d, ff = wts[4].shape
    n, width, _ = parts[0].shape
    group = len(parts)
    m = n * group * width

    def body(*refs):
        lengths, refs = refs[0], refs[1:]
        parts, refs = refs[:group], refs[group:]
        norms, wts, kept, (x_ref, last) = refs[:6], refs[6:12], refs[12:22], refs[22:]

        def put(at, block):
            x_ref[at, :] = block

        regroup(None, parts, put)
        forward_layer(0, lengths_of(lengths, n, group), x_ref, norms, wts, kept, last)

    outs = kept_shapes(m, d, ff) + [((m, d), BF), ((m, d), F32)]
    res = call(body, "forward_first", [lengths, *parts, *norms, *wts], outs, [], 12, 2 * m * (4 * d * d + 2 * d * ff), 24 << 20)
    return res[:11], res[11]


def forward_last(l, halving, lengths, h, parts, norms, wts):
    _, d, ff = wts[4].shape
    n, width, _ = parts[0].shape
    group = len(parts)
    m = n * group * width
    per = kept_shapes(m, d, ff)

    def body(*refs):
        lengths, h = refs[:2]
        refs = refs[2:]
        parts, refs = refs[:group], refs[group:]
        norms, wts, refs = refs[:6], refs[6:12], refs[12:]
        kept, pieces, refs = refs[:7], refs[7 : 7 + group], refs[7 + group :]
        keep, send, dz_ref, sm_ref, c, u, gp, last, dm_ref = refs
        lens = lengths_of(lengths, n, group)

        def put(at, block):
            dm_ref[at, :] = block.astype(BF)

        regroup(lens, parts, put)
        forward_layer(l, lens, h, norms, wts, [*kept, c, u, gp], last)
        deal(last, pieces)
        ffn_terms(parity(halving), dm_ref, u, gp, c, wts[5].at[l], keep, send, dz_ref, sm_ref)

    outs = per[:7] + [((n, width, d), BF)] * group + [chunk_shape(128)] * 2 + [((m, ff), BF), ((8, d), F32)]
    res = call(
        body, "forward_last", [lengths, h, *parts, *norms, *wts], outs,
        per[7:] + [((m, d), F32), ((m, d), BF)], 20, 2 * m * (4 * d * d + 5 * d * ff), 24 << 20)
    res, keep, send, dz, sums = res[:-4], *res[-4:]
    return list(res[:7]) + [None, None, None, h], res[7:], (keep, send), dz, sums


def mid_terms(l, dh_ref, g, o, dz, gain, wup, wo, dg_ref, do_ref, dr_ref, sm_ref):
    m, d = g.shape
    dgain = dbias = None
    for i, rows in enumerate(tiles(m)):
        dc = dot(dz[rows, :], wup[l], NT)
        dx, dg1, db1 = norm_back(dc, g[rows, :], row(gain, l))
        dg = dh_ref[rows, :] + dx
        dg_ref[rows, :] = dg
        dr_ref[rows, :] = dg.astype(BF)
        dgain, dbias = (dg1, db1) if i == 0 else (dgain + dg1, dbias + db1)
    sm_ref[...] = jnp.zeros_like(sm_ref)
    sm_ref[0:1, :] = dgain
    sm_ref[1:2, :] = dbias
    do_ref[...] = dot(dr_ref[...], wo[l], NT).astype(BF)
    return dot(o[...], dr_ref[...], TN).astype(BF).reshape(SHARDS // 2, 2, d // SHARDS, d)


def attn_terms(l, lens, dg, do, lse, q, k, v, a, h, gain, wq, wk, wv, dq_ref, dk_ref, dv_ref, put):
    m, d = dg.shape
    masks = head_masks(64)
    key = lax.broadcasted_iota(jnp.int32, (SLOTS, 1), 0)
    for i, rows in enumerate(tiles(m)):
        valid = key < lens[i]
        for pair in range(H // 2):
            cols = slice(128 * pair, 128 * pair + 128)
            qp, kp, vp, dop = q[rows, cols], k[rows, cols], v[rows, cols], do[rows, cols]
            dq = dk = dv = None
            for hh in range(2):
                mk = masks[hh]
                km = kp * mk
                st = jnp.where(valid, dot(km, qp, NT), NEG)
                pt = jnp.exp(st - lse[i * H + 2 * pair + hh, :][None, :])
                dpt = dot(vp * mk, dop, NT)
                delta = jnp.sum(pt * dpt, axis=0, keepdims=True)
                dst = (pt * (dpt - delta)).astype(BF)
                p1 = dot(dst, km, TN)
                p2 = dot(dst, qp * mk)
                p3 = dot(pt.astype(BF), dop * mk)
                dq, dk, dv = (p1, p2, p3) if dq is None else (dq + p1, dk + p2, dv + p3)
            dq_ref[rows, cols] = (dq * 0.125).astype(BF)
            dk_ref[rows, cols] = dk.astype(BF)
            dv_ref[rows, cols] = dv.astype(BF)
    terms = [dot(a[...], ref[...], TN).astype(BF).reshape(SHARDS // 2, 2, 64, d) for ref in (dq_ref, dk_ref, dv_ref)]
    dgain = dbias = None
    for i, rows in enumerate(tiles(m)):
        da = dot(dq_ref[rows, :], wq[l], NT) + dot(dk_ref[rows, :], wk[l], NT) + dot(dv_ref[rows, :], wv[l], NT)
        dx, dg1, db1 = norm_back(da, h[rows, :].astype(F32), row(gain, l))
        put(rows, dg[rows, :] + dx)
        dgain, dbias = (dg1, db1) if i == 0 else (dgain + dg1, dbias + db1)
    return terms, dgain, dbias


def back_top(l, lengths, parts, kept, dz, norms, wts):
    g, o = kept[6], kept[4]
    m, d = g.shape
    group = len(parts)

    def body(lengths, *refs):
        parts, refs = refs[:group], refs[group:]
        g, o, dz, gain, wup, wo, dg_ref, do_ref, dout_ref, sm_ref, dr_ref, dh_ref = refs

        def put(at, block):
            dh_ref[at, :] = block

        regroup(lengths_of(lengths, m // SLOTS, group), parts, put)
        dout_ref[...] = mid_terms(l, dh_ref, g, o, dz, gain, wup, wo, dg_ref, do_ref, dr_ref, sm_ref)

    outs = [((m, d), F32), ((m, d), BF), ((SHARDS // 2, 2, d // SHARDS, d), BF), ((8, d), F32)]
    return call(body, "back_top", [lengths, *parts, g, o, dz, norms[2], wts[4], wts[3]], outs, [((m, d), BF), ((m, d), F32)], 12,
                2 * m * 6 * d * d, 9 << 20)


def back_between(l, halving, lengths, dg, do, dout, kept, under, norms, wts, pieces):
    a, q, k, v, o, lse, g, c, u, gp, h = kept
    c, u, gp = under[7:10]
    m, d = dg.shape
    ff = u.shape[1]
    units, group = pieces[0].shape[0], len(pieces)

    def body(lengths, dg, do, dout, lse, q, k, v, a, h, gain, wq, wk, wv, c, u, gp, wdown,
             keep, send, keep0, send0, dh_ref, dz_ref, sm_ref, sm0_ref, dq_ref, dk_ref, dv_ref, dm_ref):
        core, lens = parity(halving), lengths_of(lengths, units, group)

        def put(rows, dh):
            dh_ref[rows, :] = dh
            dm_ref[rows, :] = dh.astype(BF)

        terms, dgain, dbias = attn_terms(l, lens, dg, do, lse, q, k, v, a, h, gain, wq, wk, wv, dq_ref, dk_ref, dv_ref, put)
        for n, term in enumerate([dout[...], *terms]):
            for z in range(SHARDS // 2):
                at, rows = 2 * (z % 2) + z // 2, slice(64 * n, 64 * n + 64)
                keep[at, rows, :] = jnp.where(core == 0, term[z, 0], term[z, 1])
                send[at, rows, :] = jnp.where(core == 0, term[z, 1], term[z, 0])
        sm_ref[...] = jnp.zeros_like(sm_ref)
        sm_ref[0:1, :] = dgain
        sm_ref[1:2, :] = dbias
        ffn_terms(core, dm_ref, u, gp, c, wdown.at[l - 1], keep0, send0, dz_ref, sm0_ref)

    outs = [((SHARDS // 2, 256, d), BF)] * 2 + [chunk_shape(128)] * 2 + [((m, d), F32), ((m, ff), BF), ((8, d), F32), ((8, d), F32)]
    keep, send, keep0, send0, *rest = call(
        body, "back_between", [lengths, dg, do, dout, lse, q, k, v, a, h, norms[0], *wts[:3], c, u, gp, wts[5]], outs,
        [((m, d), BF)] * 4, 14, 2 * m * 22 * d * d, 20 << 20)
    return (keep, send), (keep0, send0), rest


def back_bottom(halving, lengths, dh, dz, smalls, kept, norms, wts, pieces):
    a, q, k, v, o, lse, g, c, u, gp, h = kept
    m, d = dh.shape
    units, group = pieces[0].shape[0], len(pieces)

    def body(lengths, dh, g, o, dz, fgain, wup, wo, lse, q, k, v, a, h, gain, wq, wk, wv, attn1, mid1, ffn0, ffn1, keep, send, *refs):
        outs, refs = refs[:group], refs[group:]
        dg_ref, do_ref, dr_ref, mid0, dq_ref, dk_ref, dv_ref, dx_ref = refs
        core, lens = parity(halving), lengths_of(lengths, units, group)
        first = mid_terms(0, dh, g, o, dz, fgain, wup, wo, dg_ref, do_ref, dr_ref, mid0)

        def put(rows, value):
            dx_ref[rows, :] = value

        terms, dgain, dbias = attn_terms(0, lens, dg_ref, do_ref, lse, q, k, v, a, h, gain, wq, wk, wv, dq_ref, dk_ref, dv_ref, put)
        for n, term in enumerate([first, *terms]):
            for z in range(SHARDS // 2):
                store(core, keep, send, n, z, slice(0, 64), slice(None), term[z, 0], term[z, 1])
        lines = [dgain, attn1[0:1, :], dbias, attn1[1:2, :], mid0[0:1, :], mid1[0:1, :], mid0[1:2, :], mid1[1:2, :],
                 ffn0[0:1, :], ffn1[0:1, :]]
        zero = jnp.zeros((1, d), F32)
        block = jnp.concatenate(lines + [zero] * 6, axis=0).astype(BF)
        other = jnp.concatenate([ffn0[1:5, :], ffn1[1:5, :]] + [zero] * 8, axis=0).astype(BF)
        for half in (keep, send):
            for at in range(SHARDS // 2):
                half[0, at, 64:80, :] = block
                half[1, at, 64:80, :] = other
                for t in (2, 3):
                    half[t, at, 64:80, :] = jnp.zeros((16, d), BF)
        deal(dx_ref, outs)

    outs = [chunk_shape(80)] * 2 + [(pieces[0].shape, BF)] * group
    wide, narrow = ((m, d), F32), ((m, d), BF)
    keep, send, *parts = call(
        body, "back_bottom",
        [lengths, dh, g, o, dz, norms[2], wts[4], wts[3], lse, q, k, v, a, h, norms[0], *wts[:3], *smalls], outs,
        [wide, narrow, narrow, ((8, d), F32), narrow, narrow, narrow, wide], 16, 2 * m * 16 * d * d, 20 << 20)
    return (keep, send), parts


def quarters():
    first, second = bit_of(PLANE_1), bit_of(PLANE_2)
    own = 2 * first + second
    return [own, own ^ 1, own ^ 2, own ^ 3]


def finish_wide(wide0, wide1, d, ff):
    def body(*refs):
        down, up = refs[4:]
        for l in range(2):
            for n in range(4):
                at = quarters()[n]
                part = refs[2 * l + n // 2][n % 2].astype(F32)
                down[l, :, pl.ds(pl.multiple_of(at * 128, 128), 128)] = part[:, 0:256].T
                for t in range(2):
                    up[l, :, pl.ds(pl.multiple_of(at * 512 + 256 * t, 256), 256)] = part[64 * t : 64 * t + 64, 256:512]

    return call(body, "finish_wide", [*wide0, *wide1], [((2, 256, d), F32), ((2, 64, ff), F32)], [], 8, 0, 6 << 20)


def finish_last(narrow, square, d):
    def body(near, far, other, *refs):
        outs = refs[:4]
        ag, ab, fg, fb, bd, bu, vsq, vsm = refs[4:]
        for n, ref in enumerate((near.at[0], near.at[1], far.at[0], far.at[1])):
            at = quarters()[n]
            vsq[at] = ref[0:64, :].astype(F32)
            vsm[at] = ref[64:80, :].astype(F32)
        for n in range(4):
            outs[n][0] = vsq[n]
            outs[n][1] = other[64 * n : 64 * n + 64, :].astype(F32)
        s = lax.axis_index("seq")
        pair = vsm[0, :, pl.ds(pl.multiple_of((s // 2) * 128, 128), 128)]
        mine = jnp.where(s % 2 == 0, pair[:, 0:64], pair[:, 64:128])
        for n, ref in enumerate((ag, ab, fg, fb, bd)):
            ref[...] = mine[2 * n : 2 * n + 2, :]
        for l in range(2):
            bu[l : l + 1, :] = vsm[1, pl.ds(4 * l + s // 2, 1), pl.ds(pl.multiple_of((s % 2) * 256, 256), 256)]

    outs = [((2, 64, d), F32)] * 4 + [((2, 64), F32)] * 5 + [((2, 256), F32)]
    return call(body, "finish_last", [*narrow, square], outs, [((4, 64, d), F32), ((4, 16, d), F32)], 8, 0, 2 << 20)


def swap(clock, sends):
    size = lax.axis_size("seq")
    out = [None] * len(sends)
    for d, s in enumerate(sends):
        clock.send(s, [(i, i ^ (d + 1)) for i in range(size)], "seq", lambda value, d=d: out.__setitem__(d, value))
    return out


BOTH = ("dp", "seq")


def pairs_of(flip):
    out = []
    for y in range(2):
        for x in range(2):
            for z in range(4):
                for c in range(2):
                    y2, x2, z2, c2 = flip(y, x, z, c)
                    out.append((y * 16 + x * 8 + z * 2 + c, y2 * 16 + x2 * 8 + z2 * 2 + c2))
    return out


CORE = pairs_of(lambda y, x, z, c: (y, x, z, 1 - c))
PLANE_1 = pairs_of(lambda y, x, z, c: (y, 1 - x, z, c) if c == 0 else (1 - y, x, z, c))
PLANE_2 = pairs_of(lambda y, x, z, c: (y, 1 - x, z, c) if c == 1 else (1 - y, x, z, c))
LINE_1 = pairs_of(lambda y, x, z, c: (y, x, z ^ 1, c))
LINE_2 = pairs_of(lambda y, x, z, c: (y, x, z ^ 2, c))


def join_blocks(first, second):
    count = len(first)

    def body(*refs):
        for n, out in enumerate(refs[2 * count :]):
            out[0] = refs[n][...]
            out[1] = refs[count + n][...]

    return call(body, "join_blocks", [*first, *second], [((2,) + x.shape, BF) for x in first], [], 4, 0, 2 << 20)


def bit_of(pairs):
    dp, seq = lax.axis_index("dp"), lax.axis_index("seq")
    if pairs is LINE_1:
        return (seq // 2) % 2
    if pairs is LINE_2:
        return seq // 4
    y, x = dp // 2, dp % 2
    return jnp.where((seq % 2 == 0) == (pairs is PLANE_1), x, y)


def halve(kept, moved, pairs, weight):
    half = kept.shape[0] // 2
    shape = ((half,) + kept.shape[1:], BF)

    def body(a, b, sent, left):
        bit = bit_of(pairs)
        for out, side in ((sent, 1 - bit), (left, bit)):
            for i in range(half):
                at = side * half + i
                out[i] = (a[at].astype(F32) + b[at].astype(F32)).astype(BF)

    return call(body, "halve", [kept, moved], [shape] * 2, [], 4, weight, kept.size * 6)


def total(kept, moved):
    shape = kept.shape[-2:]

    def body(a, b, out):
        out[...] = (a[...].astype(F32) + b[...].astype(F32)).astype(BF).reshape(shape)

    return call(body, "total", [kept, moved], [(shape, BF)], [], 4, 0, kept.size * 6)[0]


def pair_up(near, far):
    def body(a, b, out):
        out[0] = a[...]
        out[1] = b[...]

    return call(body, "pair_up", [near, far], [((2,) + near.shape, BF)], [], 4, 0, near.size * 8)[0]


class Clock:
    def __init__(self):
        self.last, self.waiting = None, []

    def done(self, value):
        self.last = value

    def send(self, value, pairs, axes, arrived):
        self.waiting.append((value, pairs, axes, arrived))

    def after(self, value):
        waiting, self.waiting = self.waiting, []
        value, last, sent = lax.optimization_barrier((value, self.last, [w[0] for w in waiting]))
        for v, (_, pairs, axes, arrived) in zip(sent, waiting):
            arrived(lax.ppermute(v, axes, pairs))
        return value


class Reduction:
    def __init__(self, clock, halves, split, whole=()):
        self.clock, self.split, self.whole = clock, list(split), list(whole)
        self.gather = [] if whole else [PLANE_2, PLANE_1]
        self.kept = halves[0].reshape((-1,) + halves[0].shape[-2:])
        self.near = self.moved = None
        clock.send(halves[1].reshape(self.kept.shape), CORE, BOTH, self.arrived)

    def arrived(self, value):
        self.moved = value

    def step(self, weight=0):
        kept = self.clock.after(self.kept)
        if self.split:
            pairs = self.split.pop(0)
            sent, self.kept = halve(kept, self.moved, pairs, weight)
        elif self.whole:
            pairs = self.whole.pop(0)
            sent = self.kept = total(kept, self.moved)
        elif len(self.gather) == 2:
            pairs = self.gather.pop(0)
            sent = self.kept = total(kept, self.moved)
        elif self.gather:
            pairs = self.gather.pop(0)
            sent = self.kept = self.near = pair_up(kept, self.moved)
        else:
            self.kept = total(kept, self.moved)
            self.clock.done(self.kept)
            return
        self.clock.done(sent)
        self.clock.send(sent, pairs, BOTH, self.arrived)


def scattered(term):
    share = lax.psum_scatter(term.astype(F32), "seq", scatter_dimension=1, tiled=True)
    return lax.psum(share.astype(BF), "dp").astype(F32)


def joined(halves, z_first=False):
    width = halves[0].shape[-1]
    if z_first:
        shards = jnp.stack([half.reshape(2, 2, 4, -1, width) for half in halves]).transpose(2, 1, 0, 3, 4, 5)
    else:
        shards = jnp.stack([half.reshape(4, 2, 2, -1, width) for half in halves]).transpose(3, 2, 0, 1, 4, 5)
    return shards.reshape((SHARDS,) + shards.shape[3:])


def plain_sums(wide0, wide1, part, narrow, d, ff):
    part, narrow = joined(part, True), joined(narrow)
    down, up, square = [], [], []
    for wide, terms in ((wide0, narrow[:, :, :64]), (wide1, part)):
        wide = joined(wide).reshape(SHARDS, 512, 512)
        down.append(wide[:, :, :256].transpose(0, 2, 1).reshape(ff, d))
        up.append(wide[:, :, 256:].reshape(SHARDS, ff // 256, d // SHARDS, 256).transpose(0, 2, 1, 3).reshape(d, ff))
        square.append(terms.transpose(1, 0, 2, 3).reshape(4, d, d))
    square = jnp.stack(square, axis=1)
    small = narrow[0, 0, 64:74].reshape(5, 2, d)
    bias = narrow[0, 1, 64:72].reshape(2, ff)
    terms = (small[0], small[1], square[1], square[2], square[3], square[0], small[2], small[3], jnp.stack(up), bias,
             jnp.stack(down), small[4])
    return tuple(scattered(term) for term in terms)


def on_device(
    inputs, cotangent, item_lengths, attn_gain, attn_bias, query_weight, key_weight, value_weight, output_weight,
    ffn_gain, ffn_bias, up_weight, up_bias, down_weight, down_bias,
):
    rows, width, depth = inputs.shape
    ff = up_weight.shape[2]
    group = SLOTS // width
    halving = lax.axis_size("dp") == 4 and lax.axis_size("seq") == SHARDS
    lengths = item_lengths.T
    clock = Clock()
    packed = pack(inputs, group)
    clock.done(packed[0])
    x_parts = swap(clock, packed[1:])
    cotangent = clock.after(cotangent)
    first = pack(cotangent, group)
    clock.done(first[0])
    cot_parts = swap(clock, first[1:])
    clock.done(clock.after(first[0]))
    norms = (attn_gain, attn_bias, ffn_gain, ffn_bias, up_bias, down_bias)
    wts = (query_weight, key_weight, value_weight, output_weight, up_weight, down_weight)
    x_parts, cot_parts = [packed[0]] + x_parts, [first[0]] + cot_parts
    kept0, h1 = forward_first(lengths, x_parts, norms, wts)
    kept1, pieces, wide1, dz1, ffn1 = forward_last(1, halving, lengths, h1, cot_parts, norms, wts)
    clock.done(ffn1)
    sums = []

    def reduced(*args):
        sums.append(Reduction(clock, *args) if halving else None)

    def step(*names, weight=0):
        for n in names if halving else ():
            sums[n].step(weight)

    reduced(wide1, (PLANE_1, PLANE_2, LINE_1, LINE_2))
    dg, do, dout, mid1 = back_top(1, lengths, cot_parts, kept1, clock.after(dz1), norms, wts)
    clock.done(mid1)
    step(0)
    part, wide0, (dh, dz0, attn1, ffn0) = back_between(
        1, halving, lengths, clock.after(dg), do, dout, kept1, kept0, norms, wts, pieces)
    clock.done(attn1)
    reduced(part, (LINE_1, LINE_2), (PLANE_1, PLANE_2))
    reduced(wide0, (PLANE_1, PLANE_2, LINE_1, LINE_2))
    step(0, weight=LONG)
    step(2, 1)
    narrow, parts = back_bottom(
        halving, lengths, clock.after(dh), dz0, (attn1, mid1, ffn0, ffn1), kept0, norms, wts, pieces)
    clock.done(parts[0])
    reduced(narrow, (PLANE_1, PLANE_2, LINE_1, LINE_2))
    both = join_blocks(pieces, clock.after(parts))
    clock.done(both[0])
    mine = swap(clock, both[1:])
    step(0, 2)
    step(1, weight=LONG)
    step(3)
    clock.done(clock.after(clock.last))
    output, input_grad = unpack([both[0]] + mine)
    if not halving:
        return (output, input_grad) + plain_sums(wide0, wide1, part, narrow, depth, ff)

    clock.done(output)
    step(3, 1, 2, 0, 3, 1, 2, 0, 1, 3, 0, 2, 3, 2, 3)
    clock.after(clock.last)
    down, up = finish_wide((sums[2].near, sums[2].moved), (sums[0].near, sums[0].moved), depth, ff)
    do, dq, dk, dv, ag, ab, fg, fb, bd, bu = finish_last((sums[3].near, sums[3].moved), sums[1].kept, depth)
    return output, input_grad, ag, ab, dq, dk, dv, do, fg, fb, up, bu, down, bd


def solution(mesh):
    spec = jax.sharding.PartitionSpec
    whole, split = spec(), spec("dp", "seq", None)
    vec, mat = spec(None, "seq"), spec(None, "seq", None)
    return jax.shard_map(
        on_device,
        mesh=mesh,
        in_specs=(split, split, spec("dp", None)) + (whole,) * 12,
        out_specs=(split, split, vec, vec, mat, mat, mat, mat, vec, vec, mat, vec, mat, vec),
        check_vma=False,
    )
```

```python
import jax
import jax.numpy as jnp
from jax import lax
from jax.experimental import pallas as pl
from jax.experimental.pallas import tpu as pltpu

H = 8
SLOTS = 256
EPS = 1e-05
NEG = -1000000000.0
BF = jnp.bfloat16
F32 = jnp.float32
GELU_C = 0.7978845608028654
GELU_A = 0.044715
STEP = 512
SHARDS = 8
LONG = 30_000_000_000
SECOND = slice(128, 192)

NN = (((1,), (0,)), ((), ()))
NT = (((1,), (1,)), ((), ()))
TN = (((0,), (0,)), ((), ()))

SDS = jax.ShapeDtypeStruct
IN_VMEM = pl.BlockSpec(memory_space=pltpu.VMEM)
IN_SMEM = pl.BlockSpec(memory_space=pltpu.SMEM)


def dot(left, right, form=NN):
    return lax.dot_general(left, right, form, preferred_element_type=F32)


def normalize(values):
    centered = values - jnp.mean(values, axis=-1, keepdims=True)
    inv = lax.rsqrt(jnp.mean(centered * centered, axis=-1, keepdims=True) + EPS)
    return centered * inv, inv


def norm_back(dy, values, gain):
    xhat, inv = normalize(values)
    dgain = jnp.sum(dy * xhat, axis=0, keepdims=True)
    dbias = jnp.sum(dy, axis=0, keepdims=True)
    dx = dy * gain
    dx = inv * (dx - jnp.mean(dx, axis=-1, keepdims=True) - xhat * jnp.mean(dx * xhat, axis=-1, keepdims=True))
    return dx, dgain, dbias


def head_masks(width):
    lane = lax.broadcasted_iota(jnp.int32, (1, 2 * width), 1)
    low = (lane < width).astype(F32).astype(BF)
    return low, (1.0 - low.astype(F32)).astype(BF)


def tiles(m):
    return [slice(SLOTS * i, SLOTS * (i + 1)) for i in range(m // SLOTS)]


def call(body, name, operands, outs, scratch, limit, flops, moved):
    return pl.pallas_call(
        body,
        in_specs=[IN_SMEM if x.dtype == jnp.int32 else IN_VMEM for x in operands],
        out_specs=[IN_VMEM] * len(outs),
        out_shape=[SDS(*out) for out in outs],
        scratch_shapes=[pltpu.VMEM(*x) for x in scratch],
        compiler_params=pltpu.CompilerParams(vmem_limit_bytes=limit << 20),
        cost_estimate=pl.CostEstimate(flops=flops, bytes_accessed=moved, transcendentals=0),
        name=name,
    )(*operands)


def member_of(group):
    return lax.axis_index("seq") % group


def lengths_of(lengths, units, group):
    seq = lax.axis_index("seq")
    return [lengths[seq // group, (seq % group) * units + u] for u in range(units)]


def pack(local, group):
    rows, width, depth = local.shape
    n = rows // group

    def body(x_ref, *outs):
        for d, out in enumerate(outs):
            out[...] = x_ref[pl.ds((member_of(group) ^ d) * n, n)]

    return call(body, "pack", [local], [((n, width, depth), local.dtype)] * group, [], 4, 20_000_000_000, 1 << 20)


def unpack(pieces):
    _, n, width, depth = pieces[0].shape

    def body(*refs):
        outs = refs[-2:]
        for d, ref in enumerate(refs[:-2]):
            for t in range(2):
                outs[t][pl.ds((member_of(len(pieces)) ^ d) * n, n)] = ref[t]

    return call(body, "unpack", pieces, [((n * len(pieces), width, depth), BF)] * 2, [], 4, 0, 1 << 20)


def regroup(lens, pieces, put):
    n, width, _ = pieces[0].shape
    j = member_of(len(pieces))
    for d, piece in enumerate(pieces):
        for u in range(n):
            start = (j ^ d) * width
            at = pl.ds(pl.multiple_of(u * SLOTS + start, width), width)
            block = piece[u]
            if lens is not None:
                slot = lax.broadcasted_iota(jnp.int32, (width, 1), 0) + start
                block = jnp.where(slot < lens[u], block.astype(F32), 0.0)
            put(at, block)


def deal(values, pieces):
    for d, piece in enumerate(pieces):
        n, width, _ = piece.shape
        for u in range(n):
            at = pl.ds(pl.multiple_of(u * SLOTS + (member_of(len(pieces)) ^ d) * width, width), width)
            piece[u] = values[at, :].astype(BF)


def stacked(head):
    return slice(SLOTS * (head % 2), SLOTS * (head % 2) + SLOTS)


def apart(pair, masks):
    return jnp.concatenate([pair * masks[0], pair * masks[1]], axis=0)


def pair_scratch(m):
    return ((m // SLOTS * (H // 2), 2 * SLOTS, SLOTS), BF)


def forward_attention(lens, h, gain, bias, wq, wk, wv, a_ref, q_ref, k_ref, v_ref, o_ref, lse_ref, p_ref):
    masks = head_masks(64)
    for i, rows in enumerate(tiles(h.shape[0])):
        xhat, _ = normalize(h[rows, :].astype(F32))
        a = (xhat * gain + bias).astype(BF)
        a_ref[rows, :] = a
        q_ref[rows, :] = (dot(a, wq[...]).astype(BF).astype(F32) * 0.125).astype(BF)
        k_ref[rows, :] = dot(a, wk[...]).astype(BF)
        v_ref[rows, :] = dot(a, wv[...]).astype(BF)
    key = lax.broadcasted_iota(jnp.int32, (SLOTS, 1), 0)
    for i, rows in enumerate(tiles(h.shape[0])):
        valid = key < lens[i]
        for head in range(H):
            cols = slice(128 * (head // 2), 128 * (head // 2) + 128)
            st = jnp.where(valid, dot(k_ref[rows, cols] * masks[head % 2], q_ref[rows, cols], NT), NEG)
            top = jnp.max(st, axis=0, keepdims=True)
            e = jnp.exp(st - top)
            tot = jnp.sum(e, axis=0, keepdims=True)
            p_ref[i * (H // 2) + head // 2, stacked(head), :] = (e * (1.0 / tot)).astype(BF)
            lse_ref[i * H + head, :] = (top + jnp.log(tot))[0]
    for i, rows in enumerate(tiles(h.shape[0])):
        for pair in range(H // 2):
            cols = slice(128 * pair, 128 * pair + 128)
            o_ref[rows, cols] = dot(p_ref[i * (H // 2) + pair], apart(v_ref[rows, cols], masks), TN).astype(BF)


def forward_ffn(h, o, wo, gain, bias, wup, bup, wdown, bdown, g_ref, c_ref, u_ref, gp_ref, n_ref):
    m, ff = h.shape[0], wup.shape[1]
    for rows in tiles(m):
        g = h[rows, :].astype(F32) + dot(o[rows, :], wo[...])
        g_ref[rows, :] = g
        xhat, _ = normalize(g)
        c_ref[rows, :] = (xhat * gain + bias).astype(BF)
    for f in range(0, ff, 256):
        fs = slice(f, f + 256)
        for rows in tiles(m):
            z = dot(c_ref[rows, :], wup[:, fs]) + bup[:, fs]
            z2 = z * z
            t = jnp.tanh(z * (GELU_C + GELU_C * GELU_A * z2))
            half = 0.5 + 0.5 * t
            gp = half + (0.5 * z) * (1.0 - t * t) * (GELU_C + 3.0 * GELU_C * GELU_A * z2)
            u_ref[rows, fs] = (z * half).astype(BF)
            gp_ref[rows, fs] = gp.astype(BF)
    if n_ref is not None:
        layer_output(g_ref, u_ref, wdown, bdown, n_ref)


def layer_output(g_ref, u_ref, wdown, bdown, n_ref):
    for rows in tiles(g_ref.shape[0]):
        n_ref[rows, :] = g_ref[rows, :] + (dot(u_ref[rows, :], wdown[...]) + bdown)


def store(core, keep, send, quarter, z, rows, cols, even, odd):
    mine, other = jnp.where(core == 0, even, odd), jnp.where(core == 0, odd, even)
    at = 2 * (z % 2) + z // 2
    keep[quarter, at, rows, cols] = mine
    send[quarter, at, rows, cols] = other


def ffn_terms(core, dm_ref, u_ref, gp_ref, c_ref, wdown, keep, send, dz_ref, sm_ref):
    ff = u_ref.shape[1]
    dm = dm_ref[...]
    for f in range(ff // STEP):
        res = dot(dm, u_ref[:, STEP * f : STEP * f + STEP], TN).astype(BF).reshape(4, 128, STEP)
        store(core, keep, send, slice(None), f, slice(0, 128), slice(0, 256), res[:, :, 0:256], res[:, :, 256:512])
    sm_ref[...] = jnp.zeros_like(sm_ref)
    sm_ref[0:1, :] = jnp.sum(dm.astype(F32), axis=0, keepdims=True)
    for f in range(ff // STEP):
        fs = slice(STEP * f, STEP * f + STEP)
        dz = (dot(dm, wdown[fs, :], NT) * gp_ref[:, fs].astype(F32)).astype(BF)
        dz_ref[:, fs] = dz
        sm_ref[1 + f : 2 + f, :] = jnp.sum(dz.astype(F32), axis=0, keepdims=True)
        res = dot(c_ref[...], dz, TN).astype(BF).reshape(4, 128, STEP)
        for t in range(2):
            rows, part = slice(64 * t, 64 * t + 64), res[:, :, 256 * t : 256 * t + 256]
            for z in range(4):
                store(core, keep, send, f, z, rows, slice(256, 512), part[z, 0:64], part[z, 64:128])


KEPT = ("a", "q", "k", "v", "o", "lse", "g", "c", "u", "gp")


def kept_shapes(m, d, ff):
    wide, narrow = (m, ff), (m, d)
    return [(narrow, BF)] * 5 + [((m // SLOTS * H, SLOTS), F32), (narrow, F32), (narrow, BF), (wide, BF), (wide, BF)]


def row(ref, l):
    return ref[l : l + 1, :].astype(F32)


def forward_layer(l, lens, h, norms, wts, kept, last, p_ref):
    ag, ab, fg, fb, bup, bdown = norms
    wq, wk, wv, wo, wup, wdown = [w.at[l] for w in wts]
    a, q, k, v, o, lse, g, c, u, gp = kept
    forward_attention(lens, h, row(ag, l), row(ab, l), wq, wk, wv, a, q, k, v, o, lse, p_ref)
    forward_ffn(h, o, wo, row(fg, l), row(fb, l), wup, row(bup, l), wdown, row(bdown, l), g, c, u, gp, last)


def chunk_shape(rows):
    return ((4, SHARDS // 2, rows, 512), BF)


def parity(halving):
    return lax.axis_index("seq") % 2 if halving else 0


def forward_first(lengths, parts, norms, wts):
    _, d, ff = wts[4].shape
    n, width, _ = parts[0].shape
    group = len(parts)
    m = n * group * width

    def body(*refs):
        lengths, refs = refs[0], refs[1:]
        parts, refs = refs[:group], refs[group:]
        norms, wts, kept, (x_ref, last, p_ref) = refs[:6], refs[6:12], refs[12:22], refs[22:]

        def put(at, block):
            x_ref[at, :] = block

        regroup(None, parts, put)
        forward_layer(0, lengths_of(lengths, n, group), x_ref, norms, wts, kept, last, p_ref)

    outs = kept_shapes(m, d, ff) + [((m, d), BF), ((m, d), F32)]
    res = call(body, "forward_first", [lengths, *parts, *norms, *wts], outs, [pair_scratch(m)], 4, 2 * m * (4 * d * d + 2 * d * ff), 24 << 20)
    return res[:11], res[11]


def forward_last(l, halving, lengths, h, parts, norms, wts):
    _, d, ff = wts[4].shape
    n, width, _ = parts[0].shape
    group = len(parts)
    m = n * group * width
    per = kept_shapes(m, d, ff)

    def body(*refs):
        lengths, h = refs[:2]
        refs = refs[2:]
        parts, refs = refs[:group], refs[group:]
        norms, wts, refs = refs[:6], refs[6:12], refs[12:]
        kept, refs = refs[:8], refs[8:]
        keep, send, dz_ref, sm_ref, c, gp, dm_ref, p_ref = refs
        lens = lengths_of(lengths, n, group)

        def put(at, block):
            dm_ref[at, :] = block.astype(BF)

        regroup(lens, parts, put)
        forward_layer(l, lens, h, norms, wts, [*kept[:7], c, kept[7], gp], None, p_ref)
        ffn_terms(parity(halving), dm_ref, kept[7], gp, c, wts[5].at[l], keep, send, dz_ref, sm_ref)

    outs = per[:7] + [per[8]] + [chunk_shape(128)] * 2 + [((m, ff), BF), ((8, d), F32)]
    *kept, keep, send, dz, sums = call(
        body, "forward_last", [lengths, h, *parts, *norms, *wts], outs,
        [per[7], per[9], ((m, d), BF), pair_scratch(m)], 20, 2 * m * (4 * d * d + 4 * d * ff), 24 << 20)
    return kept[:7] + [None, kept[7], None, h], (keep, send), dz, sums


def mid_terms(l, dh_ref, g, o, dz, gain, wup, wo, dg_ref, do_ref, dr_ref, sm_ref):
    m, d = g.shape
    dgain = dbias = None
    for i, rows in enumerate(tiles(m)):
        dc = dot(dz[rows, :], wup[l], NT)
        dx, dg1, db1 = norm_back(dc, g[rows, :], row(gain, l))
        dg = dh_ref[rows, :] + dx
        dg_ref[rows, :] = dg
        dr_ref[rows, :] = dg.astype(BF)
        dgain, dbias = (dg1, db1) if i == 0 else (dgain + dg1, dbias + db1)
    sm_ref[...] = jnp.zeros_like(sm_ref)
    sm_ref[0:1, :] = dgain
    sm_ref[1:2, :] = dbias
    do_ref[...] = dot(dr_ref[...], wo[l], NT).astype(BF)
    return dot(o[...], dr_ref[...], TN).astype(BF).reshape(SHARDS // 2, 2, d // SHARDS, d)


def attn_terms(l, lens, dg, do, lse, q, k, v, h, gain, wq, wk, wv, dq_ref, dk_ref, dv_ref, p_ref, s_ref, put):
    m, d = dg.shape
    masks = head_masks(64)
    low = lax.broadcasted_iota(jnp.int32, (1, 128), 1) < 64
    key = lax.broadcasted_iota(jnp.int32, (SLOTS, 1), 0)
    for i, rows in enumerate(tiles(m)):
        valid = key < lens[i]
        for head in range(H):
            cols, n, mk = slice(128 * (head // 2), 128 * (head // 2) + 128), i * (H // 2) + head // 2, masks[head % 2]
            st = jnp.where(valid, dot(k[rows, cols] * mk, q[rows, cols], NT), NEG)
            pt = jnp.exp(st - lse[i * H + head, :][None, :])
            dpt = dot(v[rows, cols] * mk, do[rows, cols], NT)
            delta = jnp.sum(pt * dpt, axis=0, keepdims=True)
            p_ref[n, stacked(head), :] = pt.astype(BF)
            s_ref[n, stacked(head), :] = (pt * (dpt - delta)).astype(BF)
    for i, rows in enumerate(tiles(m)):
        for pair in range(H // 2):
            cols, n = slice(128 * pair, 128 * pair + 128), i * (H // 2) + pair
            dq_ref[rows, cols] = (dot(s_ref[n], apart(k[rows, cols], masks), TN) * 0.125).astype(BF)
            both = dot(s_ref[n], q[rows, cols])
            dk_ref[rows, cols] = jnp.where(low, both[0:SLOTS], both[SLOTS:]).astype(BF)
            both = dot(p_ref[n], do[rows, cols])
            dv_ref[rows, cols] = jnp.where(low, both[0:SLOTS], both[SLOTS:]).astype(BF)
    dgain = dbias = None
    for i, rows in enumerate(tiles(m)):
        da = dot(dq_ref[rows, :], wq[l], NT) + dot(dk_ref[rows, :], wk[l], NT) + dot(dv_ref[rows, :], wv[l], NT)
        dx, dg1, db1 = norm_back(da, h[rows, :].astype(F32), row(gain, l))
        put(rows, dg[rows, :] + dx)
        dgain, dbias = (dg1, db1) if i == 0 else (dgain + dg1, dbias + db1)
    return dgain, dbias


def square_terms(a, *grads):
    d = a.shape[1]
    return [dot(a[...], ref[...], TN).astype(BF).reshape(SHARDS // 2, 2, d // SHARDS, d) for ref in grads]


def back_top(l, lengths, parts, kept, dz, norms, wts):
    g, o = kept[6], kept[4]
    m, d = g.shape
    group = len(parts)

    def body(lengths, *refs):
        parts, refs = refs[:group], refs[group:]
        g, o, dz, gain, wup, wo, dg_ref, do_ref, dout_ref, sm_ref, dr_ref, dh_ref = refs

        def put(at, block):
            dh_ref[at, :] = block

        regroup(lengths_of(lengths, m // SLOTS, group), parts, put)
        dout_ref[...] = mid_terms(l, dh_ref, g, o, dz, gain, wup, wo, dg_ref, do_ref, dr_ref, sm_ref)

    outs = [((m, d), F32), ((m, d), BF), ((SHARDS // 2, 2, d // SHARDS, d), BF), ((8, d), F32)]
    return call(body, "back_top", [lengths, *parts, g, o, dz, norms[2], wts[4], wts[3]], outs, [((m, d), BF), ((m, d), F32)], 6,
                2 * m * 6 * d * d, 9 << 20)


def back_between(l, halving, lengths, dg, do, kept, under, norms, wts, units, group):
    a, q, k, v, o, lse, g, c, u, gp, h = kept
    c, u, gp = under[7:10]
    m, d = dg.shape
    ff = u.shape[1]

    def body(lengths, dg, do, lse, q, k, v, h, gain, wq, wk, wv, c, u, gp, wdown,
             keep0, send0, dh_ref, dz_ref, dq_ref, dk_ref, dv_ref, sm_ref, sm0_ref, dm_ref, p_ref, s_ref):
        core, lens = parity(halving), lengths_of(lengths, units, group)

        def put(rows, dh):
            dh_ref[rows, :] = dh
            dm_ref[rows, :] = dh.astype(BF)

        dgain, dbias = attn_terms(l, lens, dg, do, lse, q, k, v, h, gain, wq, wk, wv, dq_ref, dk_ref, dv_ref, p_ref, s_ref, put)
        sm_ref[...] = jnp.zeros_like(sm_ref)
        sm_ref[0:1, :] = dgain
        sm_ref[1:2, :] = dbias
        ffn_terms(core, dm_ref, u, gp, c, wdown.at[l - 1], keep0, send0, dz_ref, sm0_ref)

    outs = [chunk_shape(128)] * 2 + [((m, d), F32), ((m, ff), BF)] + [((m, d), BF)] * 3 + [((8, d), F32)] * 2
    keep0, send0, *rest = call(
        body, "back_between", [lengths, dg, do, lse, q, k, v, h, norms[0], *wts[:3], c, u, gp, wts[5]], outs,
        [((m, d), BF), pair_scratch(m), pair_scratch(m)], 9, 2 * m * 19 * d * d, 20 << 20)
    return (keep0, send0), rest


def square_halves(halving, a, grads, dout):
    d = a.shape[1]

    def body(a, dq, dk, dv, dout, keep, send):
        core = parity(halving)
        for n, term in enumerate([dout[...], *square_terms(a, dq, dk, dv)]):
            for z in range(SHARDS // 2):
                at, rows = 2 * (z % 2) + z // 2, slice(64 * n, 64 * n + 64)
                keep[at, rows, :] = jnp.where(core == 0, term[z, 0], term[z, 1])
                send[at, rows, :] = jnp.where(core == 0, term[z, 1], term[z, 0])

    outs = [((SHARDS // 2, 256, d), BF)] * 2
    return call(body, "square_halves", [a, *grads, dout], outs, [], 4, 2 * a.shape[0] * 3 * d * d, 4 << 20)


def back_bottom(halving, lengths, dh, dz, smalls, kept, norms, wts, width, group):
    a, q, k, v, o, lse, g, c, u, gp, h = kept
    m, d = dh.shape
    units = m // SLOTS

    def body(lengths, dh, g, o, dz, fgain, wup, wo, lse, q, k, v, a, h, gain, wq, wk, wv, attn1, mid1, ffn0, ffn1, keep, send, *refs):
        outs, refs = refs[:group], refs[group:]
        dg, do, dr, mid0, dq_ref, dk_ref, dv_ref, dx_ref, p_ref, s_ref = refs
        core, lens = parity(halving), lengths_of(lengths, units, group)
        first = mid_terms(0, dh, g, o, dz, fgain, wup, wo, dg, do, dr, mid0)
        for z in range(SHARDS // 2):
            store(core, keep, send, 0, z, slice(0, 64), slice(None), first[z, 0], first[z, 1])

        def put(rows, value):
            dx_ref[rows, :] = value

        dgain, dbias = attn_terms(0, lens, dg, do, lse, q, k, v, h, gain, wq, wk, wv, dq_ref, dk_ref, dv_ref, p_ref, s_ref, put)
        for n, term in enumerate(square_terms(a, dq_ref, dk_ref, dv_ref)):
            for z in range(SHARDS // 2):
                store(core, keep, send, n + 1, z, slice(0, 64), slice(None), term[z, 0], term[z, 1])
        lines = [dgain, attn1[0:1, :], dbias, attn1[1:2, :], mid0[0:1, :], mid1[0:1, :], mid0[1:2, :], mid1[1:2, :],
                 ffn0[0:1, :], ffn1[0:1, :]]
        zero = jnp.zeros((1, d), F32)
        block = jnp.concatenate(lines + [zero] * 6, axis=0).astype(BF)
        other = jnp.concatenate([ffn0[1:5, :], ffn1[1:5, :]] + [zero] * 8, axis=0).astype(BF)
        for half in (keep, send):
            for at in range(SHARDS // 2):
                half[0, at, 64:80, :] = block
                half[1, at, 64:80, :] = other
                for t in (2, 3):
                    half[t, at, 64:80, :] = jnp.zeros((16, d), BF)
        deal(dx_ref, outs)

    outs = [chunk_shape(80)] * 2 + [((units, width, d), BF)] * group
    wide, narrow = ((m, d), F32), ((m, d), BF)
    keep, send, *parts = call(
        body, "back_bottom",
        [lengths, dh, g, o, dz, norms[2], wts[4], wts[3], lse, q, k, v, a, h, norms[0], *wts[:3], *smalls], outs,
        [wide, narrow, narrow, ((8, d), F32), narrow, narrow, narrow, wide, pair_scratch(m), pair_scratch(m)], 12, 2 * m * 16 * d * d, 20 << 20)
    return (keep, send), parts


def results(l, kept, norms, wts, parts):
    g, u = kept[6], kept[8]
    group = len(parts)
    shape = (2,) + parts[0].shape

    def body(g, u, wdown, bdown, *refs):
        last = refs[-1]
        layer_output(g, u, wdown.at[l], row(bdown, l), last)
        outs = refs[group : 2 * group]
        deal(last, [out.at[0] for out in outs])
        for part, out in zip(refs[:group], outs):
            out[1] = part[...]

    return call(body, "results", [g, u, wts[5], norms[5], *parts], [(shape, BF)] * group, [(g.shape, F32)], 8,
                2 * u.shape[0] * u.shape[1] * g.shape[1], 4 << 20)


def finish_wide(wide0, wide1, d, ff):
    def body(w0, w1, down, up):
        for l, ref in enumerate((w0, w1)):
            for n in range(4):
                part = ref[n].astype(F32)
                down[l, :, 128 * n : 128 * n + 128] = part[:, 0:256].T
                for t in range(2):
                    at = 512 * n + 256 * t
                    up[l, :, at : at + 256] = part[64 * t : 64 * t + 64, 256:512]

    return call(body, "finish_wide", [wide0, wide1], [((2, 256, d), F32), ((2, 64, ff), F32)], [], 8, 0, 1024)


def finish_last(own, others, square, d):
    rows = own.shape[0]
    offsets = [first for _, first in others]

    def body(own, *refs):
        parts, other = [(own, 0), *zip(refs[:3], offsets)], refs[3]
        outs = refs[4:8]
        ag, ab, fg, fb, bd, bu, x, vsm = refs[8:]
        here = 2 * bit_of(PLANE_1) + bit_of(PLANE_2)
        for (ref, first), flip in zip(parts, (0, 2, 1, 3)):
            x[here ^ flip] = ref[first : first + rows, :]
        for n in range(4):
            outs[n][0] = x[n, 0:64, :].astype(F32)
            outs[n][1] = other[64 * n : 64 * n + 64, :].astype(F32)
        s = lax.axis_index("seq")
        vsm[...] = x[0:2, 64:80, :].astype(F32)
        pair = vsm[0, :, pl.ds(pl.multiple_of((s // 2) * 128, 128), 128)]
        mine = jnp.where(s % 2 == 0, pair[:, 0:64], pair[:, 64:128])
        for n, ref in enumerate((ag, ab, fg, fb, bd)):
            ref[...] = mine[2 * n : 2 * n + 2, :]
        for l in range(2):
            bu[l : l + 1, :] = vsm[1, pl.ds(4 * l + s // 2, 1), pl.ds(pl.multiple_of((s % 2) * 256, 256), 256)]

    outs = [((2, 64, d), F32)] * 4 + [((2, 64), F32)] * 5 + [((2, 256), F32)]
    return call(body, "finish_last", [own, *[array for array, _ in others], square], outs, [((4, rows, d), BF), ((2, 16, d), F32)], 8, 0, 2 << 20)


def swap(clock, sends):
    size = lax.axis_size("seq")
    out = [None] * len(sends)
    for d, s in enumerate(sends):
        clock.send(s, [(i, i ^ (d + 1)) for i in range(size)], "seq", lambda value, d=d: out.__setitem__(d, value))
    return out


BOTH = ("dp", "seq")


def pairs_of(flip):
    out = []
    for y in range(2):
        for x in range(2):
            for z in range(4):
                for c in range(2):
                    y2, x2, z2, c2 = flip(y, x, z, c)
                    out.append((y * 16 + x * 8 + z * 2 + c, y2 * 16 + x2 * 8 + z2 * 2 + c2))
    return out


CORE = pairs_of(lambda y, x, z, c: (y, x, z, 1 - c))
PLANE_1 = pairs_of(lambda y, x, z, c: (y, 1 - x, z, c) if c == 0 else (1 - y, x, z, c))
PLANE_2 = pairs_of(lambda y, x, z, c: (y, 1 - x, z, c) if c == 1 else (1 - y, x, z, c))
PLANE_3 = pairs_of(lambda y, x, z, c: (1 - y, 1 - x, z, c))
LINE_1 = pairs_of(lambda y, x, z, c: (y, x, z ^ 1, c))
LINE_2 = pairs_of(lambda y, x, z, c: (y, x, z ^ 2, c))


def bit_of(pairs):
    dp, seq = lax.axis_index("dp"), lax.axis_index("seq")
    if pairs is LINE_1:
        return (seq // 2) % 2
    if pairs is LINE_2:
        return seq // 4
    y, x = dp // 2, dp % 2
    return jnp.where((seq % 2 == 0) == (pairs is PLANE_1), x, y)


class Clock:
    def __init__(self):
        self.last, self.waiting = None, []

    def done(self, value):
        self.last = value

    def send(self, value, pairs, axes, arrived):
        self.waiting.append((value, pairs, axes, arrived))

    def after(self, value):
        waiting, self.waiting = self.waiting, []
        value, last, sent = lax.optimization_barrier((value, self.last, [w[0] for w in waiting]))
        for v, (_, pairs, axes, arrived) in zip(sent, waiting):
            arrived(lax.ppermute(v, axes, pairs))
        return value


class Chunk:
    def __init__(self, clock, halves):
        self.kept = halves[0].reshape(-1, halves[0].shape[-1])
        self.moved, self.paired, self.all = None, False, []
        clock.send(halves[1].reshape(self.kept.shape), CORE, BOTH, lambda value: self.arrived(value, 0))

    def arrived(self, value, first):
        self.moved = (value, first)
        self.all.append(self.moved)


BLOCK = 256


def blocks(count):
    return [(start, min(BLOCK, count - start)) for start in range(0, count, BLOCK)]


def advance(clock, items, weight=0):
    for (chunk, _, _), kept in zip(items, clock.after([chunk.kept for chunk, _, _ in items])):
        chunk.kept = kept
    arrays, lanes, keeps, plan = [], {}, [], []

    def index(array):
        for n, other in enumerate(arrays):
            if other is array:
                return n
        arrays.append(array)
        return len(arrays) - 1

    for chunk, kind, pairs in items:
        rows = chunk.kept.shape[0]
        now = 2 * rows if chunk.paired else rows
        left = rows // 2 if kind == "split" else now
        lane = []
        for each in pairs if kind == "spread" else (pairs,) if kind in ("split", "whole", "gather") else ():
            key = [n for n in lanes if lanes[n][0] is each]
            name = key[0] if key else len(lanes)
            first = lanes[name][1] if key else 0
            lane.append((name, first))
            lanes[name] = (each, first + left)
        at, by, offset = index(chunk.kept), None, 0
        if chunk.moved:
            by, offset = index(chunk.moved[0]), chunk.moved[1]
        plan.append((kind, pairs, at, by, offset, rows, chunk.paired, lane))
        keeps.append(left)
    count = len(lanes)

    def body(*refs):
        ins, outs = refs[: len(arrays)], refs[len(arrays) :]
        for n, (kind, pairs, at, by, offset, rows, paired, lane) in enumerate(plan):
            kept, moved, left = ins[at], None if by is None else ins[by], outs[count + n]
            sent, start = (outs[lane[0][0]], lane[0][1]) if lane else (None, 0)

            def summed(low, size):
                if isinstance(low, int):
                    first, second = slice(low, low + size), slice(offset + low, offset + low + size)
                else:
                    first = pl.ds(pl.multiple_of(low, 16), size)
                    second = pl.ds(pl.multiple_of(offset + low, 16), size)
                if moved is None:
                    return kept[first, :]
                return (kept[first, :].astype(F32) + moved[second, :].astype(F32)).astype(BF)

            if kind == "split":
                half = rows // 2
                bit = bit_of(pairs)
                for low, size in blocks(half):
                    sent[start + low : start + low + size, :] = summed((1 - bit) * half + low, size)
                    left[low : low + size, :] = summed(bit * half + low, size)
            elif kind == "order":
                part = rows // 2
                own = 2 * bit_of(pairs[0]) + bit_of(pairs[1])
                for m, flip in enumerate((0, 2, 1, 3)):
                    source, base = (kept, 0) if m < 2 else (moved, offset)
                    base += (m % 2) * part
                    left[pl.ds(pl.multiple_of((own ^ flip) * part, 16), part), :] = source[base : base + part, :]
            elif paired:
                for low, size in blocks(rows):
                    for source, base, to in ((kept, low, low), (moved, offset + low, rows + low)):
                        value = source[base : base + size, :]
                        left[to : to + size, :] = value
                        sent[start + to : start + to + size, :] = value
            else:
                for low, size in blocks(rows):
                    value = summed(low, size)
                    left[low : low + size, :] = value
                    for name, to in lane:
                        outs[name][to + low : to + low + size, :] = value

    width = items[0][0].kept.shape[1]
    sizes = [lanes[n][1] for n in range(count)] + keeps
    results = call(body, "advance", arrays, [((rows, width), BF) for rows in sizes], [], 4, weight, 1 << 20)
    clock.done(results[0])
    for n in range(count):
        here = [(item[0], to) for item, spec in zip(items, plan) for name, to in spec[-1] if name == n]

        def arrived(value, here=here):
            for chunk, first in here:
                chunk.arrived(value, first)

        clock.send(results[n], lanes[n][0], BOTH, arrived)
    for (chunk, kind, _), kept in zip(items, results[count:]):
        chunk.kept, chunk.moved, chunk.all = kept, None, []
        chunk.paired = kind == "gather"


def scattered(term):
    share = lax.psum_scatter(term.astype(F32), "seq", scatter_dimension=1, tiled=True)
    return lax.psum(share.astype(BF), "dp").astype(F32)


def joined(halves, z_first=False):
    width = halves[0].shape[-1]
    if z_first:
        shards = jnp.stack([half.reshape(2, 2, 4, -1, width) for half in halves]).transpose(2, 1, 0, 3, 4, 5)
    else:
        shards = jnp.stack([half.reshape(4, 2, 2, -1, width) for half in halves]).transpose(3, 2, 0, 1, 4, 5)
    return shards.reshape((SHARDS,) + shards.shape[3:])


def plain_sums(wide0, wide1, part, narrow, d, ff):
    part, narrow = joined(part, True), joined(narrow)
    down, up, square = [], [], []
    for wide, terms in ((wide0, narrow[:, :, :64]), (wide1, part)):
        wide = joined(wide).reshape(SHARDS, 512, 512)
        down.append(wide[:, :, :256].transpose(0, 2, 1).reshape(ff, d))
        up.append(wide[:, :, 256:].reshape(SHARDS, ff // 256, d // SHARDS, 256).transpose(0, 2, 1, 3).reshape(d, ff))
        square.append(terms.transpose(1, 0, 2, 3).reshape(4, d, d))
    square = jnp.stack(square, axis=1)
    small = narrow[0, 0, 64:74].reshape(5, 2, d)
    bias = narrow[0, 1, 64:72].reshape(2, ff)
    terms = (small[0], small[1], square[1], square[2], square[3], square[0], small[2], small[3], jnp.stack(up), bias,
             jnp.stack(down), small[4])
    return tuple(scattered(term) for term in terms)


def on_device(
    inputs, cotangent, item_lengths, attn_gain, attn_bias, query_weight, key_weight, value_weight, output_weight,
    ffn_gain, ffn_bias, up_weight, up_bias, down_weight, down_bias,
):
    rows, width, depth = inputs.shape
    ff = up_weight.shape[2]
    group = SLOTS // width
    halving = lax.axis_size("dp") == 4 and lax.axis_size("seq") == SHARDS
    lengths = item_lengths.T
    clock = Clock()
    packed = pack(inputs, group)
    clock.done(packed[0])
    x_parts = swap(clock, packed[1:])
    cotangent = clock.after(cotangent)
    first = pack(cotangent, group)
    clock.done(first[0])
    cot_parts = swap(clock, first[1:])
    clock.done(clock.after(first[0]))
    norms = (attn_gain, attn_bias, ffn_gain, ffn_bias, up_bias, down_bias)
    wts = (query_weight, key_weight, value_weight, output_weight, up_weight, down_weight)
    x_parts, cot_parts = [packed[0]] + x_parts, [first[0]] + cot_parts
    kept0, h1 = forward_first(lengths, x_parts, norms, wts)
    kept1, wide1, dz1, ffn1 = forward_last(1, halving, lengths, h1, cot_parts, norms, wts)
    clock.done(ffn1)
    line = rows // group, group
    if halving:
        f1 = Chunk(clock, wide1)
    dg, do, dout, mid1 = back_top(1, lengths, cot_parts, kept1, clock.after(dz1), norms, wts)
    clock.done(mid1)
    if halving:
        advance(clock, [(f1, "split", PLANE_1)])
    wide0, (dh, dz0, dq, dk, dv, attn1, ffn0) = back_between(
        1, halving, lengths, clock.after(dg), do, kept1, kept0, norms, wts, *line)
    clock.done(attn1)
    if halving:
        f0 = Chunk(clock, wide0)
    if halving:
        advance(clock, [(f1, "close", None)], LONG)
    part = square_halves(halving, clock.after(kept1[0]), (dq, dk, dv), dout)
    clock.done(part[0])
    if halving:
        a1 = Chunk(clock, part)
        advance(clock, [(f1, "split", PLANE_2), (f0, "split", PLANE_2)])
        advance(clock, [(a1, "split", LINE_1)])
    narrow, parts = back_bottom(
        halving, lengths, clock.after(dh), dz0, (attn1, mid1, ffn0, ffn1), kept0, norms, wts, width, group)
    clock.done(parts[0])
    if halving:
        a0 = Chunk(clock, narrow)
        advance(clock, [(f1, "split", LINE_1), (a1, "split", LINE_2)], LONG)
        advance(clock, [(f0, "split", PLANE_1), (a0, "split", PLANE_1)])
    both = results(1, kept1, norms, wts, clock.after(parts))
    clock.done(both[0])
    if halving:
        advance(clock, [(a0, "split", PLANE_2), (a1, "whole", PLANE_2), (f0, "split", LINE_1), (f1, "split", LINE_2)])
        advance(clock, [(f1, "gather", PLANE_1), (a1, "whole", PLANE_1), (a0, "split", LINE_1), (f0, "split", LINE_2)])
        advance(clock, [(f1, "gather", PLANE_2), (f0, "gather", PLANE_2), (a0, "split", LINE_2), (a1, "close", None)])
    mine = swap(clock, both[1:])
    if halving:
        advance(clock, [(f0, "gather", PLANE_1), (a0, "spread", (PLANE_1, PLANE_2, PLANE_3)), (f1, "order", (PLANE_1, PLANE_2))], LONG)
    own = clock.after(both[0])
    if not halving:
        output, input_grad = unpack([own] + mine)
        return (output, input_grad) + plain_sums(wide0, wide1, part, narrow, depth, ff)

    advance(clock, [(f0, "order", (PLANE_2, PLANE_1))])
    wide0, wide1 = [c.kept.reshape(4, -1, depth) for c in (f0, f1)]
    down, up = finish_wide(clock.after(wide0), wide1, depth, ff)
    clock.done(down)
    do, dq, dk, dv, ag, ab, fg, fb, bd, bu = finish_last(clock.after(a0.kept), a0.all, a1.kept, depth)
    clock.done(do)
    output, input_grad = unpack([clock.after(own)] + mine)
    return output, input_grad, ag, ab, dq, dk, dv, do, fg, fb, up, bu, down, bd


def solution(mesh):
    spec = jax.sharding.PartitionSpec
    whole, split = spec(), spec("dp", "seq", None)
    vec, mat = spec(None, "seq"), spec(None, "seq", None)
    return jax.shard_map(
        on_device,
        mesh=mesh,
        in_specs=(split, split, spec("dp", None)) + (whole,) * 12,
        out_specs=(split, split, vec, vec, mat, mat, mat, mat, vec, vec, mat, vec, mat, vec),
        check_vma=False,
    )
```

```python
import jax
import jax.numpy as jnp
from jax import lax
from jax.experimental import pallas as pl
from jax.experimental.pallas import tpu as pltpu

H = 8
SLOTS = 256
EPS = 1e-05
NEG = -1000000000.0
BF = jnp.bfloat16
F32 = jnp.float32
GELU_C = 0.7978845608028654
GELU_A = 0.044715
STEP = 512
SHARDS = 8
LONG = 30_000_000_000
FIVE = 0
SIX = 0
SECOND = slice(128, 192)

NN = (((1,), (0,)), ((), ()))
NT = (((1,), (1,)), ((), ()))
TN = (((0,), (0,)), ((), ()))

SDS = jax.ShapeDtypeStruct
IN_VMEM = pl.BlockSpec(memory_space=pltpu.VMEM)
IN_SMEM = pl.BlockSpec(memory_space=pltpu.SMEM)


def dot(left, right, form=NN):
    return lax.dot_general(left, right, form, preferred_element_type=F32)


def normalize(values):
    centered = values - jnp.mean(values, axis=-1, keepdims=True)
    inv = lax.rsqrt(jnp.mean(centered * centered, axis=-1, keepdims=True) + EPS)
    return centered * inv, inv


def norm_back(dy, values, gain):
    xhat, inv = normalize(values)
    dgain = jnp.sum(dy * xhat, axis=0, keepdims=True)
    dbias = jnp.sum(dy, axis=0, keepdims=True)
    dx = dy * gain
    dx = inv * (dx - jnp.mean(dx, axis=-1, keepdims=True) - xhat * jnp.mean(dx * xhat, axis=-1, keepdims=True))
    return dx, dgain, dbias


def head_masks(width):
    lane = lax.broadcasted_iota(jnp.int32, (1, 2 * width), 1)
    low = (lane < width).astype(F32).astype(BF)
    return low, (1.0 - low.astype(F32)).astype(BF)


def tiles(m):
    return [slice(SLOTS * i, SLOTS * (i + 1)) for i in range(m // SLOTS)]


def call(body, name, operands, outs, scratch, limit, flops, moved):
    return pl.pallas_call(
        body,
        in_specs=[IN_SMEM if x.dtype == jnp.int32 else IN_VMEM for x in operands],
        out_specs=[IN_VMEM] * len(outs),
        out_shape=[SDS(*out) for out in outs],
        scratch_shapes=[pltpu.VMEM(*x) for x in scratch],
        compiler_params=pltpu.CompilerParams(vmem_limit_bytes=limit << 20),
        cost_estimate=pl.CostEstimate(flops=flops, bytes_accessed=moved, transcendentals=0),
        name=name,
    )(*operands)


def member_of(group):
    return lax.axis_index("seq") % group


def lengths_of(lengths, units, group):
    seq = lax.axis_index("seq")
    return [lengths[seq // group, (seq % group) * units + u] for u in range(units)]


def pack(local, group):
    rows, width, depth = local.shape
    n = rows // group

    def body(x_ref, *outs):
        for d, out in enumerate(outs):
            out[...] = x_ref[pl.ds((member_of(group) ^ d) * n, n)]

    return call(body, "pack", [local], [((n, width, depth), local.dtype)] * group, [], 4, 20_000_000_000, 1 << 20)


def unpack(pieces):
    _, n, width, depth = pieces[0].shape

    def body(*refs):
        outs = refs[-2:]
        for d, ref in enumerate(refs[:-2]):
            for t in range(2):
                outs[t][pl.ds((member_of(len(pieces)) ^ d) * n, n)] = ref[t]

    return call(body, "unpack", pieces, [((n * len(pieces), width, depth), BF)] * 2, [], 4, 0, 1 << 20)


def regroup(lens, pieces, put):
    n, width, _ = pieces[0].shape
    j = member_of(len(pieces))
    for d, piece in enumerate(pieces):
        for u in range(n):
            start = (j ^ d) * width
            at = pl.ds(pl.multiple_of(u * SLOTS + start, width), width)
            block = piece[u]
            if lens is not None:
                slot = lax.broadcasted_iota(jnp.int32, (width, 1), 0) + start
                block = jnp.where(slot < lens[u], block.astype(F32), 0.0)
            put(at, block)


def deal(values, pieces):
    for d, piece in enumerate(pieces):
        n, width, _ = piece.shape
        for u in range(n):
            at = pl.ds(pl.multiple_of(u * SLOTS + (member_of(len(pieces)) ^ d) * width, width), width)
            piece[u] = values[at, :].astype(BF)


def stacked(head):
    return slice(SLOTS * (head % 2), SLOTS * (head % 2) + SLOTS)


def apart(pair, masks):
    return jnp.concatenate([pair * masks[0], pair * masks[1]], axis=0)


def pair_scratch(m):
    return ((m // SLOTS * (H // 2), 2 * SLOTS, SLOTS), BF)


def forward_attention(lens, h, gain, bias, wq, wk, wv, a_ref, q_ref, k_ref, v_ref, o_ref, lse_ref, p_ref):
    masks = head_masks(64)
    for i, rows in enumerate(tiles(h.shape[0])):
        xhat, _ = normalize(h[rows, :].astype(F32))
        a = (xhat * gain + bias).astype(BF)
        a_ref[rows, :] = a
        q_ref[rows, :] = (dot(a, wq[...]).astype(BF).astype(F32) * 0.125).astype(BF)
        k_ref[rows, :] = dot(a, wk[...]).astype(BF)
        v_ref[rows, :] = dot(a, wv[...]).astype(BF)
    key = lax.broadcasted_iota(jnp.int32, (SLOTS, 1), 0)
    for i, rows in enumerate(tiles(h.shape[0])):
        valid = key < lens[i]
        for head in range(H):
            cols = slice(128 * (head // 2), 128 * (head // 2) + 128)
            st = jnp.where(valid, dot(k_ref[rows, cols] * masks[head % 2], q_ref[rows, cols], NT), NEG)
            top = jnp.max(st, axis=0, keepdims=True)
            e = jnp.exp(st - top)
            tot = jnp.sum(e, axis=0, keepdims=True)
            p_ref[i * (H // 2) + head // 2, stacked(head), :] = (e * (1.0 / tot)).astype(BF)
            lse_ref[i * H + head, :] = (top + jnp.log(tot))[0]
    for i, rows in enumerate(tiles(h.shape[0])):
        for pair in range(H // 2):
            cols = slice(128 * pair, 128 * pair + 128)
            o_ref[rows, cols] = dot(p_ref[i * (H // 2) + pair], apart(v_ref[rows, cols], masks), TN).astype(BF)


def forward_ffn(h, o, wo, gain, bias, wup, bup, wdown, bdown, g_ref, c_ref, u_ref, gp_ref, n_ref):
    m, ff = h.shape[0], wup.shape[1]
    for rows in tiles(m):
        g = h[rows, :].astype(F32) + dot(o[rows, :], wo[...])
        g_ref[rows, :] = g
        xhat, _ = normalize(g)
        c_ref[rows, :] = (xhat * gain + bias).astype(BF)
    for f in range(0, ff, 256):
        fs = slice(f, f + 256)
        for rows in tiles(m):
            z = dot(c_ref[rows, :], wup[:, fs]) + bup[:, fs]
            z2 = z * z
            t = jnp.tanh(z * (GELU_C + GELU_C * GELU_A * z2))
            half = 0.5 + 0.5 * t
            gp = half + (0.5 * z) * (1.0 - t * t) * (GELU_C + 3.0 * GELU_C * GELU_A * z2)
            u_ref[rows, fs] = (z * half).astype(BF)
            gp_ref[rows, fs] = gp.astype(BF)
    if n_ref is not None:
        layer_output(g_ref, u_ref, wdown, bdown, n_ref)


def layer_output(g_ref, u_ref, wdown, bdown, n_ref):
    for rows in tiles(g_ref.shape[0]):
        n_ref[rows, :] = g_ref[rows, :] + (dot(u_ref[rows, :], wdown[...]) + bdown)


def store(core, keep, send, quarter, z, rows, cols, even, odd):
    mine, other = jnp.where(core == 0, even, odd), jnp.where(core == 0, odd, even)
    at = 2 * (z % 2) + z // 2
    keep[quarter, at, rows, cols] = mine
    send[quarter, at, rows, cols] = other


def ffn_terms(core, dm_ref, u_ref, gp_ref, c_ref, wdown, keep, send, dz_ref, sm_ref):
    ff = u_ref.shape[1]
    dm = dm_ref[...]
    for f in range(ff // STEP):
        res = dot(dm, u_ref[:, STEP * f : STEP * f + STEP], TN).astype(BF).reshape(4, 128, STEP)
        store(core, keep, send, slice(None), f, slice(0, 128), slice(0, 256), res[:, :, 0:256], res[:, :, 256:512])
    sm_ref[...] = jnp.zeros_like(sm_ref)
    sm_ref[0:1, :] = jnp.sum(dm.astype(F32), axis=0, keepdims=True)
    for f in range(ff // STEP):
        fs = slice(STEP * f, STEP * f + STEP)
        dz = (dot(dm, wdown[fs, :], NT) * gp_ref[:, fs].astype(F32)).astype(BF)
        dz_ref[:, fs] = dz
        sm_ref[1 + f : 2 + f, :] = jnp.sum(dz.astype(F32), axis=0, keepdims=True)
        res = dot(c_ref[...], dz, TN).astype(BF).reshape(4, 128, STEP)
        for t in range(2):
            rows, part = slice(64 * t, 64 * t + 64), res[:, :, 256 * t : 256 * t + 256]
            for z in range(4):
                store(core, keep, send, f, z, rows, slice(256, 512), part[z, 0:64], part[z, 64:128])


KEPT = ("a", "q", "k", "v", "o", "lse", "g", "c", "u", "gp")


def kept_shapes(m, d, ff):
    wide, narrow = (m, ff), (m, d)
    return [(narrow, BF)] * 5 + [((m // SLOTS * H, SLOTS), F32), (narrow, F32), (narrow, BF), (wide, BF), (wide, BF)]


def row(ref, l):
    return ref[l : l + 1, :].astype(F32)


def forward_layer(l, lens, h, norms, wts, kept, last, p_ref):
    ag, ab, fg, fb, bup, bdown = norms
    wq, wk, wv, wo, wup, wdown = [w.at[l] for w in wts]
    a, q, k, v, o, lse, g, c, u, gp = kept
    forward_attention(lens, h, row(ag, l), row(ab, l), wq, wk, wv, a, q, k, v, o, lse, p_ref)
    forward_ffn(h, o, wo, row(fg, l), row(fb, l), wup, row(bup, l), wdown, row(bdown, l), g, c, u, gp, last)


def chunk_shape(rows):
    return ((4, SHARDS // 2, rows, 512), BF)


def parity(halving):
    return lax.axis_index("seq") % 2 if halving else 0


def forward_first(lengths, parts, norms, wts):
    _, d, ff = wts[4].shape
    n, width, _ = parts[0].shape
    group = len(parts)
    m = n * group * width

    def body(*refs):
        lengths, refs = refs[0], refs[1:]
        parts, refs = refs[:group], refs[group:]
        norms, wts, kept, (x_ref, last, p_ref) = refs[:6], refs[6:12], refs[12:22], refs[22:]

        def put(at, block):
            x_ref[at, :] = block

        regroup(None, parts, put)
        forward_layer(0, lengths_of(lengths, n, group), x_ref, norms, wts, kept, last, p_ref)

    outs = kept_shapes(m, d, ff) + [((m, d), BF), ((m, d), F32)]
    res = call(body, "forward_first", [lengths, *parts, *norms, *wts], outs, [pair_scratch(m)], 4, 2 * m * (4 * d * d + 2 * d * ff), 24 << 20)
    return res[:11], res[11]


def forward_last(l, halving, lengths, h, parts, norms, wts):
    _, d, ff = wts[4].shape
    n, width, _ = parts[0].shape
    group = len(parts)
    m = n * group * width
    per = kept_shapes(m, d, ff)

    def body(*refs):
        lengths, h = refs[:2]
        refs = refs[2:]
        parts, refs = refs[:group], refs[group:]
        norms, wts, refs = refs[:6], refs[6:12], refs[12:]
        kept, refs = refs[:8], refs[8:]
        keep, send, dz_ref, sm_ref, c, gp, dm_ref, p_ref = refs
        lens = lengths_of(lengths, n, group)

        def put(at, block):
            dm_ref[at, :] = block.astype(BF)

        regroup(lens, parts, put)
        forward_layer(l, lens, h, norms, wts, [*kept[:7], c, kept[7], gp], None, p_ref)
        ffn_terms(parity(halving), dm_ref, kept[7], gp, c, wts[5].at[l], keep, send, dz_ref, sm_ref)

    outs = per[:7] + [per[8]] + [chunk_shape(128)] * 2 + [((m, ff), BF), ((8, d), F32)]
    *kept, keep, send, dz, sums = call(
        body, "forward_last", [lengths, h, *parts, *norms, *wts], outs,
        [per[7], per[9], ((m, d), BF), pair_scratch(m)], 20, 2 * m * (4 * d * d + 4 * d * ff), 24 << 20)
    return kept[:7] + [None, kept[7], None, h], (keep, send), dz, sums


def mid_terms(l, dh_ref, g, o, dz, gain, wup, wo, dg_ref, do_ref, dr_ref, sm_ref):
    m, d = g.shape
    dgain = dbias = None
    for i, rows in enumerate(tiles(m)):
        dc = dot(dz[rows, :], wup[l], NT)
        dx, dg1, db1 = norm_back(dc, g[rows, :], row(gain, l))
        dg = dh_ref[rows, :] + dx
        dg_ref[rows, :] = dg
        dr_ref[rows, :] = dg.astype(BF)
        dgain, dbias = (dg1, db1) if i == 0 else (dgain + dg1, dbias + db1)
    sm_ref[...] = jnp.zeros_like(sm_ref)
    sm_ref[0:1, :] = dgain
    sm_ref[1:2, :] = dbias
    do_ref[...] = dot(dr_ref[...], wo[l], NT).astype(BF)
    return dot(o[...], dr_ref[...], TN).astype(BF).reshape(SHARDS // 2, 2, d // SHARDS, d)


def attn_terms(l, lens, dg, do, lse, q, k, v, h, gain, wq, wk, wv, dq_ref, dk_ref, dv_ref, p_ref, s_ref, put):
    m, d = dg.shape
    masks = head_masks(64)
    low = lax.broadcasted_iota(jnp.int32, (1, 128), 1) < 64
    key = lax.broadcasted_iota(jnp.int32, (SLOTS, 1), 0)
    for i, rows in enumerate(tiles(m)):
        valid = key < lens[i]
        for head in range(H):
            cols, n, mk = slice(128 * (head // 2), 128 * (head // 2) + 128), i * (H // 2) + head // 2, masks[head % 2]
            st = jnp.where(valid, dot(k[rows, cols] * mk, q[rows, cols], NT), NEG)
            pt = jnp.exp(st - lse[i * H + head, :][None, :])
            dpt = dot(v[rows, cols] * mk, do[rows, cols], NT)
            delta = jnp.sum(pt * dpt, axis=0, keepdims=True)
            p_ref[n, stacked(head), :] = pt.astype(BF)
            s_ref[n, stacked(head), :] = (pt * (dpt - delta)).astype(BF)
    for i, rows in enumerate(tiles(m)):
        for pair in range(H // 2):
            cols, n = slice(128 * pair, 128 * pair + 128), i * (H // 2) + pair
            dq_ref[rows, cols] = (dot(s_ref[n], apart(k[rows, cols], masks), TN) * 0.125).astype(BF)
            both = dot(s_ref[n], q[rows, cols])
            dk_ref[rows, cols] = jnp.where(low, both[0:SLOTS], both[SLOTS:]).astype(BF)
            both = dot(p_ref[n], do[rows, cols])
            dv_ref[rows, cols] = jnp.where(low, both[0:SLOTS], both[SLOTS:]).astype(BF)
    dgain = dbias = None
    for i, rows in enumerate(tiles(m)):
        da = dot(dq_ref[rows, :], wq[l], NT) + dot(dk_ref[rows, :], wk[l], NT) + dot(dv_ref[rows, :], wv[l], NT)
        dx, dg1, db1 = norm_back(da, h[rows, :].astype(F32), row(gain, l))
        put(rows, dg[rows, :] + dx)
        dgain, dbias = (dg1, db1) if i == 0 else (dgain + dg1, dbias + db1)
    return dgain, dbias


def square_terms(a, *grads):
    d = a.shape[1]
    return [dot(a[...], ref[...], TN).astype(BF).reshape(SHARDS // 2, 2, d // SHARDS, d) for ref in grads]


def back_top(l, lengths, parts, kept, dz, norms, wts):
    g, o = kept[6], kept[4]
    m, d = g.shape
    group = len(parts)

    def body(lengths, *refs):
        parts, refs = refs[:group], refs[group:]
        g, o, dz, gain, wup, wo, dg_ref, do_ref, dout_ref, sm_ref, dr_ref, dh_ref = refs

        def put(at, block):
            dh_ref[at, :] = block

        regroup(lengths_of(lengths, m // SLOTS, group), parts, put)
        dout_ref[...] = mid_terms(l, dh_ref, g, o, dz, gain, wup, wo, dg_ref, do_ref, dr_ref, sm_ref)

    outs = [((m, d), F32), ((m, d), BF), ((SHARDS // 2, 2, d // SHARDS, d), BF), ((8, d), F32)]
    return call(body, "back_top", [lengths, *parts, g, o, dz, norms[2], wts[4], wts[3]], outs, [((m, d), BF), ((m, d), F32)], 6,
                2 * m * 6 * d * d, 9 << 20)


def back_between(l, halving, lengths, dg, do, kept, under, norms, wts, units, group):
    a, q, k, v, o, lse, g, c, u, gp, h = kept
    c, u, gp = under[7:10]
    m, d = dg.shape
    ff = u.shape[1]

    def body(lengths, dg, do, lse, q, k, v, h, gain, wq, wk, wv, c, u, gp, wdown,
             keep0, send0, dh_ref, dz_ref, dq_ref, dk_ref, dv_ref, sm_ref, sm0_ref, dm_ref, p_ref, s_ref):
        core, lens = parity(halving), lengths_of(lengths, units, group)

        def put(rows, dh):
            dh_ref[rows, :] = dh
            dm_ref[rows, :] = dh.astype(BF)

        dgain, dbias = attn_terms(l, lens, dg, do, lse, q, k, v, h, gain, wq, wk, wv, dq_ref, dk_ref, dv_ref, p_ref, s_ref, put)
        sm_ref[...] = jnp.zeros_like(sm_ref)
        sm_ref[0:1, :] = dgain
        sm_ref[1:2, :] = dbias
        ffn_terms(core, dm_ref, u, gp, c, wdown.at[l - 1], keep0, send0, dz_ref, sm0_ref)

    outs = [chunk_shape(128)] * 2 + [((m, d), F32), ((m, ff), BF)] + [((m, d), BF)] * 3 + [((8, d), F32)] * 2
    keep0, send0, *rest = call(
        body, "back_between", [lengths, dg, do, lse, q, k, v, h, norms[0], *wts[:3], c, u, gp, wts[5]], outs,
        [((m, d), BF), pair_scratch(m), pair_scratch(m)], 9, 2 * m * 19 * d * d, 20 << 20)
    return (keep0, send0), rest


def square_halves(halving, a, grads, dout):
    d = a.shape[1]

    def body(a, dq, dk, dv, dout, keep, send):
        core = parity(halving)
        for n, term in enumerate([dout[...], *square_terms(a, dq, dk, dv)]):
            for z in range(SHARDS // 2):
                at, rows = 2 * (z % 2) + z // 2, slice(64 * n, 64 * n + 64)
                keep[at, rows, :] = jnp.where(core == 0, term[z, 0], term[z, 1])
                send[at, rows, :] = jnp.where(core == 0, term[z, 1], term[z, 0])

    outs = [((SHARDS // 2, 256, d), BF)] * 2
    return call(body, "square_halves", [a, *grads, dout], outs, [], 4, 2 * a.shape[0] * 3 * d * d, 4 << 20)


def back_bottom(halving, lengths, dh, dz, smalls, kept, norms, wts, width, group):
    a, q, k, v, o, lse, g, c, u, gp, h = kept
    m, d = dh.shape
    units = m // SLOTS

    def body(lengths, dh, g, o, dz, fgain, wup, wo, lse, q, k, v, a, h, gain, wq, wk, wv, attn1, mid1, ffn0, ffn1, keep, send, *refs):
        outs, refs = refs[:group], refs[group:]
        dg, do, dr, mid0, dq_ref, dk_ref, dv_ref, dx_ref, p_ref, s_ref = refs
        core, lens = parity(halving), lengths_of(lengths, units, group)
        first = mid_terms(0, dh, g, o, dz, fgain, wup, wo, dg, do, dr, mid0)
        for z in range(SHARDS // 2):
            store(core, keep, send, 0, z, slice(0, 64), slice(None), first[z, 0], first[z, 1])

        def put(rows, value):
            dx_ref[rows, :] = value

        dgain, dbias = attn_terms(0, lens, dg, do, lse, q, k, v, h, gain, wq, wk, wv, dq_ref, dk_ref, dv_ref, p_ref, s_ref, put)
        for n, term in enumerate(square_terms(a, dq_ref, dk_ref, dv_ref)):
            for z in range(SHARDS // 2):
                store(core, keep, send, n + 1, z, slice(0, 64), slice(None), term[z, 0], term[z, 1])
        lines = [dgain, attn1[0:1, :], dbias, attn1[1:2, :], mid0[0:1, :], mid1[0:1, :], mid0[1:2, :], mid1[1:2, :],
                 ffn0[0:1, :], ffn1[0:1, :]]
        zero = jnp.zeros((1, d), F32)
        block = jnp.concatenate(lines + [zero] * 6, axis=0).astype(BF)
        other = jnp.concatenate([ffn0[1:5, :], ffn1[1:5, :]] + [zero] * 8, axis=0).astype(BF)
        for half in (keep, send):
            for at in range(SHARDS // 2):
                half[0, at, 64:80, :] = block
                half[1, at, 64:80, :] = other
                for t in (2, 3):
                    half[t, at, 64:80, :] = jnp.zeros((16, d), BF)
        deal(dx_ref, outs)

    outs = [chunk_shape(80)] * 2 + [((units, width, d), BF)] * group
    wide, narrow = ((m, d), F32), ((m, d), BF)
    keep, send, *parts = call(
        body, "back_bottom",
        [lengths, dh, g, o, dz, norms[2], wts[4], wts[3], lse, q, k, v, a, h, norms[0], *wts[:3], *smalls], outs,
        [wide, narrow, narrow, ((8, d), F32), narrow, narrow, narrow, wide, pair_scratch(m), pair_scratch(m)], 12, 2 * m * 16 * d * d, 20 << 20)
    return (keep, send), parts


def results(l, kept, norms, wts, parts):
    g, u = kept[6], kept[8]
    group = len(parts)
    shape = (2,) + parts[0].shape

    def body(g, u, wdown, bdown, *refs):
        last = refs[-1]
        layer_output(g, u, wdown.at[l], row(bdown, l), last)
        outs = refs[group : 2 * group]
        deal(last, [out.at[0] for out in outs])
        for part, out in zip(refs[:group], outs):
            out[1] = part[...]

    return call(body, "results", [g, u, wts[5], norms[5], *parts], [(shape, BF)] * group, [(g.shape, F32)], 8,
                2 * u.shape[0] * u.shape[1] * g.shape[1], 4 << 20)


def finish_wide(wide0, wide1, d, ff):
    def body(w0, w1, down, up):
        for l, ref in enumerate((w0, w1)):
            for n in range(4):
                part = ref[n].astype(F32)
                down[l, :, 128 * n : 128 * n + 128] = part[:, 0:256].T
                for t in range(2):
                    at = 512 * n + 256 * t
                    up[l, :, at : at + 256] = part[64 * t : 64 * t + 64, 256:512]

    return call(body, "finish_wide", [wide0, wide1], [((2, 256, d), F32), ((2, 64, ff), F32)], [], 8, 0, 1024)


def finish_last(own, others, square, d):
    rows = own.shape[0]
    offsets = [first for _, first in others]

    def body(own, *refs):
        parts, other = [(own, 0), *zip(refs[:3], offsets)], refs[3]
        outs = refs[4:8]
        ag, ab, fg, fb, bd, bu, x, vsm = refs[8:]
        here = 2 * bit_of(PLANE_1) + bit_of(PLANE_2)
        for (ref, first), flip in zip(parts, (0, 2, 1, 3)):
            x[here ^ flip] = ref[first : first + rows, :]
        for n in range(4):
            outs[n][0] = x[n, 0:64, :].astype(F32)
            outs[n][1] = other[64 * n : 64 * n + 64, :].astype(F32)
        s = lax.axis_index("seq")
        vsm[...] = x[0:2, 64:80, :].astype(F32)
        pair = vsm[0, :, pl.ds(pl.multiple_of((s // 2) * 128, 128), 128)]
        mine = jnp.where(s % 2 == 0, pair[:, 0:64], pair[:, 64:128])
        for n, ref in enumerate((ag, ab, fg, fb, bd)):
            ref[...] = mine[2 * n : 2 * n + 2, :]
        for l in range(2):
            bu[l : l + 1, :] = vsm[1, pl.ds(4 * l + s // 2, 1), pl.ds(pl.multiple_of((s % 2) * 256, 256), 256)]

    outs = [((2, 64, d), F32)] * 4 + [((2, 64), F32)] * 5 + [((2, 256), F32)]
    return call(body, "finish_last", [own, *[array for array, _ in others], square], outs, [((4, rows, d), BF), ((2, 16, d), F32)], 8, 0, 2 << 20)


def swap(clock, sends):
    size = lax.axis_size("seq")
    out = [None] * len(sends)
    for d, s in enumerate(sends):
        clock.send(s, [(i, i ^ (d + 1)) for i in range(size)], "seq", lambda value, d=d: out.__setitem__(d, value))
    return out


BOTH = ("dp", "seq")


def pairs_of(flip):
    out = []
    for y in range(2):
        for x in range(2):
            for z in range(4):
                for c in range(2):
                    y2, x2, z2, c2 = flip(y, x, z, c)
                    out.append((y * 16 + x * 8 + z * 2 + c, y2 * 16 + x2 * 8 + z2 * 2 + c2))
    return out


CORE = pairs_of(lambda y, x, z, c: (y, x, z, 1 - c))
PLANE_1 = pairs_of(lambda y, x, z, c: (y, 1 - x, z, c) if c == 0 else (1 - y, x, z, c))
PLANE_2 = pairs_of(lambda y, x, z, c: (y, 1 - x, z, c) if c == 1 else (1 - y, x, z, c))
PLANE_3 = pairs_of(lambda y, x, z, c: (1 - y, 1 - x, z, c))
LINE_1 = pairs_of(lambda y, x, z, c: (y, x, z ^ 1, c))
LINE_2 = pairs_of(lambda y, x, z, c: (y, x, z ^ 2, c))


def bit_of(pairs):
    dp, seq = lax.axis_index("dp"), lax.axis_index("seq")
    if pairs is LINE_1:
        return (seq // 2) % 2
    if pairs is LINE_2:
        return seq // 4
    y, x = dp // 2, dp % 2
    return jnp.where((seq % 2 == 0) == (pairs is PLANE_1), x, y)


class Clock:
    def __init__(self):
        self.last, self.waiting = None, []

    def done(self, value):
        self.last = value

    def send(self, value, pairs, axes, arrived):
        self.waiting.append((value, pairs, axes, arrived))

    def after(self, value):
        waiting, self.waiting = self.waiting, []
        value, last, sent = lax.optimization_barrier((value, self.last, [w[0] for w in waiting]))
        for v, (_, pairs, axes, arrived) in zip(sent, waiting):
            arrived(lax.ppermute(v, axes, pairs))
        return value


class Chunk:
    def __init__(self, clock, halves):
        self.kept = halves[0].reshape(-1, halves[0].shape[-1])
        self.moved, self.paired, self.all = None, False, []
        clock.send(halves[1].reshape(self.kept.shape), CORE, BOTH, lambda value: self.arrived(value, 0))

    def arrived(self, value, first):
        self.moved = (value, first)
        self.all.append(self.moved)


BLOCK = 256


def blocks(count):
    return [(start, min(BLOCK, count - start)) for start in range(0, count, BLOCK)]


def advance(clock, items, weight=0):
    for (chunk, _, _), kept in zip(items, clock.after([chunk.kept for chunk, _, _ in items])):
        chunk.kept = kept
    arrays, lanes, keeps, plan = [], {}, [], []

    def index(array):
        for n, other in enumerate(arrays):
            if other is array:
                return n
        arrays.append(array)
        return len(arrays) - 1

    for chunk, kind, pairs in items:
        rows = chunk.kept.shape[0]
        now = 2 * rows if chunk.paired else rows
        left = rows // 2 if kind == "split" else now
        lane = []
        for each in pairs if kind == "spread" else (pairs,) if kind in ("split", "whole", "gather") else ():
            key = [n for n in lanes if lanes[n][0] is each]
            name = key[0] if key else len(lanes)
            first = lanes[name][1] if key else 0
            lane.append((name, first))
            lanes[name] = (each, first + left)
        at, by, offset = index(chunk.kept), None, 0
        if chunk.moved:
            by, offset = index(chunk.moved[0]), chunk.moved[1]
        plan.append((kind, pairs, at, by, offset, rows, chunk.paired, lane))
        keeps.append(left)
    count = len(lanes)

    def body(*refs):
        ins, outs = refs[: len(arrays)], refs[len(arrays) :]
        for n, (kind, pairs, at, by, offset, rows, paired, lane) in enumerate(plan):
            kept, moved, left = ins[at], None if by is None else ins[by], outs[count + n]
            sent, start = (outs[lane[0][0]], lane[0][1]) if lane else (None, 0)

            def summed(low, size):
                if isinstance(low, int):
                    first, second = slice(low, low + size), slice(offset + low, offset + low + size)
                else:
                    first = pl.ds(pl.multiple_of(low, 16), size)
                    second = pl.ds(pl.multiple_of(offset + low, 16), size)
                if moved is None:
                    return kept[first, :]
                return (kept[first, :].astype(F32) + moved[second, :].astype(F32)).astype(BF)

            if kind == "split":
                half = rows // 2
                bit = bit_of(pairs)
                for low, size in blocks(half):
                    sent[start + low : start + low + size, :] = summed((1 - bit) * half + low, size)
                    left[low : low + size, :] = summed(bit * half + low, size)
            elif kind == "order":
                part = rows // 2
                own = 2 * bit_of(pairs[0]) + bit_of(pairs[1])
                for m, flip in enumerate((0, 2, 1, 3)):
                    source, base = (kept, 0) if m < 2 else (moved, offset)
                    base += (m % 2) * part
                    left[pl.ds(pl.multiple_of((own ^ flip) * part, 16), part), :] = source[base : base + part, :]
            elif paired:
                for low, size in blocks(rows):
                    for source, base, to in ((kept, low, low), (moved, offset + low, rows + low)):
                        value = source[base : base + size, :]
                        left[to : to + size, :] = value
                        sent[start + to : start + to + size, :] = value
            else:
                for low, size in blocks(rows):
                    value = summed(low, size)
                    left[low : low + size, :] = value
                    for name, to in lane:
                        outs[name][to + low : to + low + size, :] = value

    width = items[0][0].kept.shape[1]
    sizes = [lanes[n][1] for n in range(count)] + keeps
    results = call(body, "advance", arrays, [((rows, width), BF) for rows in sizes], [], 4, weight, 1 << 20)
    clock.done(results[0])
    for n in range(count):
        here = [(item[0], to) for item, spec in zip(items, plan) for name, to in spec[-1] if name == n]

        def arrived(value, here=here):
            for chunk, first in here:
                chunk.arrived(value, first)

        clock.send(results[n], lanes[n][0], BOTH, arrived)
    for (chunk, kind, _), kept in zip(items, results[count:]):
        chunk.kept, chunk.moved, chunk.all = kept, None, []
        chunk.paired = kind == "gather"


def scattered(term):
    share = lax.psum_scatter(term.astype(F32), "seq", scatter_dimension=1, tiled=True)
    return lax.psum(share.astype(BF), "dp").astype(F32)


def joined(halves, z_first=False):
    width = halves[0].shape[-1]
    if z_first:
        shards = jnp.stack([half.reshape(2, 2, 4, -1, width) for half in halves]).transpose(2, 1, 0, 3, 4, 5)
    else:
        shards = jnp.stack([half.reshape(4, 2, 2, -1, width) for half in halves]).transpose(3, 2, 0, 1, 4, 5)
    return shards.reshape((SHARDS,) + shards.shape[3:])


def plain_sums(wide0, wide1, part, narrow, d, ff):
    part, narrow = joined(part, True), joined(narrow)
    down, up, square = [], [], []
    for wide, terms in ((wide0, narrow[:, :, :64]), (wide1, part)):
        wide = joined(wide).reshape(SHARDS, 512, 512)
        down.append(wide[:, :, :256].transpose(0, 2, 1).reshape(ff, d))
        up.append(wide[:, :, 256:].reshape(SHARDS, ff // 256, d // SHARDS, 256).transpose(0, 2, 1, 3).reshape(d, ff))
        square.append(terms.transpose(1, 0, 2, 3).reshape(4, d, d))
    square = jnp.stack(square, axis=1)
    small = narrow[0, 0, 64:74].reshape(5, 2, d)
    bias = narrow[0, 1, 64:72].reshape(2, ff)
    terms = (small[0], small[1], square[1], square[2], square[3], square[0], small[2], small[3], jnp.stack(up), bias,
             jnp.stack(down), small[4])
    return tuple(scattered(term) for term in terms)


def on_device(
    inputs, cotangent, item_lengths, attn_gain, attn_bias, query_weight, key_weight, value_weight, output_weight,
    ffn_gain, ffn_bias, up_weight, up_bias, down_weight, down_bias,
):
    rows, width, depth = inputs.shape
    ff = up_weight.shape[2]
    group = SLOTS // width
    halving = lax.axis_size("dp") == 4 and lax.axis_size("seq") == SHARDS
    lengths = item_lengths.T
    clock = Clock()
    packed = pack(inputs, group)
    clock.done(packed[0])
    x_parts = swap(clock, packed[1:])
    cotangent = clock.after(cotangent)
    first = pack(cotangent, group)
    clock.done(first[0])
    cot_parts = swap(clock, first[1:])
    clock.done(clock.after(first[0]))
    norms = (attn_gain, attn_bias, ffn_gain, ffn_bias, up_bias, down_bias)
    wts = (query_weight, key_weight, value_weight, output_weight, up_weight, down_weight)
    x_parts, cot_parts = [packed[0]] + x_parts, [first[0]] + cot_parts
    kept0, h1 = forward_first(lengths, x_parts, norms, wts)
    kept1, wide1, dz1, ffn1 = forward_last(1, halving, lengths, h1, cot_parts, norms, wts)
    clock.done(ffn1)
    line = rows // group, group
    if halving:
        f1 = Chunk(clock, wide1)
    dg, do, dout, mid1 = back_top(1, lengths, cot_parts, kept1, clock.after(dz1), norms, wts)
    clock.done(mid1)
    if halving:
        advance(clock, [(f1, "split", PLANE_1)])
    wide0, (dh, dz0, dq, dk, dv, attn1, ffn0) = back_between(
        1, halving, lengths, clock.after(dg), do, kept1, kept0, norms, wts, *line)
    clock.done(attn1)
    if halving:
        f0 = Chunk(clock, wide0)
    if halving:
        advance(clock, [(f1, "close", None)], LONG)
    part = square_halves(halving, clock.after(kept1[0]), (dq, dk, dv), dout)
    clock.done(part[0])
    if halving:
        a1 = Chunk(clock, part)
        advance(clock, [(f1, "split", PLANE_2), (f0, "split", PLANE_2)])
        advance(clock, [(a1, "split", LINE_1)])
    narrow, parts = back_bottom(
        halving, lengths, clock.after(dh), dz0, (attn1, mid1, ffn0, ffn1), kept0, norms, wts, width, group)
    clock.done(parts[0])
    if halving:
        a0 = Chunk(clock, narrow)
        advance(clock, [(f1, "split", LINE_1), (a1, "split", LINE_2)], LONG)
        advance(clock, [(f0, "split", PLANE_1), (a0, "split", PLANE_1)])
    both = results(1, kept1, norms, wts, clock.after(parts))
    clock.done(both[0])
    if halving:
        advance(clock, [(a0, "split", PLANE_2), (a1, "whole", PLANE_2), (f0, "split", LINE_1), (f1, "split", LINE_2)])
        advance(clock, [(f1, "gather", PLANE_1), (a1, "whole", PLANE_1), (a0, "split", LINE_1), (f0, "split", LINE_2)])
    mine = swap(clock, both[1:])
    if halving:
        advance(clock, [(f1, "gather", PLANE_2), (f0, "gather", PLANE_2), (a0, "split", LINE_2), (a1, "close", None)], FIVE)
        clock.done(mine[0])
        advance(clock, [(f0, "gather", PLANE_1), (a0, "spread", (PLANE_1, PLANE_2, PLANE_3)), (f1, "order", (PLANE_1, PLANE_2))], SIX)
    own = clock.after(both[0])
    if not halving:
        output, input_grad = unpack([own] + mine)
        return (output, input_grad) + plain_sums(wide0, wide1, part, narrow, depth, ff)

    do, dq, dk, dv, ag, ab, fg, fb, bd, bu = finish_last(clock.after(a0.kept), a0.all, a1.kept, depth)
    clock.done(do)
    advance(clock, [(f0, "order", (PLANE_2, PLANE_1))])
    wide0, wide1 = [c.kept.reshape(4, -1, depth) for c in (f0, f1)]
    down, up = finish_wide(clock.after(wide0), wide1, depth, ff)
    clock.done(down)
    output, input_grad = unpack([clock.after(own)] + mine)
    return output, input_grad, ag, ab, dq, dk, dv, do, fg, fb, up, bu, down, bd


def solution(mesh):
    spec = jax.sharding.PartitionSpec
    whole, split = spec(), spec("dp", "seq", None)
    vec, mat = spec(None, "seq"), spec(None, "seq", None)
    return jax.shard_map(
        on_device,
        mesh=mesh,
        in_specs=(split, split, spec("dp", None)) + (whole,) * 12,
        out_specs=(split, split, vec, vec, mat, mat, mat, mat, vec, vec, mat, vec, mat, vec),
        check_vma=False,
    )
```

```python
import jax
import jax.numpy as jnp
from jax import lax
from jax.experimental import pallas as pl
from jax.experimental.pallas import tpu as pltpu

H = 8
SLOTS = 256
EPS = 1e-05
NEG = -1000000000.0
BF = jnp.bfloat16
F32 = jnp.float32
GELU_C = 0.7978845608028654
GELU_A = 0.044715
STEP = 512
SHARDS = 8
LONG = 30_000_000_000
FIVE = 0
SIX = 0
SECOND = slice(128, 192)

NN = (((1,), (0,)), ((), ()))
NT = (((1,), (1,)), ((), ()))
TN = (((0,), (0,)), ((), ()))

SDS = jax.ShapeDtypeStruct
IN_VMEM = pl.BlockSpec(memory_space=pltpu.VMEM)
IN_SMEM = pl.BlockSpec(memory_space=pltpu.SMEM)


def dot(left, right, form=NN):
    return lax.dot_general(left, right, form, preferred_element_type=F32)


def normalize(values):
    centered = values - jnp.mean(values, axis=-1, keepdims=True)
    inv = lax.rsqrt(jnp.mean(centered * centered, axis=-1, keepdims=True) + EPS)
    return centered * inv, inv


def norm_back(dy, values, gain):
    xhat, inv = normalize(values)
    dgain = jnp.sum(dy * xhat, axis=0, keepdims=True)
    dbias = jnp.sum(dy, axis=0, keepdims=True)
    dx = dy * gain
    dx = inv * (dx - jnp.mean(dx, axis=-1, keepdims=True) - xhat * jnp.mean(dx * xhat, axis=-1, keepdims=True))
    return dx, dgain, dbias


def head_masks(width):
    lane = lax.broadcasted_iota(jnp.int32, (1, 2 * width), 1)
    low = (lane < width).astype(F32).astype(BF)
    return low, (1.0 - low.astype(F32)).astype(BF)


def tiles(m):
    return [slice(SLOTS * i, SLOTS * (i + 1)) for i in range(m // SLOTS)]


def call(body, name, operands, outs, scratch, limit, flops, moved):
    return pl.pallas_call(
        body,
        in_specs=[IN_SMEM if x.dtype == jnp.int32 else IN_VMEM for x in operands],
        out_specs=[IN_VMEM] * len(outs),
        out_shape=[SDS(*out) for out in outs],
        scratch_shapes=[pltpu.VMEM(*x) for x in scratch],
        compiler_params=pltpu.CompilerParams(vmem_limit_bytes=limit << 20),
        cost_estimate=pl.CostEstimate(flops=flops, bytes_accessed=moved, transcendentals=0),
        name=name,
    )(*operands)


def member_of(group):
    return lax.axis_index("seq") % group


def lengths_of(lengths, units, group):
    seq = lax.axis_index("seq")
    return [lengths[seq // group, (seq % group) * units + u] for u in range(units)]


def pack(local, group):
    rows, width, depth = local.shape
    n = rows // group

    def body(x_ref, *outs):
        for d, out in enumerate(outs):
            out[...] = x_ref[pl.ds((member_of(group) ^ d) * n, n)]

    return call(body, "pack", [local], [((n, width, depth), local.dtype)] * group, [], 4, 20_000_000_000, 1 << 20)


def unpack(pieces):
    _, n, width, depth = pieces[0].shape

    def body(*refs):
        outs = refs[-2:]
        for d, ref in enumerate(refs[:-2]):
            for t in range(2):
                outs[t][pl.ds((member_of(len(pieces)) ^ d) * n, n)] = ref[t]

    return call(body, "unpack", pieces, [((n * len(pieces), width, depth), BF)] * 2, [], 4, 0, 1 << 20)


def regroup(lens, pieces, put):
    n, width, _ = pieces[0].shape
    j = member_of(len(pieces))
    for d, piece in enumerate(pieces):
        for u in range(n):
            start = (j ^ d) * width
            at = pl.ds(pl.multiple_of(u * SLOTS + start, width), width)
            block = piece[u]
            if lens is not None:
                slot = lax.broadcasted_iota(jnp.int32, (width, 1), 0) + start
                block = jnp.where(slot < lens[u], block.astype(F32), 0.0)
            put(at, block)


def deal(values, pieces):
    for d, piece in enumerate(pieces):
        n, width, _ = piece.shape
        for u in range(n):
            at = pl.ds(pl.multiple_of(u * SLOTS + (member_of(len(pieces)) ^ d) * width, width), width)
            piece[u] = values[at, :].astype(BF)


def stacked(head):
    return slice(SLOTS * (head % 2), SLOTS * (head % 2) + SLOTS)


def apart(pair, masks):
    return jnp.concatenate([pair * masks[0], pair * masks[1]], axis=0)


def pair_scratch(m):
    return ((m // SLOTS * (H // 2), 2 * SLOTS, SLOTS), BF)


def forward_attention(lens, h, gain, bias, wq, wk, wv, a_ref, q_ref, k_ref, v_ref, o_ref, lse_ref, p_ref):
    masks = head_masks(64)
    for i, rows in enumerate(tiles(h.shape[0])):
        xhat, _ = normalize(h[rows, :].astype(F32))
        a = (xhat * gain + bias).astype(BF)
        a_ref[rows, :] = a
        q_ref[rows, :] = (dot(a, wq[...]).astype(BF).astype(F32) * 0.125).astype(BF)
        k_ref[rows, :] = dot(a, wk[...]).astype(BF)
        v_ref[rows, :] = dot(a, wv[...]).astype(BF)
    key = lax.broadcasted_iota(jnp.int32, (SLOTS, 1), 0)
    for i, rows in enumerate(tiles(h.shape[0])):
        valid = key < lens[i]
        for head in range(H):
            cols = slice(128 * (head // 2), 128 * (head // 2) + 128)
            st = jnp.where(valid, dot(k_ref[rows, cols] * masks[head % 2], q_ref[rows, cols], NT), NEG)
            top = jnp.max(st, axis=0, keepdims=True)
            e = jnp.exp(st - top)
            tot = jnp.sum(e, axis=0, keepdims=True)
            p_ref[i * (H // 2) + head // 2, stacked(head), :] = (e * (1.0 / tot)).astype(BF)
            lse_ref[i * H + head, :] = (top + jnp.log(tot))[0]
    for i, rows in enumerate(tiles(h.shape[0])):
        for pair in range(H // 2):
            cols = slice(128 * pair, 128 * pair + 128)
            o_ref[rows, cols] = dot(p_ref[i * (H // 2) + pair], apart(v_ref[rows, cols], masks), TN).astype(BF)


def forward_ffn(h, o, wo, gain, bias, wup, bup, wdown, bdown, g_ref, c_ref, u_ref, gp_ref, n_ref):
    m, ff = h.shape[0], wup.shape[1]
    for rows in tiles(m):
        g = h[rows, :].astype(F32) + dot(o[rows, :], wo[...])
        g_ref[rows, :] = g
        xhat, _ = normalize(g)
        c_ref[rows, :] = (xhat * gain + bias).astype(BF)
    for f in range(0, ff, 256):
        fs = slice(f, f + 256)
        for rows in tiles(m):
            z = dot(c_ref[rows, :], wup[:, fs]) + bup[:, fs]
            z2 = z * z
            t = jnp.tanh(z * (GELU_C + GELU_C * GELU_A * z2))
            half = 0.5 + 0.5 * t
            gp = half + (0.5 * z) * (1.0 - t * t) * (GELU_C + 3.0 * GELU_C * GELU_A * z2)
            u_ref[rows, fs] = (z * half).astype(BF)
            gp_ref[rows, fs] = gp.astype(BF)
    if n_ref is not None:
        layer_output(g_ref, u_ref, wdown, bdown, n_ref)


def layer_output(g_ref, u_ref, wdown, bdown, n_ref):
    for rows in tiles(g_ref.shape[0]):
        n_ref[rows, :] = g_ref[rows, :] + (dot(u_ref[rows, :], wdown[...]) + bdown)


def store(core, keep, send, quarter, z, rows, cols, even, odd):
    mine, other = jnp.where(core == 0, even, odd), jnp.where(core == 0, odd, even)
    at = 2 * (z % 2) + z // 2
    keep[quarter, at, rows, cols] = mine
    send[quarter, at, rows, cols] = other


def ffn_terms(core, dm_ref, u_ref, gp_ref, c_ref, wdown, keep, send, dz_ref, sm_ref):
    ff = u_ref.shape[1]
    dm = dm_ref[...]
    for f in range(ff // STEP):
        res = dot(dm, u_ref[:, STEP * f : STEP * f + STEP], TN).astype(BF).reshape(4, 128, STEP)
        store(core, keep, send, slice(None), f, slice(0, 128), slice(0, 256), res[:, :, 0:256], res[:, :, 256:512])
    sm_ref[...] = jnp.zeros_like(sm_ref)
    sm_ref[0:1, :] = jnp.sum(dm.astype(F32), axis=0, keepdims=True)
    for f in range(ff // STEP):
        fs = slice(STEP * f, STEP * f + STEP)
        dz = (dot(dm, wdown[fs, :], NT) * gp_ref[:, fs].astype(F32)).astype(BF)
        dz_ref[:, fs] = dz
        sm_ref[1 + f : 2 + f, :] = jnp.sum(dz.astype(F32), axis=0, keepdims=True)
        res = dot(c_ref[...], dz, TN).astype(BF).reshape(4, 128, STEP)
        for t in range(2):
            rows, part = slice(64 * t, 64 * t + 64), res[:, :, 256 * t : 256 * t + 256]
            for z in range(4):
                store(core, keep, send, f, z, rows, slice(256, 512), part[z, 0:64], part[z, 64:128])


KEPT = ("a", "q", "k", "v", "o", "lse", "g", "c", "u", "gp")


def kept_shapes(m, d, ff):
    wide, narrow = (m, ff), (m, d)
    return [(narrow, BF)] * 5 + [((m // SLOTS * H, SLOTS), F32), (narrow, F32), (narrow, BF), (wide, BF), (wide, BF)]


def row(ref, l):
    return ref[l : l + 1, :].astype(F32)


def forward_layer(l, lens, h, norms, wts, kept, last, p_ref):
    ag, ab, fg, fb, bup, bdown = norms
    wq, wk, wv, wo, wup, wdown = [w.at[l] for w in wts]
    a, q, k, v, o, lse, g, c, u, gp = kept
    forward_attention(lens, h, row(ag, l), row(ab, l), wq, wk, wv, a, q, k, v, o, lse, p_ref)
    forward_ffn(h, o, wo, row(fg, l), row(fb, l), wup, row(bup, l), wdown, row(bdown, l), g, c, u, gp, last)


def chunk_shape(rows):
    return ((4, SHARDS // 2, rows, 512), BF)


def parity(halving):
    return lax.axis_index("seq") % 2 if halving else 0


def forward_first(lengths, parts, norms, wts):
    _, d, ff = wts[4].shape
    n, width, _ = parts[0].shape
    group = len(parts)
    m = n * group * width

    def body(*refs):
        lengths, refs = refs[0], refs[1:]
        parts, refs = refs[:group], refs[group:]
        norms, wts, kept, (x_ref, last, p_ref) = refs[:6], refs[6:12], refs[12:22], refs[22:]

        def put(at, block):
            x_ref[at, :] = block

        regroup(None, parts, put)
        forward_layer(0, lengths_of(lengths, n, group), x_ref, norms, wts, kept, last, p_ref)

    outs = kept_shapes(m, d, ff) + [((m, d), BF), ((m, d), F32)]
    res = call(body, "forward_first", [lengths, *parts, *norms, *wts], outs, [pair_scratch(m)], 4, 2 * m * (4 * d * d + 2 * d * ff), 24 << 20)
    return res[:11], res[11]


def forward_last(l, halving, lengths, h, parts, norms, wts):
    _, d, ff = wts[4].shape
    n, width, _ = parts[0].shape
    group = len(parts)
    m = n * group * width
    per = kept_shapes(m, d, ff)

    def body(*refs):
        lengths, h = refs[:2]
        refs = refs[2:]
        parts, refs = refs[:group], refs[group:]
        norms, wts, refs = refs[:6], refs[6:12], refs[12:]
        kept, refs = refs[:8], refs[8:]
        keep, send, dz_ref, sm_ref, c, gp, dm_ref, p_ref = refs
        lens = lengths_of(lengths, n, group)

        def put(at, block):
            dm_ref[at, :] = block.astype(BF)

        regroup(lens, parts, put)
        forward_layer(l, lens, h, norms, wts, [*kept[:7], c, kept[7], gp], None, p_ref)
        ffn_terms(parity(halving), dm_ref, kept[7], gp, c, wts[5].at[l], keep, send, dz_ref, sm_ref)

    outs = per[:7] + [per[8]] + [chunk_shape(128)] * 2 + [((m, ff), BF), ((8, d), F32)]
    *kept, keep, send, dz, sums = call(
        body, "forward_last", [lengths, h, *parts, *norms, *wts], outs,
        [per[7], per[9], ((m, d), BF), pair_scratch(m)], 20, 2 * m * (4 * d * d + 4 * d * ff), 24 << 20)
    return kept[:7] + [None, kept[7], None, h], (keep, send), dz, sums


def mid_terms(l, dh_ref, g, o, dz, gain, wup, wo, dg_ref, do_ref, dr_ref, sm_ref):
    m, d = g.shape
    dgain = dbias = None
    for i, rows in enumerate(tiles(m)):
        dc = dot(dz[rows, :], wup[l], NT)
        dx, dg1, db1 = norm_back(dc, g[rows, :], row(gain, l))
        dg = dh_ref[rows, :] + dx
        dg_ref[rows, :] = dg
        dr_ref[rows, :] = dg.astype(BF)
        dgain, dbias = (dg1, db1) if i == 0 else (dgain + dg1, dbias + db1)
    sm_ref[...] = jnp.zeros_like(sm_ref)
    sm_ref[0:1, :] = dgain
    sm_ref[1:2, :] = dbias
    do_ref[...] = dot(dr_ref[...], wo[l], NT).astype(BF)
    return dot(o[...], dr_ref[...], TN).astype(BF).reshape(SHARDS // 2, 2, d // SHARDS, d)


def attn_terms(l, lens, dg, do, lse, q, k, v, h, gain, wq, wk, wv, dq_ref, dk_ref, dv_ref, p_ref, s_ref, put):
    m, d = dg.shape
    masks = head_masks(64)
    low = lax.broadcasted_iota(jnp.int32, (1, 128), 1) < 64
    key = lax.broadcasted_iota(jnp.int32, (SLOTS, 1), 0)
    for i, rows in enumerate(tiles(m)):
        valid = key < lens[i]
        for head in range(H):
            cols, n, mk = slice(128 * (head // 2), 128 * (head // 2) + 128), i * (H // 2) + head // 2, masks[head % 2]
            st = jnp.where(valid, dot(k[rows, cols] * mk, q[rows, cols], NT), NEG)
            pt = jnp.exp(st - lse[i * H + head, :][None, :])
            dpt = dot(v[rows, cols] * mk, do[rows, cols], NT)
            delta = jnp.sum(pt * dpt, axis=0, keepdims=True)
            p_ref[n, stacked(head), :] = pt.astype(BF)
            s_ref[n, stacked(head), :] = (pt * (dpt - delta)).astype(BF)
    for i, rows in enumerate(tiles(m)):
        for pair in range(H // 2):
            cols, n = slice(128 * pair, 128 * pair + 128), i * (H // 2) + pair
            dq_ref[rows, cols] = (dot(s_ref[n], apart(k[rows, cols], masks), TN) * 0.125).astype(BF)
            both = dot(s_ref[n], q[rows, cols])
            dk_ref[rows, cols] = jnp.where(low, both[0:SLOTS], both[SLOTS:]).astype(BF)
            both = dot(p_ref[n], do[rows, cols])
            dv_ref[rows, cols] = jnp.where(low, both[0:SLOTS], both[SLOTS:]).astype(BF)
    dgain = dbias = None
    for i, rows in enumerate(tiles(m)):
        da = dot(dq_ref[rows, :], wq[l], NT) + dot(dk_ref[rows, :], wk[l], NT) + dot(dv_ref[rows, :], wv[l], NT)
        dx, dg1, db1 = norm_back(da, h[rows, :].astype(F32), row(gain, l))
        put(rows, dg[rows, :] + dx)
        dgain, dbias = (dg1, db1) if i == 0 else (dgain + dg1, dbias + db1)
    return dgain, dbias


def square_terms(a, *grads):
    d = a.shape[1]
    return [dot(a[...], ref[...], TN).astype(BF).reshape(SHARDS // 2, 2, d // SHARDS, d) for ref in grads]


def back_top(l, lengths, parts, kept, dz, norms, wts):
    g, o = kept[6], kept[4]
    m, d = g.shape
    group = len(parts)

    def body(lengths, *refs):
        parts, refs = refs[:group], refs[group:]
        g, o, dz, gain, wup, wo, dg_ref, do_ref, dout_ref, sm_ref, dr_ref, dh_ref = refs

        def put(at, block):
            dh_ref[at, :] = block

        regroup(lengths_of(lengths, m // SLOTS, group), parts, put)
        dout_ref[...] = mid_terms(l, dh_ref, g, o, dz, gain, wup, wo, dg_ref, do_ref, dr_ref, sm_ref)

    outs = [((m, d), F32), ((m, d), BF), ((SHARDS // 2, 2, d // SHARDS, d), BF), ((8, d), F32)]
    return call(body, "back_top", [lengths, *parts, g, o, dz, norms[2], wts[4], wts[3]], outs, [((m, d), BF), ((m, d), F32)], 6,
                2 * m * 6 * d * d, 9 << 20)


def back_between(l, halving, lengths, dg, do, kept, under, norms, wts, units, group):
    a, q, k, v, o, lse, g, c, u, gp, h = kept
    c, u, gp = under[7:10]
    m, d = dg.shape
    ff = u.shape[1]

    def body(lengths, dg, do, lse, q, k, v, h, gain, wq, wk, wv, c, u, gp, wdown,
             keep0, send0, dh_ref, dz_ref, dq_ref, dk_ref, dv_ref, sm_ref, sm0_ref, dm_ref, p_ref, s_ref):
        core, lens = parity(halving), lengths_of(lengths, units, group)

        def put(rows, dh):
            dh_ref[rows, :] = dh
            dm_ref[rows, :] = dh.astype(BF)

        dgain, dbias = attn_terms(l, lens, dg, do, lse, q, k, v, h, gain, wq, wk, wv, dq_ref, dk_ref, dv_ref, p_ref, s_ref, put)
        sm_ref[...] = jnp.zeros_like(sm_ref)
        sm_ref[0:1, :] = dgain
        sm_ref[1:2, :] = dbias
        ffn_terms(core, dm_ref, u, gp, c, wdown.at[l - 1], keep0, send0, dz_ref, sm0_ref)

    outs = [chunk_shape(128)] * 2 + [((m, d), F32), ((m, ff), BF)] + [((m, d), BF)] * 3 + [((8, d), F32)] * 2
    keep0, send0, *rest = call(
        body, "back_between", [lengths, dg, do, lse, q, k, v, h, norms[0], *wts[:3], c, u, gp, wts[5]], outs,
        [((m, d), BF), pair_scratch(m), pair_scratch(m)], 9, 2 * m * 19 * d * d, 20 << 20)
    return (keep0, send0), rest


def square_halves(halving, a, grads, dout):
    d = a.shape[1]

    def body(a, dq, dk, dv, dout, keep, send):
        core = parity(halving)
        for n, term in enumerate([dout[...], *square_terms(a, dq, dk, dv)]):
            for z in range(SHARDS // 2):
                at, rows = 2 * (z % 2) + z // 2, slice(64 * n, 64 * n + 64)
                keep[at, rows, :] = jnp.where(core == 0, term[z, 0], term[z, 1])
                send[at, rows, :] = jnp.where(core == 0, term[z, 1], term[z, 0])

    outs = [((SHARDS // 2, 256, d), BF)] * 2
    return call(body, "square_halves", [a, *grads, dout], outs, [], 4, 2 * a.shape[0] * 3 * d * d, 4 << 20)


def back_bottom(halving, lengths, dh, dz, smalls, kept, norms, wts, width, group):
    a, q, k, v, o, lse, g, c, u, gp, h = kept
    m, d = dh.shape
    units = m // SLOTS

    def body(lengths, dh, g, o, dz, fgain, wup, wo, lse, q, k, v, a, h, gain, wq, wk, wv, attn1, mid1, ffn0, ffn1, keep, send, *refs):
        outs, refs = refs[:group], refs[group:]
        dg, do, dr, mid0, dq_ref, dk_ref, dv_ref, dx_ref, p_ref, s_ref = refs
        core, lens = parity(halving), lengths_of(lengths, units, group)
        first = mid_terms(0, dh, g, o, dz, fgain, wup, wo, dg, do, dr, mid0)
        for z in range(SHARDS // 2):
            store(core, keep, send, 0, z, slice(0, 64), slice(None), first[z, 0], first[z, 1])

        def put(rows, value):
            dx_ref[rows, :] = value

        dgain, dbias = attn_terms(0, lens, dg, do, lse, q, k, v, h, gain, wq, wk, wv, dq_ref, dk_ref, dv_ref, p_ref, s_ref, put)
        for n, term in enumerate(square_terms(a, dq_ref, dk_ref, dv_ref)):
            for z in range(SHARDS // 2):
                store(core, keep, send, n + 1, z, slice(0, 64), slice(None), term[z, 0], term[z, 1])
        lines = [dgain, attn1[0:1, :], dbias, attn1[1:2, :], mid0[0:1, :], mid1[0:1, :], mid0[1:2, :], mid1[1:2, :],
                 ffn0[0:1, :], ffn1[0:1, :]]
        zero = jnp.zeros((1, d), F32)
        block = jnp.concatenate(lines + [zero] * 6, axis=0).astype(BF)
        other = jnp.concatenate([ffn0[1:5, :], ffn1[1:5, :]] + [zero] * 8, axis=0).astype(BF)
        for half in (keep, send):
            for at in range(SHARDS // 2):
                half[0, at, 64:80, :] = block
                half[1, at, 64:80, :] = other
                for t in (2, 3):
                    half[t, at, 64:80, :] = jnp.zeros((16, d), BF)
        deal(dx_ref, outs)

    outs = [chunk_shape(80)] * 2 + [((units, width, d), BF)] * group
    wide, narrow = ((m, d), F32), ((m, d), BF)
    keep, send, *parts = call(
        body, "back_bottom",
        [lengths, dh, g, o, dz, norms[2], wts[4], wts[3], lse, q, k, v, a, h, norms[0], *wts[:3], *smalls], outs,
        [wide, narrow, narrow, ((8, d), F32), narrow, narrow, narrow, wide, pair_scratch(m), pair_scratch(m)], 12, 2 * m * 16 * d * d, 20 << 20)
    return (keep, send), parts


def results(l, kept, norms, wts, parts):
    g, u = kept[6], kept[8]
    group = len(parts)
    shape = (2,) + parts[0].shape

    def body(g, u, wdown, bdown, *refs):
        last = refs[-1]
        layer_output(g, u, wdown.at[l], row(bdown, l), last)
        outs = refs[group : 2 * group]
        deal(last, [out.at[0] for out in outs])
        for part, out in zip(refs[:group], outs):
            out[1] = part[...]

    return call(body, "results", [g, u, wts[5], norms[5], *parts], [(shape, BF)] * group, [(g.shape, F32)], 8,
                2 * u.shape[0] * u.shape[1] * g.shape[1], 4 << 20)


def finish_wide(wide0, wide1, d, ff):
    def body(w0, w1, down, up):
        for l, ref in enumerate((w0, w1)):
            for n in range(4):
                part = ref[n].astype(F32)
                down[l, :, 128 * n : 128 * n + 128] = part[:, 0:256].T
                for t in range(2):
                    at = 512 * n + 256 * t
                    up[l, :, at : at + 256] = part[64 * t : 64 * t + 64, 256:512]

    return call(body, "finish_wide", [wide0, wide1], [((2, 256, d), F32), ((2, 64, ff), F32)], [], 8, 0, 1024)


def finish_last(own, others, square, d):
    rows = own.shape[0]
    offsets = [first for _, first in others]

    def body(own, *refs):
        parts, other = [(own, 0), *zip(refs[:3], offsets)], refs[3]
        outs = refs[4:8]
        ag, ab, fg, fb, bd, bu, x, vsm = refs[8:]
        here = 2 * bit_of(PLANE_1) + bit_of(PLANE_2)
        for (ref, first), flip in zip(parts, (0, 2, 1, 3)):
            x[here ^ flip] = ref[first : first + rows, :]
        for n in range(4):
            outs[n][0] = x[n, 0:64, :].astype(F32)
            outs[n][1] = other[64 * n : 64 * n + 64, :].astype(F32)
        s = lax.axis_index("seq")
        vsm[...] = x[0:2, 64:80, :].astype(F32)
        pair = vsm[0, :, pl.ds(pl.multiple_of((s // 2) * 128, 128), 128)]
        mine = jnp.where(s % 2 == 0, pair[:, 0:64], pair[:, 64:128])
        for n, ref in enumerate((ag, ab, fg, fb, bd)):
            ref[...] = mine[2 * n : 2 * n + 2, :]
        for l in range(2):
            bu[l : l + 1, :] = vsm[1, pl.ds(4 * l + s // 2, 1), pl.ds(pl.multiple_of((s % 2) * 256, 256), 256)]

    outs = [((2, 64, d), F32)] * 4 + [((2, 64), F32)] * 5 + [((2, 256), F32)]
    return call(body, "finish_last", [own, *[array for array, _ in others], square], outs, [((4, rows, d), BF), ((2, 16, d), F32)], 8, 0, 2 << 20)


def swap(clock, sends):
    size = lax.axis_size("seq")
    out = [None] * len(sends)
    for d, s in enumerate(sends):
        clock.send(s, [(i, i ^ (d + 1)) for i in range(size)], "seq", lambda value, d=d: out.__setitem__(d, value))
    return out


BOTH = ("dp", "seq")


def pairs_of(flip):
    out = []
    for y in range(2):
        for x in range(2):
            for z in range(4):
                for c in range(2):
                    y2, x2, z2, c2 = flip(y, x, z, c)
                    out.append((y * 16 + x * 8 + z * 2 + c, y2 * 16 + x2 * 8 + z2 * 2 + c2))
    return out


CORE = pairs_of(lambda y, x, z, c: (y, x, z, 1 - c))
PLANE_1 = pairs_of(lambda y, x, z, c: (y, 1 - x, z, c) if c == 0 else (1 - y, x, z, c))
PLANE_2 = pairs_of(lambda y, x, z, c: (y, 1 - x, z, c) if c == 1 else (1 - y, x, z, c))
PLANE_3 = pairs_of(lambda y, x, z, c: (1 - y, 1 - x, z, c))
LINE_1 = pairs_of(lambda y, x, z, c: (y, x, z ^ 1, c))
LINE_2 = pairs_of(lambda y, x, z, c: (y, x, z ^ 2, c))


def bit_of(pairs):
    dp, seq = lax.axis_index("dp"), lax.axis_index("seq")
    if pairs is LINE_1:
        return (seq // 2) % 2
    if pairs is LINE_2:
        return seq // 4
    y, x = dp // 2, dp % 2
    return jnp.where((seq % 2 == 0) == (pairs is PLANE_1), x, y)


class Clock:
    def __init__(self):
        self.last, self.waiting = None, []

    def done(self, value):
        self.last = value

    def send(self, value, pairs, axes, arrived):
        self.waiting.append((value, pairs, axes, arrived))

    def after(self, value):
        waiting, self.waiting = self.waiting, []
        value, last, sent = lax.optimization_barrier((value, self.last, [w[0] for w in waiting]))
        for v, (_, pairs, axes, arrived) in zip(sent, waiting):
            arrived(lax.ppermute(v, axes, pairs))
        return value


class Chunk:
    def __init__(self, clock, halves):
        self.kept = halves[0].reshape(-1, halves[0].shape[-1])
        self.moved, self.paired, self.all = None, False, []
        clock.send(halves[1].reshape(self.kept.shape), CORE, BOTH, lambda value: self.arrived(value, 0))

    def arrived(self, value, first):
        self.moved = (value, first)
        self.all.append(self.moved)


BLOCK = 256


def blocks(count):
    return [(start, min(BLOCK, count - start)) for start in range(0, count, BLOCK)]


def advance(clock, items, weight=0):
    for (chunk, _, _), kept in zip(items, clock.after([chunk.kept for chunk, _, _ in items])):
        chunk.kept = kept
    arrays, lanes, keeps, plan = [], {}, [], []

    def index(array):
        for n, other in enumerate(arrays):
            if other is array:
                return n
        arrays.append(array)
        return len(arrays) - 1

    for chunk, kind, pairs in items:
        rows = chunk.kept.shape[0]
        now = 2 * rows if chunk.paired else rows
        left = rows // 2 if kind == "split" else now
        lane = []
        for each in pairs if kind == "spread" else (pairs,) if kind in ("split", "whole", "gather") else ():
            key = [n for n in lanes if lanes[n][0] is each]
            name = key[0] if key else len(lanes)
            first = lanes[name][1] if key else 0
            lane.append((name, first))
            lanes[name] = (each, first + left)
        at, by, offset = index(chunk.kept), None, 0
        if chunk.moved:
            by, offset = index(chunk.moved[0]), chunk.moved[1]
        plan.append((kind, pairs, at, by, offset, rows, chunk.paired, lane))
        keeps.append(left)
    count = len(lanes)

    def body(*refs):
        ins, outs = refs[: len(arrays)], refs[len(arrays) :]
        for n, (kind, pairs, at, by, offset, rows, paired, lane) in enumerate(plan):
            kept, moved, left = ins[at], None if by is None else ins[by], outs[count + n]
            sent, start = (outs[lane[0][0]], lane[0][1]) if lane else (None, 0)

            def summed(low, size):
                if isinstance(low, int):
                    first, second = slice(low, low + size), slice(offset + low, offset + low + size)
                else:
                    first = pl.ds(pl.multiple_of(low, 16), size)
                    second = pl.ds(pl.multiple_of(offset + low, 16), size)
                if moved is None:
                    return kept[first, :]
                return (kept[first, :].astype(F32) + moved[second, :].astype(F32)).astype(BF)

            if kind == "split":
                half = rows // 2
                bit = bit_of(pairs)
                for low, size in blocks(half):
                    sent[start + low : start + low + size, :] = summed((1 - bit) * half + low, size)
                    left[low : low + size, :] = summed(bit * half + low, size)
            elif kind == "order":
                part = rows // 2
                own = 2 * bit_of(pairs[0]) + bit_of(pairs[1])
                for m, flip in enumerate((0, 2, 1, 3)):
                    source, base = (kept, 0) if m < 2 else (moved, offset)
                    base += (m % 2) * part
                    left[pl.ds(pl.multiple_of((own ^ flip) * part, 16), part), :] = source[base : base + part, :]
            elif paired:
                for low, size in blocks(rows):
                    for source, base, to in ((kept, low, low), (moved, offset + low, rows + low)):
                        value = source[base : base + size, :]
                        left[to : to + size, :] = value
                        sent[start + to : start + to + size, :] = value
            else:
                for low, size in blocks(rows):
                    value = summed(low, size)
                    left[low : low + size, :] = value
                    for name, to in lane:
                        outs[name][to + low : to + low + size, :] = value

    width = items[0][0].kept.shape[1]
    sizes = [lanes[n][1] for n in range(count)] + keeps
    results = call(body, "advance", arrays, [((rows, width), BF) for rows in sizes], [], 4, weight, 1 << 20)
    clock.done(results[0])
    for n in range(count):
        here = [(item[0], to) for item, spec in zip(items, plan) for name, to in spec[-1] if name == n]

        def arrived(value, here=here):
            for chunk, first in here:
                chunk.arrived(value, first)

        clock.send(results[n], lanes[n][0], BOTH, arrived)
    for (chunk, kind, _), kept in zip(items, results[count:]):
        chunk.kept, chunk.moved, chunk.all = kept, None, []
        chunk.paired = kind == "gather"


def scattered(term):
    share = lax.psum_scatter(term.astype(F32), "seq", scatter_dimension=1, tiled=True)
    return lax.psum(share.astype(BF), "dp").astype(F32)


def joined(halves, z_first=False):
    width = halves[0].shape[-1]
    if z_first:
        shards = jnp.stack([half.reshape(2, 2, 4, -1, width) for half in halves]).transpose(2, 1, 0, 3, 4, 5)
    else:
        shards = jnp.stack([half.reshape(4, 2, 2, -1, width) for half in halves]).transpose(3, 2, 0, 1, 4, 5)
    return shards.reshape((SHARDS,) + shards.shape[3:])


def plain_sums(wide0, wide1, part, narrow, d, ff):
    part, narrow = joined(part, True), joined(narrow)
    down, up, square = [], [], []
    for wide, terms in ((wide0, narrow[:, :, :64]), (wide1, part)):
        wide = joined(wide).reshape(SHARDS, 512, 512)
        down.append(wide[:, :, :256].transpose(0, 2, 1).reshape(ff, d))
        up.append(wide[:, :, 256:].reshape(SHARDS, ff // 256, d // SHARDS, 256).transpose(0, 2, 1, 3).reshape(d, ff))
        square.append(terms.transpose(1, 0, 2, 3).reshape(4, d, d))
    square = jnp.stack(square, axis=1)
    small = narrow[0, 0, 64:74].reshape(5, 2, d)
    bias = narrow[0, 1, 64:72].reshape(2, ff)
    terms = (small[0], small[1], square[1], square[2], square[3], square[0], small[2], small[3], jnp.stack(up), bias,
             jnp.stack(down), small[4])
    return tuple(scattered(term) for term in terms)


def on_device(
    inputs, cotangent, item_lengths, attn_gain, attn_bias, query_weight, key_weight, value_weight, output_weight,
    ffn_gain, ffn_bias, up_weight, up_bias, down_weight, down_bias,
):
    rows, width, depth = inputs.shape
    ff = up_weight.shape[2]
    group = SLOTS // width
    halving = lax.axis_size("dp") == 4 and lax.axis_size("seq") == SHARDS
    lengths = item_lengths.T
    clock = Clock()
    packed = pack(inputs, group)
    clock.done(packed[0])
    x_parts = swap(clock, packed[1:])
    cotangent = clock.after(cotangent)
    first = pack(cotangent, group)
    clock.done(first[0])
    cot_parts = swap(clock, first[1:])
    clock.done(clock.after(first[0]))
    norms = (attn_gain, attn_bias, ffn_gain, ffn_bias, up_bias, down_bias)
    wts = (query_weight, key_weight, value_weight, output_weight, up_weight, down_weight)
    x_parts, cot_parts = [packed[0]] + x_parts, [first[0]] + cot_parts
    kept0, h1 = forward_first(lengths, x_parts, norms, wts)
    kept1, wide1, dz1, ffn1 = forward_last(1, halving, lengths, h1, cot_parts, norms, wts)
    clock.done(ffn1)
    line = rows // group, group
    if halving:
        f1 = Chunk(clock, wide1)
    dg, do, dout, mid1 = back_top(1, lengths, cot_parts, kept1, clock.after(dz1), norms, wts)
    clock.done(mid1)
    if halving:
        advance(clock, [(f1, "split", PLANE_1)])
    wide0, (dh, dz0, dq, dk, dv, attn1, ffn0) = back_between(
        1, halving, lengths, clock.after(dg), do, kept1, kept0, norms, wts, *line)
    clock.done(attn1)
    if halving:
        f0 = Chunk(clock, wide0)
    if halving:
        advance(clock, [(f1, "close", None)], LONG)
    part = square_halves(halving, clock.after(kept1[0]), (dq, dk, dv), dout)
    clock.done(part[0])
    if halving:
        a1 = Chunk(clock, part)
        advance(clock, [(f1, "split", PLANE_2), (f0, "split", PLANE_2)])
        advance(clock, [(a1, "split", LINE_1)])
    narrow, parts = back_bottom(
        halving, lengths, clock.after(dh), dz0, (attn1, mid1, ffn0, ffn1), kept0, norms, wts, width, group)
    clock.done(parts[0])
    if halving:
        a0 = Chunk(clock, narrow)
        advance(clock, [(f1, "split", LINE_1), (a1, "split", LINE_2)], LONG)
        advance(clock, [(f0, "split", PLANE_1), (a0, "split", PLANE_1)])
    both = results(1, kept1, norms, wts, clock.after(parts))
    clock.done(both[0])
    if halving:
        advance(clock, [(a0, "split", PLANE_2), (a1, "whole", PLANE_2), (f0, "split", LINE_1), (f1, "split", LINE_2)])
        advance(clock, [(f1, "gather", PLANE_1), (a1, "whole", PLANE_1), (a0, "split", LINE_1), (f0, "split", LINE_2)])
    mine = swap(clock, both[1:])
    if halving:
        advance(clock, [(f1, "gather", PLANE_2), (f0, "gather", PLANE_2), (a0, "split", LINE_2), (a1, "close", None)], FIVE)
        clock.done(mine[0])
        advance(clock, [(f0, "gather", PLANE_1), (a0, "spread", (PLANE_1, PLANE_2, PLANE_3)), (f1, "order", (PLANE_1, PLANE_2))], SIX)
    own = clock.after(both[0])
    if not halving:
        output, input_grad = unpack([own] + mine)
        return (output, input_grad) + plain_sums(wide0, wide1, part, narrow, depth, ff)

    advance(clock, [(f0, "order", (PLANE_2, PLANE_1))])
    wide0, wide1 = [c.kept.reshape(4, -1, depth) for c in (f0, f1)]
    down, up = finish_wide(clock.after(wide0), wide1, depth, ff)
    clock.done(down)
    do, dq, dk, dv, ag, ab, fg, fb, bd, bu = finish_last(clock.after(a0.kept), a0.all, a1.kept, depth)
    clock.done(do)
    output, input_grad = unpack([clock.after(own)] + mine)
    return output, input_grad, ag, ab, dq, dk, dv, do, fg, fb, up, bu, down, bd


def solution(mesh):
    spec = jax.sharding.PartitionSpec
    whole, split = spec(), spec("dp", "seq", None)
    vec, mat = spec(None, "seq"), spec(None, "seq", None)
    return jax.shard_map(
        on_device,
        mesh=mesh,
        in_specs=(split, split, spec("dp", None)) + (whole,) * 12,
        out_specs=(split, split, vec, vec, mat, mat, mat, mat, vec, vec, mat, vec, mat, vec),
        check_vma=False,
    )
```

```python
import jax
import jax.numpy as jnp
from jax import lax
from jax.experimental import pallas as pl
from jax.experimental.pallas import tpu as pltpu

H = 8
SLOTS = 256
EPS = 1e-05
NEG = -1000000000.0
BF = jnp.bfloat16
F32 = jnp.float32
GELU_C = 0.7978845608028654
GELU_A = 0.044715
STEP = 512
SHARDS = 8
LONG = 30_000_000_000
FIVE = 0
SIX = 0
SECOND = slice(128, 192)

NN = (((1,), (0,)), ((), ()))
NT = (((1,), (1,)), ((), ()))
TN = (((0,), (0,)), ((), ()))

SDS = jax.ShapeDtypeStruct
IN_VMEM = pl.BlockSpec(memory_space=pltpu.VMEM)
IN_SMEM = pl.BlockSpec(memory_space=pltpu.SMEM)


def dot(left, right, form=NN):
    return lax.dot_general(left, right, form, preferred_element_type=F32)


def normalize(values):
    centered = values - jnp.mean(values, axis=-1, keepdims=True)
    inv = lax.rsqrt(jnp.mean(centered * centered, axis=-1, keepdims=True) + EPS)
    return centered * inv, inv


def norm_back(dy, values, gain):
    xhat, inv = normalize(values)
    dgain = jnp.sum(dy * xhat, axis=0, keepdims=True)
    dbias = jnp.sum(dy, axis=0, keepdims=True)
    dx = dy * gain
    dx = inv * (dx - jnp.mean(dx, axis=-1, keepdims=True) - xhat * jnp.mean(dx * xhat, axis=-1, keepdims=True))
    return dx, dgain, dbias


def head_masks(width):
    lane = lax.broadcasted_iota(jnp.int32, (1, 2 * width), 1)
    low = (lane < width).astype(F32).astype(BF)
    return low, (1.0 - low.astype(F32)).astype(BF)


def tiles(m):
    return [slice(SLOTS * i, SLOTS * (i + 1)) for i in range(m // SLOTS)]


def call(body, name, operands, outs, scratch, limit, flops, moved):
    return pl.pallas_call(
        body,
        in_specs=[IN_SMEM if x.dtype == jnp.int32 else IN_VMEM for x in operands],
        out_specs=[IN_VMEM] * len(outs),
        out_shape=[SDS(*out) for out in outs],
        scratch_shapes=[pltpu.VMEM(*x) for x in scratch],
        compiler_params=pltpu.CompilerParams(vmem_limit_bytes=limit << 20),
        cost_estimate=pl.CostEstimate(flops=flops, bytes_accessed=moved, transcendentals=0),
        name=name,
    )(*operands)


def member_of(group):
    return lax.axis_index("seq") % group


def lengths_of(lengths, units, group):
    seq = lax.axis_index("seq")
    return [lengths[seq // group, (seq % group) * units + u] for u in range(units)]


def pack(local, group):
    rows, width, depth = local.shape
    n = rows // group

    def body(x_ref, *outs):
        for d, out in enumerate(outs):
            out[...] = x_ref[pl.ds((member_of(group) ^ d) * n, n)]

    return call(body, "pack", [local], [((n, width, depth), local.dtype)] * group, [], 4, 20_000_000_000, 1 << 20)


def unpack(pieces):
    _, n, width, depth = pieces[0].shape

    def body(*refs):
        outs = refs[-2:]
        for d, ref in enumerate(refs[:-2]):
            for t in range(2):
                outs[t][pl.ds((member_of(len(pieces)) ^ d) * n, n)] = ref[t]

    return call(body, "unpack", pieces, [((n * len(pieces), width, depth), BF)] * 2, [], 4, 0, 1 << 20)


def regroup(lens, pieces, put):
    n, width, _ = pieces[0].shape
    j = member_of(len(pieces))
    for d, piece in enumerate(pieces):
        for u in range(n):
            start = (j ^ d) * width
            at = pl.ds(pl.multiple_of(u * SLOTS + start, width), width)
            block = piece[u]
            if lens is not None:
                slot = lax.broadcasted_iota(jnp.int32, (width, 1), 0) + start
                block = jnp.where(slot < lens[u], block.astype(F32), 0.0)
            put(at, block)


def deal(values, pieces):
    for d, piece in enumerate(pieces):
        n, width, _ = piece.shape
        for u in range(n):
            at = pl.ds(pl.multiple_of(u * SLOTS + (member_of(len(pieces)) ^ d) * width, width), width)
            piece[u] = values[at, :].astype(BF)


def stacked(head):
    return slice(SLOTS * (head % 2), SLOTS * (head % 2) + SLOTS)


def apart(pair, masks):
    return jnp.concatenate([pair * masks[0], pair * masks[1]], axis=0)


def pair_scratch(m):
    return ((m // SLOTS * (H // 2), 2 * SLOTS, SLOTS), BF)


def forward_attention(lens, h, gain, bias, wq, wk, wv, a_ref, q_ref, k_ref, v_ref, o_ref, lse_ref, p_ref):
    masks = head_masks(64)
    for i, rows in enumerate(tiles(h.shape[0])):
        xhat, _ = normalize(h[rows, :].astype(F32))
        a = (xhat * gain + bias).astype(BF)
        a_ref[rows, :] = a
        q_ref[rows, :] = (dot(a, wq[...]).astype(BF).astype(F32) * 0.125).astype(BF)
        k_ref[rows, :] = dot(a, wk[...]).astype(BF)
        v_ref[rows, :] = dot(a, wv[...]).astype(BF)
    key = lax.broadcasted_iota(jnp.int32, (SLOTS, 1), 0)
    for i, rows in enumerate(tiles(h.shape[0])):
        valid = key < lens[i]
        for head in range(H):
            cols = slice(128 * (head // 2), 128 * (head // 2) + 128)
            st = jnp.where(valid, dot(k_ref[rows, cols] * masks[head % 2], q_ref[rows, cols], NT), NEG)
            top = jnp.max(st, axis=0, keepdims=True)
            e = jnp.exp(st - top)
            tot = jnp.sum(e, axis=0, keepdims=True)
            p_ref[i * (H // 2) + head // 2, stacked(head), :] = (e * (1.0 / tot)).astype(BF)
            lse_ref[i * H + head, :] = (top + jnp.log(tot))[0]
    for i, rows in enumerate(tiles(h.shape[0])):
        for pair in range(H // 2):
            cols = slice(128 * pair, 128 * pair + 128)
            o_ref[rows, cols] = dot(p_ref[i * (H // 2) + pair], apart(v_ref[rows, cols], masks), TN).astype(BF)


def forward_ffn(h, o, wo, gain, bias, wup, bup, wdown, bdown, g_ref, c_ref, u_ref, gp_ref, n_ref):
    m, ff = h.shape[0], wup.shape[1]
    for rows in tiles(m):
        g = h[rows, :].astype(F32) + dot(o[rows, :], wo[...])
        g_ref[rows, :] = g
        xhat, _ = normalize(g)
        c_ref[rows, :] = (xhat * gain + bias).astype(BF)
    for f in range(0, ff, 256):
        fs = slice(f, f + 256)
        for rows in tiles(m):
            z = dot(c_ref[rows, :], wup[:, fs]) + bup[:, fs]
            z2 = z * z
            t = jnp.tanh(z * (GELU_C + GELU_C * GELU_A * z2))
            half = 0.5 + 0.5 * t
            gp = half + (0.5 * z) * (1.0 - t * t) * (GELU_C + 3.0 * GELU_C * GELU_A * z2)
            u_ref[rows, fs] = (z * half).astype(BF)
            gp_ref[rows, fs] = gp.astype(BF)
    if n_ref is not None:
        layer_output(g_ref, u_ref, wdown, bdown, n_ref)


def layer_output(g_ref, u_ref, wdown, bdown, n_ref):
    for rows in tiles(g_ref.shape[0]):
        n_ref[rows, :] = g_ref[rows, :] + (dot(u_ref[rows, :], wdown[...]) + bdown)


def store(core, keep, send, quarter, z, rows, cols, even, odd):
    mine, other = jnp.where(core == 0, even, odd), jnp.where(core == 0, odd, even)
    at = 2 * (z % 2) + z // 2
    keep[quarter, at, rows, cols] = mine
    send[quarter, at, rows, cols] = other


def ffn_terms(core, dm_ref, u_ref, gp_ref, c_ref, wdown, keep, send, dz_ref, sm_ref):
    ff = u_ref.shape[1]
    dm = dm_ref[...]
    for f in range(ff // STEP):
        res = dot(dm, u_ref[:, STEP * f : STEP * f + STEP], TN).astype(BF).reshape(4, 128, STEP)
        store(core, keep, send, slice(None), f, slice(0, 128), slice(0, 256), res[:, :, 0:256], res[:, :, 256:512])
    sm_ref[...] = jnp.zeros_like(sm_ref)
    sm_ref[0:1, :] = jnp.sum(dm.astype(F32), axis=0, keepdims=True)
    for f in range(ff // STEP):
        fs = slice(STEP * f, STEP * f + STEP)
        dz = (dot(dm, wdown[fs, :], NT) * gp_ref[:, fs].astype(F32)).astype(BF)
        dz_ref[:, fs] = dz
        sm_ref[1 + f : 2 + f, :] = jnp.sum(dz.astype(F32), axis=0, keepdims=True)
        res = dot(c_ref[...], dz, TN).astype(BF).reshape(4, 128, STEP)
        for t in range(2):
            rows, part = slice(64 * t, 64 * t + 64), res[:, :, 256 * t : 256 * t + 256]
            for z in range(4):
                store(core, keep, send, f, z, rows, slice(256, 512), part[z, 0:64], part[z, 64:128])


KEPT = ("a", "q", "k", "v", "o", "lse", "g", "c", "u", "gp")


def kept_shapes(m, d, ff):
    wide, narrow = (m, ff), (m, d)
    return [(narrow, BF)] * 5 + [((m // SLOTS * H, SLOTS), F32), (narrow, F32), (narrow, BF), (wide, BF), (wide, BF)]


def row(ref, l):
    return ref[l : l + 1, :].astype(F32)


def forward_layer(l, lens, h, norms, wts, kept, last, p_ref):
    ag, ab, fg, fb, bup, bdown = norms
    wq, wk, wv, wo, wup, wdown = [w.at[l] for w in wts]
    a, q, k, v, o, lse, g, c, u, gp = kept
    forward_attention(lens, h, row(ag, l), row(ab, l), wq, wk, wv, a, q, k, v, o, lse, p_ref)
    forward_ffn(h, o, wo, row(fg, l), row(fb, l), wup, row(bup, l), wdown, row(bdown, l), g, c, u, gp, last)


def chunk_shape(rows):
    return ((4, SHARDS // 2, rows, 512), BF)


def parity(halving):
    return lax.axis_index("seq") % 2 if halving else 0


def forward_first(lengths, parts, norms, wts):
    _, d, ff = wts[4].shape
    n, width, _ = parts[0].shape
    group = len(parts)
    m = n * group * width

    def body(*refs):
        lengths, refs = refs[0], refs[1:]
        parts, refs = refs[:group], refs[group:]
        norms, wts, kept, (x_ref, last, p_ref) = refs[:6], refs[6:12], refs[12:22], refs[22:]

        def put(at, block):
            x_ref[at, :] = block

        regroup(None, parts, put)
        forward_layer(0, lengths_of(lengths, n, group), x_ref, norms, wts, kept, last, p_ref)

    outs = kept_shapes(m, d, ff) + [((m, d), BF), ((m, d), F32)]
    res = call(body, "forward_first", [lengths, *parts, *norms, *wts], outs, [pair_scratch(m)], 4, 2 * m * (4 * d * d + 2 * d * ff), 24 << 20)
    return res[:11], res[11]


def forward_last(l, halving, lengths, h, parts, norms, wts):
    _, d, ff = wts[4].shape
    n, width, _ = parts[0].shape
    group = len(parts)
    m = n * group * width
    per = kept_shapes(m, d, ff)

    def body(*refs):
        lengths, h = refs[:2]
        refs = refs[2:]
        parts, refs = refs[:group], refs[group:]
        norms, wts, refs = refs[:6], refs[6:12], refs[12:]
        kept, refs = refs[:8], refs[8:]
        keep, send, dz_ref, sm_ref, c, gp, dm_ref, p_ref = refs
        lens = lengths_of(lengths, n, group)

        def put(at, block):
            dm_ref[at, :] = block.astype(BF)

        regroup(lens, parts, put)
        forward_layer(l, lens, h, norms, wts, [*kept[:7], c, kept[7], gp], None, p_ref)
        ffn_terms(parity(halving), dm_ref, kept[7], gp, c, wts[5].at[l], keep, send, dz_ref, sm_ref)

    outs = per[:7] + [per[8]] + [chunk_shape(128)] * 2 + [((m, ff), BF), ((8, d), F32)]
    *kept, keep, send, dz, sums = call(
        body, "forward_last", [lengths, h, *parts, *norms, *wts], outs,
        [per[7], per[9], ((m, d), BF), pair_scratch(m)], 20, 2 * m * (4 * d * d + 4 * d * ff), 24 << 20)
    return kept[:7] + [None, kept[7], None, h], (keep, send), dz, sums


def mid_terms(l, dh_ref, g, o, dz, gain, wup, wo, dg_ref, do_ref, dr_ref, sm_ref):
    m, d = g.shape
    dgain = dbias = None
    for i, rows in enumerate(tiles(m)):
        dc = dot(dz[rows, :], wup[l], NT)
        dx, dg1, db1 = norm_back(dc, g[rows, :], row(gain, l))
        dg = dh_ref[rows, :] + dx
        dg_ref[rows, :] = dg
        dr_ref[rows, :] = dg.astype(BF)
        dgain, dbias = (dg1, db1) if i == 0 else (dgain + dg1, dbias + db1)
    sm_ref[...] = jnp.zeros_like(sm_ref)
    sm_ref[0:1, :] = dgain
    sm_ref[1:2, :] = dbias
    do_ref[...] = dot(dr_ref[...], wo[l], NT).astype(BF)
    return dot(o[...], dr_ref[...], TN).astype(BF).reshape(SHARDS // 2, 2, d // SHARDS, d)


def attn_terms(l, lens, dg, do, lse, q, k, v, h, gain, wq, wk, wv, dq_ref, dk_ref, dv_ref, p_ref, s_ref, put):
    m, d = dg.shape
    masks = head_masks(64)
    low = lax.broadcasted_iota(jnp.int32, (1, 128), 1) < 64
    key = lax.broadcasted_iota(jnp.int32, (SLOTS, 1), 0)
    for i, rows in enumerate(tiles(m)):
        valid = key < lens[i]
        for head in range(H):
            cols, n, mk = slice(128 * (head // 2), 128 * (head // 2) + 128), i * (H // 2) + head // 2, masks[head % 2]
            st = jnp.where(valid, dot(k[rows, cols] * mk, q[rows, cols], NT), NEG)
            pt = jnp.exp(st - lse[i * H + head, :][None, :])
            dpt = dot(v[rows, cols] * mk, do[rows, cols], NT)
            delta = jnp.sum(pt * dpt, axis=0, keepdims=True)
            p_ref[n, stacked(head), :] = pt.astype(BF)
            s_ref[n, stacked(head), :] = (pt * (dpt - delta)).astype(BF)
    for i, rows in enumerate(tiles(m)):
        for pair in range(H // 2):
            cols, n = slice(128 * pair, 128 * pair + 128), i * (H // 2) + pair
            dq_ref[rows, cols] = (dot(s_ref[n], apart(k[rows, cols], masks), TN) * 0.125).astype(BF)
            both = dot(s_ref[n], q[rows, cols])
            dk_ref[rows, cols] = jnp.where(low, both[0:SLOTS], both[SLOTS:]).astype(BF)
            both = dot(p_ref[n], do[rows, cols])
            dv_ref[rows, cols] = jnp.where(low, both[0:SLOTS], both[SLOTS:]).astype(BF)
    dgain = dbias = None
    for i, rows in enumerate(tiles(m)):
        da = dot(dq_ref[rows, :], wq[l], NT) + dot(dk_ref[rows, :], wk[l], NT) + dot(dv_ref[rows, :], wv[l], NT)
        dx, dg1, db1 = norm_back(da, h[rows, :].astype(F32), row(gain, l))
        put(rows, dg[rows, :] + dx)
        dgain, dbias = (dg1, db1) if i == 0 else (dgain + dg1, dbias + db1)
    return dgain, dbias


def square_terms(a, *grads):
    d = a.shape[1]
    return [dot(a[...], ref[...], TN).astype(BF).reshape(SHARDS // 2, 2, d // SHARDS, d) for ref in grads]


def back_top(l, lengths, parts, kept, dz, norms, wts):
    g, o = kept[6], kept[4]
    m, d = g.shape
    group = len(parts)

    def body(lengths, *refs):
        parts, refs = refs[:group], refs[group:]
        g, o, dz, gain, wup, wo, dg_ref, do_ref, dout_ref, sm_ref, dr_ref, dh_ref = refs

        def put(at, block):
            dh_ref[at, :] = block

        regroup(lengths_of(lengths, m // SLOTS, group), parts, put)
        dout_ref[...] = mid_terms(l, dh_ref, g, o, dz, gain, wup, wo, dg_ref, do_ref, dr_ref, sm_ref)

    outs = [((m, d), F32), ((m, d), BF), ((SHARDS // 2, 2, d // SHARDS, d), BF), ((8, d), F32)]
    return call(body, "back_top", [lengths, *parts, g, o, dz, norms[2], wts[4], wts[3]], outs, [((m, d), BF), ((m, d), F32)], 6,
                2 * m * 6 * d * d, 9 << 20)


def back_between(l, halving, lengths, dg, do, kept, under, norms, wts, units, group):
    a, q, k, v, o, lse, g, c, u, gp, h = kept
    c, u, gp = under[7:10]
    m, d = dg.shape
    ff = u.shape[1]

    def body(lengths, dg, do, lse, q, k, v, h, gain, wq, wk, wv, c, u, gp, wdown,
             keep0, send0, dh_ref, dz_ref, dq_ref, dk_ref, dv_ref, sm_ref, sm0_ref, dm_ref, p_ref, s_ref):
        core, lens = parity(halving), lengths_of(lengths, units, group)

        def put(rows, dh):
            dh_ref[rows, :] = dh
            dm_ref[rows, :] = dh.astype(BF)

        dgain, dbias = attn_terms(l, lens, dg, do, lse, q, k, v, h, gain, wq, wk, wv, dq_ref, dk_ref, dv_ref, p_ref, s_ref, put)
        sm_ref[...] = jnp.zeros_like(sm_ref)
        sm_ref[0:1, :] = dgain
        sm_ref[1:2, :] = dbias
        ffn_terms(core, dm_ref, u, gp, c, wdown.at[l - 1], keep0, send0, dz_ref, sm0_ref)

    outs = [chunk_shape(128)] * 2 + [((m, d), F32), ((m, ff), BF)] + [((m, d), BF)] * 3 + [((8, d), F32)] * 2
    keep0, send0, *rest = call(
        body, "back_between", [lengths, dg, do, lse, q, k, v, h, norms[0], *wts[:3], c, u, gp, wts[5]], outs,
        [((m, d), BF), pair_scratch(m), pair_scratch(m)], 9, 2 * m * 19 * d * d, 20 << 20)
    return (keep0, send0), rest


def square_halves(halving, a, grads, dout):
    d = a.shape[1]

    def body(a, dq, dk, dv, dout, keep, send):
        core = parity(halving)
        for n, term in enumerate([dout[...], *square_terms(a, dq, dk, dv)]):
            for z in range(SHARDS // 2):
                at, rows = 2 * (z % 2) + z // 2, slice(64 * n, 64 * n + 64)
                keep[at, rows, :] = jnp.where(core == 0, term[z, 0], term[z, 1])
                send[at, rows, :] = jnp.where(core == 0, term[z, 1], term[z, 0])

    outs = [((SHARDS // 2, 256, d), BF)] * 2
    return call(body, "square_halves", [a, *grads, dout], outs, [], 4, 2 * a.shape[0] * 3 * d * d, 4 << 20)


def back_bottom(halving, lengths, dh, dz, smalls, kept, norms, wts, width, group):
    a, q, k, v, o, lse, g, c, u, gp, h = kept
    m, d = dh.shape
    units = m // SLOTS

    def body(lengths, dh, g, o, dz, fgain, wup, wo, lse, q, k, v, a, h, gain, wq, wk, wv, attn1, mid1, ffn0, ffn1, keep, send, *refs):
        outs, refs = refs[:group], refs[group:]
        dg, do, dr, mid0, dq_ref, dk_ref, dv_ref, dx_ref, p_ref, s_ref = refs
        core, lens = parity(halving), lengths_of(lengths, units, group)
        first = mid_terms(0, dh, g, o, dz, fgain, wup, wo, dg, do, dr, mid0)
        for z in range(SHARDS // 2):
            store(core, keep, send, 0, z, slice(0, 64), slice(None), first[z, 0], first[z, 1])

        def put(rows, value):
            dx_ref[rows, :] = value

        dgain, dbias = attn_terms(0, lens, dg, do, lse, q, k, v, h, gain, wq, wk, wv, dq_ref, dk_ref, dv_ref, p_ref, s_ref, put)
        for n, term in enumerate(square_terms(a, dq_ref, dk_ref, dv_ref)):
            for z in range(SHARDS // 2):
                store(core, keep, send, n + 1, z, slice(0, 64), slice(None), term[z, 0], term[z, 1])
        lines = [dgain, attn1[0:1, :], dbias, attn1[1:2, :], mid0[0:1, :], mid1[0:1, :], mid0[1:2, :], mid1[1:2, :],
                 ffn0[0:1, :], ffn1[0:1, :]]
        zero = jnp.zeros((1, d), F32)
        block = jnp.concatenate(lines + [zero] * 6, axis=0).astype(BF)
        other = jnp.concatenate([ffn0[1:5, :], ffn1[1:5, :]] + [zero] * 8, axis=0).astype(BF)
        for half in (keep, send):
            for at in range(SHARDS // 2):
                half[0, at, 64:80, :] = block
                half[1, at, 64:80, :] = other
                for t in (2, 3):
                    half[t, at, 64:80, :] = jnp.zeros((16, d), BF)
        deal(dx_ref, outs)

    outs = [chunk_shape(80)] * 2 + [((units, width, d), BF)] * group
    wide, narrow = ((m, d), F32), ((m, d), BF)
    keep, send, *parts = call(
        body, "back_bottom",
        [lengths, dh, g, o, dz, norms[2], wts[4], wts[3], lse, q, k, v, a, h, norms[0], *wts[:3], *smalls], outs,
        [wide, narrow, narrow, ((8, d), F32), narrow, narrow, narrow, wide, pair_scratch(m), pair_scratch(m)], 12, 2 * m * 16 * d * d, 20 << 20)
    return (keep, send), parts


def results(l, kept, norms, wts, parts):
    g, u = kept[6], kept[8]
    group = len(parts)
    shape = (2,) + parts[0].shape

    def body(g, u, wdown, bdown, *refs):
        last = refs[-1]
        layer_output(g, u, wdown.at[l], row(bdown, l), last)
        outs = refs[group : 2 * group]
        deal(last, [out.at[0] for out in outs])
        for part, out in zip(refs[:group], outs):
            out[1] = part[...]

    return call(body, "results", [g, u, wts[5], norms[5], *parts], [(shape, BF)] * group, [(g.shape, F32)], 8,
                2 * u.shape[0] * u.shape[1] * g.shape[1], 4 << 20)


def finish_wide(wide0, wide1, d, ff):
    def body(w0, w1, down, up):
        for l, ref in enumerate((w0, w1)):
            for n in range(4):
                part = ref[n].astype(F32)
                down[l, :, 128 * n : 128 * n + 128] = part[:, 0:256].T
                for t in range(2):
                    at = 512 * n + 256 * t
                    up[l, :, at : at + 256] = part[64 * t : 64 * t + 64, 256:512]

    return call(body, "finish_wide", [wide0, wide1], [((2, 256, d), F32), ((2, 64, ff), F32)], [], 8, 0, 1024)


def finish_last(own, others, square, d):
    rows = own.shape[0]
    offsets = [first for _, first in others]

    def body(own, *refs):
        parts, other = [(own, 0), *zip(refs[:3], offsets)], refs[3]
        outs = refs[4:8]
        ag, ab, fg, fb, bd, bu, x, vsm = refs[8:]
        here = 2 * bit_of(PLANE_1) + bit_of(PLANE_2)
        for (ref, first), flip in zip(parts, (0, 2, 1, 3)):
            x[here ^ flip] = ref[first : first + rows, :]
        for n in range(4):
            outs[n][0] = x[n, 0:64, :].astype(F32)
            outs[n][1] = other[64 * n : 64 * n + 64, :].astype(F32)
        s = lax.axis_index("seq")
        vsm[...] = x[0:2, 64:80, :].astype(F32)
        pair = vsm[0, :, pl.ds(pl.multiple_of((s // 2) * 128, 128), 128)]
        mine = jnp.where(s % 2 == 0, pair[:, 0:64], pair[:, 64:128])
        for n, ref in enumerate((ag, ab, fg, fb, bd)):
            ref[...] = mine[2 * n : 2 * n + 2, :]
        for l in range(2):
            bu[l : l + 1, :] = vsm[1, pl.ds(4 * l + s // 2, 1), pl.ds(pl.multiple_of((s % 2) * 256, 256), 256)]

    outs = [((2, 64, d), F32)] * 4 + [((2, 64), F32)] * 5 + [((2, 256), F32)]
    return call(body, "finish_last", [own, *[array for array, _ in others], square], outs, [((4, rows, d), BF), ((2, 16, d), F32)], 8, 0, 2 << 20)


def swap(clock, sends):
    size = lax.axis_size("seq")
    out = [None] * len(sends)
    for d, s in enumerate(sends):
        clock.send(s, [(i, i ^ (d + 1)) for i in range(size)], "seq", lambda value, d=d: out.__setitem__(d, value))
    return out


BOTH = ("dp", "seq")


def pairs_of(flip):
    out = []
    for y in range(2):
        for x in range(2):
            for z in range(4):
                for c in range(2):
                    y2, x2, z2, c2 = flip(y, x, z, c)
                    out.append((y * 16 + x * 8 + z * 2 + c, y2 * 16 + x2 * 8 + z2 * 2 + c2))
    return out


CORE = pairs_of(lambda y, x, z, c: (y, x, z, 1 - c))
PLANE_1 = pairs_of(lambda y, x, z, c: (y, 1 - x, z, c) if c == 0 else (1 - y, x, z, c))
PLANE_2 = pairs_of(lambda y, x, z, c: (y, 1 - x, z, c) if c == 1 else (1 - y, x, z, c))
PLANE_3 = pairs_of(lambda y, x, z, c: (1 - y, 1 - x, z, c))
LINE_1 = pairs_of(lambda y, x, z, c: (y, x, z ^ 1, c))
LINE_2 = pairs_of(lambda y, x, z, c: (y, x, z ^ 2, c))


def bit_of(pairs):
    dp, seq = lax.axis_index("dp"), lax.axis_index("seq")
    if pairs is LINE_1:
        return (seq // 2) % 2
    if pairs is LINE_2:
        return seq // 4
    y, x = dp // 2, dp % 2
    return jnp.where((seq % 2 == 0) == (pairs is PLANE_1), x, y)


class Clock:
    def __init__(self):
        self.last, self.waiting = None, []

    def done(self, value):
        self.last = value

    def send(self, value, pairs, axes, arrived):
        self.waiting.append((value, pairs, axes, arrived))

    def after(self, value):
        waiting, self.waiting = self.waiting, []
        value, last, sent = lax.optimization_barrier((value, self.last, [w[0] for w in waiting]))
        for v, (_, pairs, axes, arrived) in zip(sent, waiting):
            arrived(lax.ppermute(v, axes, pairs))
        return value


class Chunk:
    def __init__(self, clock, halves):
        self.kept = halves[0].reshape(-1, halves[0].shape[-1])
        self.moved, self.paired, self.all = None, False, []
        clock.send(halves[1].reshape(self.kept.shape), CORE, BOTH, lambda value: self.arrived(value, 0))

    def arrived(self, value, first):
        self.moved = (value, first)
        self.all.append(self.moved)


BLOCK = 256


def blocks(count):
    return [(start, min(BLOCK, count - start)) for start in range(0, count, BLOCK)]


def advance(clock, items, weight=0):
    for (chunk, _, _), kept in zip(items, clock.after([chunk.kept for chunk, _, _ in items])):
        chunk.kept = kept
    arrays, lanes, keeps, plan = [], {}, [], []

    def index(array):
        for n, other in enumerate(arrays):
            if other is array:
                return n
        arrays.append(array)
        return len(arrays) - 1

    for chunk, kind, pairs in items:
        rows = chunk.kept.shape[0]
        now = 2 * rows if chunk.paired else rows
        left = rows // 2 if kind == "split" else now
        lane = []
        for each in pairs if kind == "spread" else (pairs,) if kind in ("split", "whole", "gather") else ():
            key = [n for n in lanes if lanes[n][0] is each]
            name = key[0] if key else len(lanes)
            first = lanes[name][1] if key else 0
            lane.append((name, first))
            lanes[name] = (each, first + left)
        at, by, offset = index(chunk.kept), None, 0
        if chunk.moved:
            by, offset = index(chunk.moved[0]), chunk.moved[1]
        plan.append((kind, pairs, at, by, offset, rows, chunk.paired, lane))
        keeps.append(left)
    count = len(lanes)

    def body(*refs):
        ins, outs = refs[: len(arrays)], refs[len(arrays) :]
        for n, (kind, pairs, at, by, offset, rows, paired, lane) in enumerate(plan):
            kept, moved, left = ins[at], None if by is None else ins[by], outs[count + n]
            sent, start = (outs[lane[0][0]], lane[0][1]) if lane else (None, 0)

            def summed(low, size):
                if isinstance(low, int):
                    first, second = slice(low, low + size), slice(offset + low, offset + low + size)
                else:
                    first = pl.ds(pl.multiple_of(low, 16), size)
                    second = pl.ds(pl.multiple_of(offset + low, 16), size)
                if moved is None:
                    return kept[first, :]
                return (kept[first, :].astype(F32) + moved[second, :].astype(F32)).astype(BF)

            if kind == "split":
                half = rows // 2
                bit = bit_of(pairs)
                for low, size in blocks(half):
                    sent[start + low : start + low + size, :] = summed((1 - bit) * half + low, size)
                    left[low : low + size, :] = summed(bit * half + low, size)
            elif kind == "order":
                part = rows // 2
                own = 2 * bit_of(pairs[0]) + bit_of(pairs[1])
                for m, flip in enumerate((0, 2, 1, 3)):
                    source, base = (kept, 0) if m < 2 else (moved, offset)
                    base += (m % 2) * part
                    left[pl.ds(pl.multiple_of((own ^ flip) * part, 16), part), :] = source[base : base + part, :]
            elif paired:
                for low, size in blocks(rows):
                    for source, base, to in ((kept, low, low), (moved, offset + low, rows + low)):
                        value = source[base : base + size, :]
                        left[to : to + size, :] = value
                        sent[start + to : start + to + size, :] = value
            else:
                for low, size in blocks(rows):
                    value = summed(low, size)
                    left[low : low + size, :] = value
                    for name, to in lane:
                        outs[name][to + low : to + low + size, :] = value

    width = items[0][0].kept.shape[1]
    sizes = [lanes[n][1] for n in range(count)] + keeps
    results = call(body, "advance", arrays, [((rows, width), BF) for rows in sizes], [], 4, weight, 1 << 20)
    clock.done(results[0])
    for n in range(count):
        here = [(item[0], to) for item, spec in zip(items, plan) for name, to in spec[-1] if name == n]

        def arrived(value, here=here):
            for chunk, first in here:
                chunk.arrived(value, first)

        clock.send(results[n], lanes[n][0], BOTH, arrived)
    for (chunk, kind, _), kept in zip(items, results[count:]):
        chunk.kept, chunk.moved, chunk.all = kept, None, []
        chunk.paired = kind == "gather"


def scattered(term):
    share = lax.psum_scatter(term.astype(F32), "seq", scatter_dimension=1, tiled=True)
    return lax.psum(share.astype(BF), "dp").astype(F32)


def joined(halves, z_first=False):
    width = halves[0].shape[-1]
    if z_first:
        shards = jnp.stack([half.reshape(2, 2, 4, -1, width) for half in halves]).transpose(2, 1, 0, 3, 4, 5)
    else:
        shards = jnp.stack([half.reshape(4, 2, 2, -1, width) for half in halves]).transpose(3, 2, 0, 1, 4, 5)
    return shards.reshape((SHARDS,) + shards.shape[3:])


def plain_sums(wide0, wide1, part, narrow, d, ff):
    part, narrow = joined(part, True), joined(narrow)
    down, up, square = [], [], []
    for wide, terms in ((wide0, narrow[:, :, :64]), (wide1, part)):
        wide = joined(wide).reshape(SHARDS, 512, 512)
        down.append(wide[:, :, :256].transpose(0, 2, 1).reshape(ff, d))
        up.append(wide[:, :, 256:].reshape(SHARDS, ff // 256, d // SHARDS, 256).transpose(0, 2, 1, 3).reshape(d, ff))
        square.append(terms.transpose(1, 0, 2, 3).reshape(4, d, d))
    square = jnp.stack(square, axis=1)
    small = narrow[0, 0, 64:74].reshape(5, 2, d)
    bias = narrow[0, 1, 64:72].reshape(2, ff)
    terms = (small[0], small[1], square[1], square[2], square[3], square[0], small[2], small[3], jnp.stack(up), bias,
             jnp.stack(down), small[4])
    return tuple(scattered(term) for term in terms)


def on_device(
    inputs, cotangent, item_lengths, attn_gain, attn_bias, query_weight, key_weight, value_weight, output_weight,
    ffn_gain, ffn_bias, up_weight, up_bias, down_weight, down_bias,
):
    rows, width, depth = inputs.shape
    ff = up_weight.shape[2]
    group = SLOTS // width
    halving = lax.axis_size("dp") == 4 and lax.axis_size("seq") == SHARDS
    lengths = item_lengths.T
    clock = Clock()
    packed = pack(inputs, group)
    clock.done(packed[0])
    x_parts = swap(clock, packed[1:])
    cotangent = clock.after(cotangent)
    first = pack(cotangent, group)
    clock.done(first[0])
    cot_parts = swap(clock, first[1:])
    clock.done(clock.after(first[0]))
    norms = (attn_gain, attn_bias, ffn_gain, ffn_bias, up_bias, down_bias)
    wts = (query_weight, key_weight, value_weight, output_weight, up_weight, down_weight)
    x_parts, cot_parts = [packed[0]] + x_parts, [first[0]] + cot_parts
    kept0, h1 = forward_first(lengths, x_parts, norms, wts)
    kept1, wide1, dz1, ffn1 = forward_last(1, halving, lengths, h1, cot_parts, norms, wts)
    clock.done(ffn1)
    line = rows // group, group
    if halving:
        f1 = Chunk(clock, wide1)
    dg, do, dout, mid1 = back_top(1, lengths, cot_parts, kept1, clock.after(dz1), norms, wts)
    clock.done(mid1)
    if halving:
        advance(clock, [(f1, "split", PLANE_1)])
    wide0, (dh, dz0, dq, dk, dv, attn1, ffn0) = back_between(
        1, halving, lengths, clock.after(dg), do, kept1, kept0, norms, wts, *line)
    clock.done(attn1)
    if halving:
        f0 = Chunk(clock, wide0)
    if halving:
        advance(clock, [(f1, "close", None)], LONG)
    part = square_halves(halving, clock.after(kept1[0]), (dq, dk, dv), dout)
    clock.done(part[0])
    if halving:
        a1 = Chunk(clock, part)
        advance(clock, [(f1, "split", PLANE_2), (f0, "split", PLANE_2)])
        advance(clock, [(a1, "split", LINE_1)])
    narrow, parts = back_bottom(
        halving, lengths, clock.after(dh), dz0, (attn1, mid1, ffn0, ffn1), kept0, norms, wts, width, group)
    clock.done(parts[0])
    if halving:
        a0 = Chunk(clock, narrow)
        advance(clock, [(f1, "split", LINE_1), (a1, "split", LINE_2)], LONG)
        advance(clock, [(f0, "split", PLANE_1), (a0, "split", PLANE_1)])
    both = results(1, kept1, norms, wts, clock.after(parts))
    clock.done(both[0])
    if halving:
        advance(clock, [(f0, "split", LINE_1), (f1, "split", LINE_2), (a0, "split", PLANE_2), (a1, "whole", PLANE_2)])
        advance(clock, [(f0, "split", LINE_2), (a0, "split", LINE_1), (f1, "gather", PLANE_1), (a1, "whole", PLANE_1)])
    mine = swap(clock, both[1:])
    if halving:
        advance(clock, [(a0, "split", LINE_2), (f1, "gather", PLANE_2), (f0, "gather", PLANE_2), (a1, "close", None)], FIVE)
        clock.done(mine[0])
        advance(clock, [(f0, "gather", PLANE_1), (a0, "spread", (PLANE_1, PLANE_2, PLANE_3)), (f1, "order", (PLANE_1, PLANE_2))], SIX)
    own = clock.after(both[0])
    if not halving:
        output, input_grad = unpack([own] + mine)
        return (output, input_grad) + plain_sums(wide0, wide1, part, narrow, depth, ff)

    advance(clock, [(f0, "order", (PLANE_2, PLANE_1))])
    wide0, wide1 = [c.kept.reshape(4, -1, depth) for c in (f0, f1)]
    down, up = finish_wide(clock.after(wide0), wide1, depth, ff)
    clock.done(down)
    do, dq, dk, dv, ag, ab, fg, fb, bd, bu = finish_last(clock.after(a0.kept), a0.all, a1.kept, depth)
    clock.done(do)
    output, input_grad = unpack([clock.after(own)] + mine)
    return output, input_grad, ag, ab, dq, dk, dv, do, fg, fb, up, bu, down, bd


def solution(mesh):
    spec = jax.sharding.PartitionSpec
    whole, split = spec(), spec("dp", "seq", None)
    vec, mat = spec(None, "seq"), spec(None, "seq", None)
    return jax.shard_map(
        on_device,
        mesh=mesh,
        in_specs=(split, split, spec("dp", None)) + (whole,) * 12,
        out_specs=(split, split, vec, vec, mat, mat, mat, mat, vec, vec, mat, vec, mat, vec),
        check_vma=False,
    )
```
